256 devices in a mesh: space: 32 (over y, z), dp: 8 (over x, core).
Axes of the slice: x: 4, y: 4, z: 8, core: 2. Of those that a mesh axis runs over, the one named last changes fastest.
Arguments:
- tokens: bfloat16 [8, 256, 32, 512], P('dp', 'space'), may hold values from -6 to 6
- region: int32 [8, 64, 8], P('dp'), may hold values from 0 to 2
- valid: int32 [8, 256, 32], P('dp'), may hold values 0 or 1
- qkv_weight: bfloat16 [512, 1536], replicated, may hold values from -0.25 to 0.25
- proj_weight: bfloat16 [512, 512], replicated, may hold values from -0.25 to 0.25
- merge_weight: bfloat16 [2048, 1024], replicated, may hold values from -0.125 to 0.125
- logit_scale: float32 [16], replicated, may hold values from 4 to 100
- bias_table: float32 [16, 225], replicated, may hold values from -8 to 8
- gain_attn: float32 [512], replicated, may hold values from 0.5 to 1.5
- gain_merge: float32 [1024], replicated, may hold values from 0.5 to 1.5
- cotangent: bfloat16 [8, 128, 16, 1024], P('dp', 'space'), may hold values from -6 to 6
Outputs:
- merged: bfloat16 [8, 128, 16, 1024], P('dp', 'space')
- grad_tokens: bfloat16 [8, 256, 32, 512], P('dp', 'space')
- grad_qkv: float32 [512, 1536], P('space', 'dp')
- grad_proj: float32 [512, 512], P('space', 'dp')
- grad_merge: float32 [2048, 1024], P('space', 'dp')
- grad_bias: float32 [16, 225], replicated
The draws below stay inside these ranges and needn't reach their ends.
All inputs are finite; a program needn't handle non-finite values. No bound on the sum of `valid` on one device may be relied on, other than what follows from the above.
Results may differ from the reference program's by a relative error of at most 0.038.
Values may be sent and summed in bfloat16 or wider, within the bound.
A program may use at most 128 MiB of HBM per device.

```python
import math
import jax
import jax.numpy as jnp
from jax import lax

D = 512
HEADS = 16
WIN = 8
COLS = 32
HEAD_DIM = 32
SHIFT = 4
OFFSETS = 225
IMAGES = 8
HEIGHT = 256


def with_ends(result, key, smallest, top_value):
    spot = [jax.random.randint(jax.random.fold_in(key, axis), (), 0, length) for axis, length in enumerate(result.shape)]
    main_axis = result.shape.index(max(result.shape))
    beside = spot[:main_axis] + [(spot[main_axis] + 1) % result.shape[main_axis]] + spot[main_axis + 1:]
    return result.at[tuple(spot)].set(smallest).at[tuple(beside)].set(top_value)


def level_of(stream_key, shape, cuts, smallest, top_value):
    level, own = 1.0, jax.random.fold_in(stream_key, 6)
    for dim, parts in cuts:
        draws = jnp.exp(jax.random.uniform(jax.random.fold_in(own, dim), (parts,), jnp.float32, smallest / len(cuts), top_value / len(cuts)))
        level = level * jnp.repeat(draws, shape[dim] // parts).reshape([-1 if axis == dim else 1 for axis in range(len(shape))])
    return level


def bell_draw(own_key, dims, deviation, limit, split=(), kind=jnp.bfloat16):
    values = jax.random.normal(own_key, dims, jnp.float32) * deviation
    if len(split) > 0:
        values = level_of(own_key, dims, split, -0.22, 0.18) * values
    return jnp.clip(values, min=-limit, max=limit).astype(kind)


def setup_inputs(seed: int = 0) -> dict:
    streams_of = jax.random.split(jax.random.key(seed), 12)
    tokens = bell_draw(streams_of[0], (IMAGES, HEIGHT, COLS, D), 1.0, 6.0, ((0, 8), (1, 32)))
    region = with_ends(jax.random.randint(streams_of[1], (IMAGES, HEIGHT // 4, COLS // 4), 0, 3), jax.random.fold_in(streams_of[1], 1), 0, 2).astype(jnp.int32)
    valid = with_ends((jax.random.randint(streams_of[2], (IMAGES, HEIGHT, COLS), 0, 8) < 7).astype(jnp.int32), jax.random.fold_in(streams_of[2], 1), 0, 1)
    qkv_weight = bell_draw(streams_of[3], (D, 3 * D), D ** -0.5, 0.25)
    proj_weight = bell_draw(streams_of[4], (D, D), D ** -0.5, 0.25)
    merge_weight = bell_draw(streams_of[5], (4 * D, 2 * D), (4 * D) ** -0.5, 0.125)
    logit_scale = jnp.clip(jnp.exp(jax.random.uniform(streams_of[6], (HEADS,), jnp.float32, math.log(4.0), math.log(100.0))), 4.0, 100.0)
    bias_table = bell_draw(streams_of[7], (HEADS, OFFSETS), 2.0, 8.0, (), jnp.float32)
    gain_attn = jnp.clip(1.0 + 0.1 * jax.random.normal(streams_of[8], (D,), jnp.float32), 0.5, 1.5)
    gain_merge = jnp.clip(1.0 + 0.1 * jax.random.normal(streams_of[9], (2 * D,), jnp.float32), 0.5, 1.5)
    cotangent = bell_draw(streams_of[10], (IMAGES, HEIGHT // 2, COLS // 2, 2 * D), 1.0, 6.0, ((0, 8), (1, 32)))
    return dict(tokens=tokens, region=region, valid=valid, qkv_weight=qkv_weight, proj_weight=proj_weight, merge_weight=merge_weight, logit_scale=logit_scale, bias_table=bias_table, gain_attn=gain_attn, gain_merge=gain_merge, cotangent=cotangent)


def split_windows(t):
    b, r, w = (t.shape[0], t.shape[1], t.shape[2])
    rest = t.shape[3:]
    t = t.reshape((b, r // WIN, WIN, w // WIN, WIN) + rest)
    order = (0, 1, 3, 2, 4) + tuple(range(5, t.ndim))
    t = t.transpose(order)
    return t.reshape((b * (r // WIN) * (w // WIN), WIN * WIN) + rest)

def join_windows(t, b, r, w):
    rest = t.shape[2:]
    t = t.reshape((b, r // WIN, w // WIN, WIN, WIN) + rest)
    order = (0, 1, 3, 2, 4) + tuple(range(5, t.ndim))
    return t.transpose(order).reshape((b, r, w) + rest)

def offsets_table():
    place = jnp.arange(WIN * WIN, dtype=jnp.int32)
    prow = place // WIN
    pcol = place % WIN
    rel = (prow[:, None] - prow[None, :] + WIN - 1) * (2 * WIN - 1) + pcol[:, None] - pcol[None, :] + WIN - 1
    return (rel[None, :, :] == jnp.arange(OFFSETS, dtype=jnp.int32)[:, None, None]).astype(jnp.float32)

def wrap_part(index, extent):
    return jnp.where(index < extent - WIN, 0, jnp.where(index < extent - SHIFT, 1, 2)).astype(jnp.int32)

def region_labels(swath, rows, cols, height, width):
    return swath * 9 + wrap_part(rows, height)[None, :, None] * 3 + wrap_part(cols, width)[None, None, :]

def layer_norm(t, gain):
    centred = t - lax.optimization_barrier(jnp.mean(t, -1, keepdims=True))
    spread = lax.optimization_barrier(jnp.mean(centred * centred, -1, keepdims=True))
    return (centred * lax.rsqrt(spread + 1e-05) * gain).astype(jnp.bfloat16)

def attend(qkv, labels, valid, logit_scale, bias_table):
    b, r, w, three = qkv.shape
    width = three // 3
    heads = width // HEAD_DIM
    windows = split_windows(qkv).reshape(-1, WIN * WIN, 3, heads, HEAD_DIM)
    query = windows[:, :, 0].astype(jnp.float32)
    keys = windows[:, :, 1].astype(jnp.float32)
    values = windows[:, :, 2].astype(jnp.float32)
    query = query * lax.rsqrt(lax.optimization_barrier(jnp.sum(query * query, -1, keepdims=True)) + 1e-06)
    keys = keys * lax.rsqrt(lax.optimization_barrier(jnp.sum(keys * keys, -1, keepdims=True)) + 1e-06)
    scores = jnp.einsum('nihd,njhd->nhij', query, keys, precision=lax.Precision.HIGHEST)
    scores = scores * logit_scale[None, :, None, None]
    bias = jnp.einsum('hk,kij->hij', bias_table, offsets_table(), precision=lax.Precision.HIGHEST)
    scores = scores + bias[None]
    label_win = split_windows(labels)
    live_win = split_windows(valid)
    diagonal = jnp.eye(WIN * WIN, dtype=bool)
    allowed = (label_win[:, :, None] == label_win[:, None, :]) & ((live_win[:, None, :] == 1) | diagonal[None])
    scores = jnp.where(allowed[:, None], scores, -1000000000.0)
    top = lax.stop_gradient(lax.optimization_barrier(jnp.max(scores, -1, keepdims=True)))
    expo = jnp.exp(scores - top)
    probs = (expo / lax.optimization_barrier(jnp.sum(expo, -1, keepdims=True))).astype(jnp.bfloat16)
    mixed = jnp.einsum('nhij,njhd->nihd', probs.astype(jnp.float32), values, precision=lax.Precision.HIGHEST)
    mixed = mixed.astype(jnp.bfloat16).reshape(-1, WIN * WIN, width)
    return join_windows(mixed, b, r, w)

def attention_forward(shifted, labels, valid, qkv_weight, proj_weight, logit_scale, bias_table, gain_attn):
    b, r, w, c = shifted.shape
    qkv = jnp.dot(shifted.reshape(-1, c), qkv_weight, preferred_element_type=jnp.float32)
    qkv = qkv.astype(jnp.bfloat16).reshape(b, r, w, 3 * c)
    mixed = attend(qkv, labels, valid, logit_scale, bias_table)
    proj = jnp.dot(mixed.reshape(-1, c), proj_weight, preferred_element_type=jnp.float32)
    return (qkv, mixed, proj, layer_norm(proj, gain_attn).reshape(b, r, w, c))

def fold_quads(hidden):
    b, r, w, c = hidden.shape
    t = hidden.reshape(b, r // 2, 2, w // 2, 2, c).transpose(0, 1, 3, 4, 2, 5)
    return t.reshape(b * (r // 2) * (w // 2), 4 * c)

def unfold_quads(t, b, r, w):
    c = t.shape[-1] // 4
    t = t.reshape(b, r // 2, w // 2, 2, 2, c).transpose(0, 1, 4, 2, 3, 5)
    return t.reshape(b, r, w, c)

def merge_forward(hidden, merge_weight, gain_merge):
    b, r, w, c = hidden.shape
    quads = fold_quads(hidden)
    pre = jnp.dot(quads, merge_weight, preferred_element_type=jnp.float32)
    return (quads, pre, layer_norm(pre, gain_merge).reshape(b, r // 2, w // 2, 2 * c))

def merge_backward(quads, pre, seed_grad, merge_weight, gain_merge, b, r, w):
    _, back = jax.vjp(lambda t: layer_norm(t, gain_merge), pre)
    grad_pre, = back(seed_grad.reshape(pre.shape[0], pre.shape[1]))
    grad_pre = grad_pre.astype(jnp.bfloat16)
    grad_weight = jnp.dot(quads.T, grad_pre, preferred_element_type=jnp.float32)
    grad_quads = jnp.dot(grad_pre, merge_weight.T, preferred_element_type=jnp.float32).astype(jnp.bfloat16)
    return (grad_weight, unfold_quads(grad_quads, b, r, w))

def attention_backward(shifted, labels, valid, qkv, mixed, proj, grad_normed, qkv_weight, proj_weight, logit_scale, bias_table, gain_attn):
    b, r, w, c = shifted.shape
    _, back = jax.vjp(lambda t: layer_norm(t, gain_attn), proj)
    grad_out, = back(grad_normed.reshape(-1, c))
    grad_out = grad_out.astype(jnp.bfloat16)
    grad_pw = jnp.dot(mixed.reshape(-1, c).T, grad_out, preferred_element_type=jnp.float32)
    grad_mixed = jnp.dot(grad_out, proj_weight.T, preferred_element_type=jnp.float32)
    grad_mixed = grad_mixed.astype(jnp.bfloat16).reshape(b, r, w, c)
    _, back = jax.vjp(lambda t, table: attend(t, labels, valid, logit_scale, table), qkv, bias_table)
    grad_act, grad_table = back(grad_mixed)
    grad_act = grad_act.reshape(-1, 3 * c)
    grad_qw = jnp.dot(shifted.reshape(-1, c).T, grad_act, preferred_element_type=jnp.float32)
    grad_shifted = jnp.dot(grad_act, qkv_weight.T, preferred_element_type=jnp.float32)
    return (grad_qw, grad_pw, grad_table, grad_shifted.astype(jnp.bfloat16).reshape(b, r, w, c))

def reference(tokens, region, valid, qkv_weight, proj_weight, merge_weight, logit_scale, bias_table, gain_attn, gain_merge, cotangent):
    height, width = (tokens.shape[1], tokens.shape[2])
    rows = jnp.arange(height, dtype=jnp.int32)
    cols = jnp.arange(width, dtype=jnp.int32)

    def one_image(totals, item):
        image, swath, mask, seed_grad = item
        x = image[None]
        shifted = jnp.roll(x, (-SHIFT, -SHIFT), (1, 2))
        blocks = jnp.repeat(jnp.repeat(swath, 4, 0), 4, 1)
        labels = region_labels(jnp.roll(blocks, (-SHIFT, -SHIFT), (0, 1))[None], rows, cols, height, width)
        live = jnp.roll(mask, (-SHIFT, -SHIFT), (0, 1))[None]
        qkv, mixed, proj, normed = attention_forward(shifted, labels, live, qkv_weight, proj_weight, logit_scale, bias_table, gain_attn)
        added = jnp.roll(normed, (SHIFT, SHIFT), (1, 2))
        hidden = (x.astype(jnp.float32) + added.astype(jnp.float32)).astype(jnp.bfloat16)
        quads, pre, merged = merge_forward(hidden, merge_weight, gain_merge)
        grad_mw, grad_hidden = merge_backward(quads, pre, seed_grad[None], merge_weight, gain_merge, 1, height, width)
        grad_normed = jnp.roll(grad_hidden, (-SHIFT, -SHIFT), (1, 2))
        grad_qw, grad_pw, grad_table, grad_shifted = attention_backward(shifted, labels, live, qkv, mixed, proj, grad_normed, qkv_weight, proj_weight, logit_scale, bias_table, gain_attn)
        grad_x = grad_hidden.astype(jnp.float32) + jnp.roll(grad_shifted, (SHIFT, SHIFT), (1, 2)).astype(jnp.float32)
        totals = (totals[0] + grad_qw, totals[1] + grad_pw, totals[2] + grad_mw, totals[3] + grad_table)
        return (totals, (merged[0], grad_x.astype(jnp.bfloat16)[0]))
    start = (jnp.zeros(qkv_weight.shape, jnp.float32), jnp.zeros(proj_weight.shape, jnp.float32), jnp.zeros(merge_weight.shape, jnp.float32), jnp.zeros(bias_table.shape, jnp.float32))
    totals, outputs = lax.scan(one_image, start, (tokens, region, valid, cotangent))
    return (outputs[0], outputs[1], totals[0], totals[1], totals[2], totals[3])
```

```python
import functools

import jax
import jax.numpy as jnp
from jax import lax
from jax.experimental import pallas as pl
from jax.experimental.pallas import tpu as pltpu
from jax.sharding import PartitionSpec as P

WIN = 8
HEAD_DIM = 32
SHIFT = 4
OFFSETS = 225


def from_behind(value, axis, steps):
    count = lax.axis_size(axis)
    pairs = [(source, (source + steps) % count) for source in range(count)]
    return lax.ppermute(value, axis, pairs)


def split_windows(t):
    b, r, w = (t.shape[0], t.shape[1], t.shape[2])
    rest = t.shape[3:]
    t = t.reshape((b, r // WIN, WIN, w // WIN, WIN) + rest)
    order = (0, 1, 3, 2, 4) + tuple(range(5, t.ndim))
    t = t.transpose(order)
    return t.reshape((b * (r // WIN) * (w // WIN), WIN * WIN) + rest)


def join_windows(t, b, r, w):
    rest = t.shape[2:]
    t = t.reshape((b, r // WIN, w // WIN, WIN, WIN) + rest)
    order = (0, 1, 3, 2, 4) + tuple(range(5, t.ndim))
    return t.transpose(order).reshape((b, r, w) + rest)


def offsets_table():
    place = jnp.arange(WIN * WIN, dtype=jnp.int32)
    prow = place // WIN
    pcol = place % WIN
    rel = (
        (prow[:, None] - prow[None, :] + WIN - 1) * (2 * WIN - 1)
        + pcol[:, None]
        - pcol[None, :]
        + WIN
        - 1
    )
    return (rel[None, :, :] == jnp.arange(OFFSETS, dtype=jnp.int32)[:, None, None]).astype(
        jnp.float32
    )


def wrap_part(index, extent):
    return jnp.where(index < extent - WIN, 0, jnp.where(index < extent - SHIFT, 1, 2)).astype(
        jnp.int32
    )


def region_labels(swath, rows, cols, height, width):
    return (
        swath * 9
        + wrap_part(rows, height)[None, :, None] * 3
        + wrap_part(cols, width)[None, None, :]
    )


def layer_norm(t, gain):
    centred = t - jnp.mean(t, -1, keepdims=True)
    spread = jnp.mean(centred * centred, -1, keepdims=True)
    return (centred * lax.rsqrt(spread + 1e-05) * gain).astype(jnp.bfloat16)


def attend(qkv, labels, valid, logit_scale, bias_table):
    b, r, w, three = qkv.shape
    width = three // 3
    heads = width // HEAD_DIM
    windows = split_windows(qkv).reshape(-1, WIN * WIN, 3, heads, HEAD_DIM)
    query = windows[:, :, 0].astype(jnp.float32)
    keys = windows[:, :, 1].astype(jnp.float32)
    values = windows[:, :, 2].astype(jnp.float32)
    query = query * lax.rsqrt(jnp.sum(query * query, -1, keepdims=True) + 1e-06)
    keys = keys * lax.rsqrt(jnp.sum(keys * keys, -1, keepdims=True) + 1e-06)
    scores = jnp.einsum("nihd,njhd->nhij", query, keys, precision=lax.Precision.HIGHEST)
    scores = scores * logit_scale[None, :, None, None]
    bias = jnp.einsum("hk,kij->hij", bias_table, offsets_table(), precision=lax.Precision.HIGHEST)
    scores = scores + bias[None]
    label_win = split_windows(labels)
    live_win = split_windows(valid)
    diagonal = jnp.eye(WIN * WIN, dtype=bool)
    allowed = (label_win[:, :, None] == label_win[:, None, :]) & (
        (live_win[:, None, :] == 1) | diagonal[None]
    )
    scores = jnp.where(allowed[:, None], scores, -1000000000.0)
    top = lax.stop_gradient(jnp.max(scores, -1, keepdims=True))
    expo = jnp.exp(scores - top)
    probs = (expo / jnp.sum(expo, -1, keepdims=True)).astype(jnp.bfloat16)
    mixed = jnp.einsum(
        "nhij,njhd->nihd", probs.astype(jnp.float32), values, precision=lax.Precision.HIGHEST
    )
    mixed = mixed.astype(jnp.bfloat16).reshape(-1, WIN * WIN, width)
    return join_windows(mixed, b, r, w)


def attention_forward(
    shifted, labels, valid, qkv_weight, proj_weight, logit_scale, bias_table, gain_attn
):
    b, r, w, c = shifted.shape
    qkv = jnp.dot(shifted.reshape(-1, c), qkv_weight, preferred_element_type=jnp.float32)
    qkv = qkv.astype(jnp.bfloat16).reshape(b, r, w, 3 * c)
    mixed = attend(qkv, labels, valid, logit_scale, bias_table)
    proj = jnp.dot(mixed.reshape(-1, c), proj_weight, preferred_element_type=jnp.float32)
    return (qkv, mixed, proj, layer_norm(proj, gain_attn).reshape(b, r, w, c))


def fold_quads(hidden):
    b, r, w, c = hidden.shape
    t = hidden.reshape(b, r // 2, 2, w // 2, 2, c).transpose(0, 1, 3, 4, 2, 5)
    return t.reshape(b * (r // 2) * (w // 2), 4 * c)


def unfold_quads(t, b, r, w):
    c = t.shape[-1] // 4
    t = t.reshape(b, r // 2, w // 2, 2, 2, c).transpose(0, 1, 4, 2, 3, 5)
    return t.reshape(b, r, w, c)


def merge_forward(hidden, merge_weight, gain_merge):
    b, r, w, c = hidden.shape
    quads = fold_quads(hidden)
    pre = jnp.dot(quads, merge_weight, preferred_element_type=jnp.float32)
    return (quads, pre, layer_norm(pre, gain_merge).reshape(b, r // 2, w // 2, 2 * c))


def merge_backward(quads, pre, seed_grad, merge_weight, gain_merge, b, r, w):
    _, back = jax.vjp(lambda t: layer_norm(t, gain_merge), pre)
    (grad_pre,) = back(seed_grad.reshape(pre.shape[0], pre.shape[1]))
    grad_pre = grad_pre.astype(jnp.bfloat16)
    grad_weight = jnp.dot(quads.T, grad_pre, preferred_element_type=jnp.float32)
    grad_quads = jnp.dot(grad_pre, merge_weight.T, preferred_element_type=jnp.float32).astype(
        jnp.bfloat16
    )
    return (grad_weight, unfold_quads(grad_quads, b, r, w))


def attention_backward(
    shifted,
    labels,
    valid,
    qkv,
    mixed,
    proj,
    grad_normed,
    qkv_weight,
    proj_weight,
    logit_scale,
    bias_table,
    gain_attn,
):
    b, r, w, c = shifted.shape
    _, back = jax.vjp(lambda t: layer_norm(t, gain_attn), proj)
    (grad_out,) = back(grad_normed.reshape(-1, c))
    grad_out = grad_out.astype(jnp.bfloat16)
    grad_pw = jnp.dot(mixed.reshape(-1, c).T, grad_out, preferred_element_type=jnp.float32)
    grad_mixed = jnp.dot(grad_out, proj_weight.T, preferred_element_type=jnp.float32)
    grad_mixed = grad_mixed.astype(jnp.bfloat16).reshape(b, r, w, c)
    _, back = jax.vjp(
        lambda t, table: attend(t, labels, valid, logit_scale, table), qkv, bias_table
    )
    grad_act, grad_table = back(grad_mixed)
    grad_act = grad_act.reshape(-1, 3 * c)
    grad_qw = jnp.dot(shifted.reshape(-1, c).T, grad_act, preferred_element_type=jnp.float32)
    grad_shifted = jnp.dot(grad_act, qkv_weight.T, preferred_element_type=jnp.float32)
    return (grad_qw, grad_pw, grad_table, grad_shifted.astype(jnp.bfloat16).reshape(b, r, w, c))


def from_next(strip):
    incoming = from_behind(strip[:, :SHIFT], "space", -1)
    return jnp.roll(jnp.concatenate([strip[:, SHIFT:], incoming], axis=1), -SHIFT, axis=2)


def from_previous(strip):
    incoming = from_behind(strip[:, SHIFT:], "space", 1)
    return jnp.roll(jnp.concatenate([incoming, strip[:, :SHIFT]], axis=1), SHIFT, axis=2)


NX, NY, NZ, CORES = 4, 4, 8, 2
LANES = 128
MESH = pl.DeviceIdType.MESH


class Place:
    def __init__(self):
        strip, image = lax.axis_index("space"), lax.axis_index("dp")
        self.y, self.z = strip // NZ, lax.rem(strip, NZ)
        self.x, self.c = image // CORES, lax.rem(image, CORES)

    def at(self, x=None, y=None, z=None, c=None):
        x = self.x if x is None else x
        y = self.y if y is None else y
        z = self.z if z is None else z
        c = self.c if c is None else c
        return (y * NZ + z, x * CORES + c)

    def along(self, axis, step):
        count = {"x": NX, "y": NY, "z": NZ, "c": CORES}[axis]
        return self.at(**{axis: lax.rem(getattr(self, axis) + step, count)})

    def partners(self):
        return (
            [self.along("c", 1)]
            + [self.along("x", step) for step in range(1, NX)]
            + [self.along("y", step) for step in range(1, NY)]
            + [self.along("z", step) for step in range(1, NZ)]
        )


class Sems:
    def __init__(self, send, recv):
        self.send, self.recv, self.used = send, recv, 0

    def copy(self, source, target, device):
        index = self.used
        self.used += 1
        made = pltpu.make_async_remote_copy(
            src_ref=source,
            dst_ref=target,
            send_sem=self.send.at[index],
            recv_sem=self.recv.at[index],
            device_id=device,
            device_id_type=MESH,
        )
        made.start()
        return made


def add_blocks(count, put, parts):
    def body(index, carry):
        total = parts[0](index).astype(jnp.float32)
        for part in parts[1:]:
            total = total + part(index).astype(jnp.float32)
        put(index, total.astype(jnp.bfloat16))
        return carry

    lax.fori_loop(0, count, body, 0)


def ring_sum(place, sems, axis, held, halves, blocks, far_lo, far_hi, from_dn, from_up, out):
    me = getattr(place, axis)
    up, dn, far = lax.rem(me + 1, 4), lax.rem(me + 3, 4), lax.rem(me + 2, 4)
    to_up, to_dn = place.along(axis, 1), place.along(axis, 3)
    half = blocks // 2
    lo, hi = pl.ds(0, half), pl.ds(half, half)
    one = sems.copy(held.at[far, lo], far_lo, to_up)
    two = sems.copy(held.at[far, hi], far_hi, to_dn)
    three = sems.copy(held.at[up, hi], from_dn.at[hi], to_up)
    four = sems.copy(held.at[dn, lo], from_up.at[lo], to_dn)
    yield

    def put_up(i, v):
        held[up, i] = v

    def put_dn(i, v):
        held[dn, half + i] = v

    one.wait_recv()
    add_blocks(half, put_up, [lambda i: held[up, i], lambda i: far_lo[i]])
    five = sems.copy(held.at[up, lo], from_dn.at[lo], to_up)
    yield
    two.wait_recv()
    add_blocks(half, put_dn, [lambda i: held[dn, half + i], lambda i: far_hi[i]])
    six = sems.copy(held.at[dn, hi], from_up.at[hi], to_dn)
    yield
    three.wait_recv()
    four.wait_recv()
    five.wait_recv()
    six.wait_recv()

    def put_out(i, v):
        out[i] = v

    add_blocks(
        blocks, put_out, [lambda i: held[me, i], lambda i: from_dn[i], lambda i: from_up[i]]
    )
    for copy in (one, two, three, four, five, six):
        copy.wait_send()


def stream_scratch(rows):
    full = NZ * rows
    shapes = [
        (4, 4, full, LANES),
        (4, 4, full, LANES),
        (2, full, LANES),
        (2, full, LANES),
        (4, full, LANES),
        (4, full, LANES),
        (4, NZ, rows, LANES),
        (NZ // 2, rows, LANES),
        (NZ // 2, rows, LANES),
        (NZ, rows, LANES),
        (NZ, rows, LANES),
        (NZ, rows, LANES),
        (NZ, rows, LANES),
    ]
    return [pltpu.VMEM(shape, jnp.bfloat16) for shape in shapes]


STREAM_COPIES = 1 + 6 + 6 + (NZ - 1)


def stream(place, sems, first, second, rows, source, out, bufs):
    other, core, a1, a2, a3, a4, one, b1, b2, b3, b4, two, last = bufs
    mine = place.c
    cross = sems.copy(source.at[1 - mine], other, place.along("c", 1))
    yield
    cross.wait_recv()

    def put_core(i, v):
        core[i // 4, lax.rem(i, 4)] = v

    add_blocks(
        16,
        put_core,
        [
            lambda i: source[mine, i // 4, lax.rem(i, 4)],
            lambda i: other[i // 4, lax.rem(i, 4)],
        ],
    )

    class Fold:
        def __setitem__(self, i, v):
            one[i] = v.reshape(NZ, rows, LANES)

    yield from ring_sum(place, sems, first, core, None, 4, a1, a2, a3, a4, Fold())
    yield from ring_sum(place, sems, second, one, None, NZ, b1, b2, b3, b4, two)
    sent = []
    for step in range(1, NZ):
        target = lax.rem(place.z + step, NZ)
        sent.append(sems.copy(two.at[target], last.at[step], place.along("z", step)))
    yield
    total = two[place.z].astype(jnp.float32)
    for step in range(1, NZ):
        sent[step - 1].wait_recv()
        total = total + last[step].astype(jnp.float32)
    out[...] = total
    for copy in sent:
        copy.wait_send()
    cross.wait_send()


BIAS_ROWS, BIAS_LANES = 16, 256
BIAS_COPIES = 1 + (NX - 1) + (NY - 1) + (NZ - 1)


def bias_scratch():
    return [
        pltpu.VMEM((count, BIAS_ROWS, BIAS_LANES), jnp.float32)
        for count in (CORES, NX, NY, NZ)
    ]


def bias_sum(place, sems, value, out, bufs):
    copies = []
    for axis, count, buf in zip("cxyz", (CORES, NX, NY, NZ), bufs):
        me = getattr(place, axis)
        buf[me] = value
        sent = [
            sems.copy(buf.at[me], buf.at[me], place.along(axis, step)) for step in range(1, count)
        ]
        yield
        for copy in sent:
            copy.wait_recv()
        value = buf[0]
        for index in range(1, count):
            value = value + buf[index]
        copies += sent
    out[...] = value
    for copy in copies:
        copy.wait_send()


def run_all(tasks):
    tasks = list(tasks)
    while tasks:
        for task in list(tasks):
            try:
                next(task)
            except StopIteration:
                tasks.remove(task)


def enter(partners):
    barrier = pltpu.get_barrier_semaphore()
    for device in partners:
        pl.semaphore_signal(barrier, inc=1, device_id=device, device_id_type=MESH)
    pl.semaphore_wait(barrier, len(partners))


def sum_kernel(rows, sa_ref, sb_ref, bias_ref, out_a, out_b, out_bias, *scratch):
    count = len(stream_scratch(rows))
    bufs_a, bufs_b = scratch[:count], scratch[count : 2 * count]
    bias_bufs = scratch[2 * count : 2 * count + 4]
    send, recv = scratch[2 * count + 4 :]
    place = Place()
    sems = Sems(send, recv)
    enter(place.partners())
    run_all(
        [
            stream(place, sems, "x", "y", rows, sa_ref, out_a, bufs_a),
            stream(place, sems, "y", "x", rows, sb_ref, out_b, bufs_b),
            bias_sum(place, sems, bias_ref[...], out_bias, bias_bufs),
        ]
    )


def sum_all(rows, sa, sb, bias):
    total = 2 * STREAM_COPIES + BIAS_COPIES
    vmem = pl.BlockSpec(memory_space=pltpu.VMEM)
    return pl.pallas_call(
        functools.partial(sum_kernel, rows),
        out_shape=[
            jax.ShapeDtypeStruct((rows, LANES), jnp.float32),
            jax.ShapeDtypeStruct((rows, LANES), jnp.float32),
            jax.ShapeDtypeStruct((BIAS_ROWS, BIAS_LANES), jnp.float32),
        ],
        in_specs=[vmem] * 3,
        out_specs=[vmem] * 3,
        scratch_shapes=stream_scratch(rows)
        + stream_scratch(rows)
        + bias_scratch()
        + [pltpu.SemaphoreType.DMA((total,)), pltpu.SemaphoreType.DMA((total,))],
        compiler_params=pltpu.CompilerParams(
            collective_id=0, has_side_effects=True, vmem_limit_bytes=48 * 1024 * 1024
        ),
        name="sum_all",
    )(sa, sb, bias)

def sum_grads(grad_qw, grad_pw, grad_mw, grad_table):
    merge = grad_mw.astype(jnp.bfloat16).reshape(NY, NZ, 2, 32, NX, CORES, LANES)
    merge = merge.transpose(2, 5, 4, 0, 1, 3, 6)
    both = jnp.concatenate(
        [
            grad_qw.astype(jnp.bfloat16).reshape(512, NX, CORES, 192),
            grad_pw.astype(jnp.bfloat16).reshape(512, NX, CORES, 64),
        ],
        axis=-1,
    )
    both = both.reshape(NY, NZ, 16, NX, CORES, 2, LANES).transpose(5, 4, 3, 0, 1, 2, 6)
    packed = jnp.concatenate([merge, both], axis=5)
    sa = packed[0].reshape(CORES, NX, NY, NZ * 48, LANES)
    sb = packed[1].transpose(0, 2, 1, 3, 4, 5).reshape(CORES, NY, NX, NZ * 48, LANES)
    bias = jnp.pad(grad_table, ((0, 0), (0, BIAS_LANES - OFFSETS)))
    out_a, out_b, out_bias = sum_all(48, sa, sb, bias)
    grad_merge = jnp.concatenate([out_a[:32], out_b[:32]], axis=0)
    both = jnp.concatenate([out_a[32:], out_b[32:]], axis=1)
    return both[:, :192], both[:, 192:], grad_merge, out_bias[:, :OFFSETS]


def shards(
    tokens,
    region,
    valid,
    qkv_weight,
    proj_weight,
    merge_weight,
    logit_scale,
    bias_table,
    gain_attn,
    gain_merge,
    cotangent,
):
    place = lax.axis_index("space")
    images, rows_dev, width, channels = tokens.shape
    height = rows_dev * lax.axis_size("space")
    rows = place * rows_dev + jnp.arange(rows_dev, dtype=jnp.int32)
    cols = jnp.arange(width, dtype=jnp.int32)
    source_rows = (rows + SHIFT) % height
    swath = jnp.take(region, source_rows // 4, axis=1)
    swath = jnp.roll(jnp.repeat(swath, 4, axis=2), -SHIFT, axis=2)
    labels = region_labels(swath, rows, cols, height, width)
    live = jnp.roll(jnp.take(valid, source_rows, axis=1), -SHIFT, axis=2)
    shifted = from_next(tokens)
    qkv, mixed, proj, normed = attention_forward(
        shifted, labels, live, qkv_weight, proj_weight, logit_scale, bias_table, gain_attn
    )
    added = from_previous(normed)
    hidden = (tokens.astype(jnp.float32) + added.astype(jnp.float32)).astype(jnp.bfloat16)
    quads, pre, merged = merge_forward(hidden, merge_weight, gain_merge)
    grad_mw, grad_hidden = merge_backward(
        quads, pre, cotangent, merge_weight, gain_merge, images, rows_dev, width
    )
    grad_normed = from_next(grad_hidden)
    grad_qw, grad_pw, grad_table, grad_shifted = attention_backward(
        shifted,
        labels,
        live,
        qkv,
        mixed,
        proj,
        grad_normed,
        qkv_weight,
        proj_weight,
        logit_scale,
        bias_table,
        gain_attn,
    )
    grad_back = from_previous(grad_shifted)
    grad_tokens = (grad_hidden.astype(jnp.float32) + grad_back.astype(jnp.float32)).astype(
        jnp.bfloat16
    )
    grad_qkv, grad_proj, grad_merge, grad_bias = sum_grads(grad_qw, grad_pw, grad_mw, grad_table)
    return (merged, grad_tokens, grad_qkv, grad_proj, grad_merge, grad_bias)


def solution(mesh):
    return jax.shard_map(
        shards,
        mesh=mesh,
        in_specs=(
            P("dp", "space", None, None),
            P("dp", None, None),
            P("dp", None, None),
            P(),
            P(),
            P(),
            P(),
            P(),
            P(),
            P(),
            P("dp", "space", None, None),
        ),
        out_specs=(
            P("dp", "space", None, None),
            P("dp", "space", None, None),
            P("space", "dp"),
            P("space", "dp"),
            P("space", "dp"),
            P(),
        ),
        check_vma=False,
    )
```

```python
import jax
import jax.numpy as jnp
import numpy as np
from jax import lax
from jax.experimental import pallas as pl
from jax.experimental.pallas import tpu as pltpu
from jax.sharding import PartitionSpec as P

WIN = 8
HEAD_DIM = 32
SHIFT = 4
OFFSETS = 225
NX, NY, NZ, CORES = 4, 4, 8, 2
LANES = 128
MESH = pl.DeviceIdType.MESH


class Place:
    def __init__(self):
        strip, image = lax.axis_index("space"), lax.axis_index("dp")
        self.y, self.z = strip // NZ, lax.rem(strip, NZ)
        self.x, self.c = image // CORES, lax.rem(image, CORES)

    def at(self, x=None, y=None, z=None, c=None):
        x = self.x if x is None else x
        y = self.y if y is None else y
        z = self.z if z is None else z
        c = self.c if c is None else c
        return (y * NZ + z, x * CORES + c)

    def along(self, axis, step):
        count = {"x": NX, "y": NY, "z": NZ, "c": CORES}[axis]
        return self.at(**{axis: lax.rem(getattr(self, axis) + step, count)})

    def partners(self):
        return (
            [self.along("c", 1)]
            + [self.along("x", step) for step in range(1, NX)]
            + [self.along("y", step) for step in range(1, NY)]
            + [self.along("z", step) for step in range(1, NZ)]
        )


class Sems:
    def __init__(self, send, recv):
        self.send, self.recv, self.used = send, recv, 0

    def copy(self, source, target, device):
        index = self.used
        self.used += 1
        made = pltpu.make_async_remote_copy(
            src_ref=source,
            dst_ref=target,
            send_sem=self.send.at[index],
            recv_sem=self.recv.at[index],
            device_id=device,
            device_id_type=MESH,
        )
        made.start()
        return made


def add_blocks(count, put, parts):
    def body(index, carry):
        total = parts[0](index).astype(jnp.float32)
        for part in parts[1:]:
            total = total + part(index).astype(jnp.float32)
        put(index, total.astype(jnp.bfloat16))
        return carry

    lax.fori_loop(0, count, body, 0)


def ring_sum(place, sems, axis, held, halves, blocks, far_lo, far_hi, from_dn, from_up, out):
    me = getattr(place, axis)
    up, dn, far = lax.rem(me + 1, 4), lax.rem(me + 3, 4), lax.rem(me + 2, 4)
    to_up, to_dn = place.along(axis, 1), place.along(axis, 3)
    half = blocks // 2
    lo, hi = pl.ds(0, half), pl.ds(half, half)
    one = sems.copy(held.at[far, lo], far_lo, to_up)
    two = sems.copy(held.at[far, hi], far_hi, to_dn)
    three = sems.copy(held.at[up, hi], from_dn.at[hi], to_up)
    four = sems.copy(held.at[dn, lo], from_up.at[lo], to_dn)
    yield

    def put_up(i, v):
        held[up, i] = v

    def put_dn(i, v):
        held[dn, half + i] = v

    one.wait_recv()
    add_blocks(half, put_up, [lambda i: held[up, i], lambda i: far_lo[i]])
    five = sems.copy(held.at[up, lo], from_dn.at[lo], to_up)
    yield
    two.wait_recv()
    add_blocks(half, put_dn, [lambda i: held[dn, half + i], lambda i: far_hi[i]])
    six = sems.copy(held.at[dn, hi], from_up.at[hi], to_dn)
    yield
    three.wait_recv()
    four.wait_recv()
    five.wait_recv()
    six.wait_recv()

    def put_out(i, v):
        out[i] = v

    add_blocks(
        blocks, put_out, [lambda i: held[me, i], lambda i: from_dn[i], lambda i: from_up[i]]
    )
    for copy in (one, two, three, four, five, six):
        copy.wait_send()


def stream_scratch(rows):
    full = NZ * rows
    shapes = [
        (4, 4, full, LANES),
        (4, 4, full, LANES),
        (2, full, LANES),
        (2, full, LANES),
        (4, full, LANES),
        (4, full, LANES),
        (4, NZ, rows, LANES),
        (NZ // 2, rows, LANES),
        (NZ // 2, rows, LANES),
        (NZ, rows, LANES),
        (NZ, rows, LANES),
        (NZ, rows, LANES),
        (NZ, rows, LANES),
    ]
    return [pltpu.VMEM(shape, jnp.bfloat16) for shape in shapes]


STREAM_COPIES = 1 + 6 + 6 + (NZ - 1)


def stream(place, sems, first, second, rows, source, out, bufs):
    other, core, a1, a2, a3, a4, one, b1, b2, b3, b4, two, last = bufs
    mine = place.c
    cross = sems.copy(source.at[1 - mine], other, place.along("c", 1))
    yield
    cross.wait_recv()

    def put_core(i, v):
        core[i // 4, lax.rem(i, 4)] = v

    add_blocks(
        16,
        put_core,
        [
            lambda i: source[mine, i // 4, lax.rem(i, 4)],
            lambda i: other[i // 4, lax.rem(i, 4)],
        ],
    )

    class Fold:
        def __setitem__(self, i, v):
            one[i] = v.reshape(NZ, rows, LANES)

    yield from ring_sum(place, sems, first, core, None, 4, a1, a2, a3, a4, Fold())
    yield from ring_sum(place, sems, second, one, None, NZ, b1, b2, b3, b4, two)
    sent = []
    for step in range(1, NZ):
        target = lax.rem(place.z + step, NZ)
        sent.append(sems.copy(two.at[target], last.at[step], place.along("z", step)))
    yield
    total = two[place.z].astype(jnp.float32)
    for step in range(1, NZ):
        sent[step - 1].wait_recv()
        total = total + last[step].astype(jnp.float32)
    out[...] = total
    for copy in sent:
        copy.wait_send()
    cross.wait_send()


BIAS_ROWS, BIAS_LANES = 16, 256
BIAS_COPIES = 1 + (NX - 1) + (NY - 1) + (NZ - 1)


def bias_scratch():
    return [
        pltpu.VMEM((count, BIAS_ROWS, BIAS_LANES), jnp.float32)
        for count in (CORES, NX, NY, NZ)
    ]


def bias_sum(place, sems, value, out, bufs):
    copies = []
    for axis, count, buf in zip("cxyz", (CORES, NX, NY, NZ), bufs):
        me = getattr(place, axis)
        buf[me] = value
        sent = [
            sems.copy(buf.at[me], buf.at[me], place.along(axis, step)) for step in range(1, count)
        ]
        yield
        for copy in sent:
            copy.wait_recv()
        value = buf[0]
        for index in range(1, count):
            value = value + buf[index]
        copies += sent
    out[...] = value
    for copy in copies:
        copy.wait_send()


def run_all(tasks):
    tasks = list(tasks)
    while tasks:
        for task in list(tasks):
            try:
                next(task)
            except StopIteration:
                tasks.remove(task)


def enter(partners):
    barrier = pltpu.get_barrier_semaphore()
    for device in partners:
        pl.semaphore_signal(barrier, inc=1, device_id=device, device_id_type=MESH)
    pl.semaphore_wait(barrier, len(partners))


F32, BF16 = jnp.float32, jnp.bfloat16
TOKENS, D, GROUPS = 256, 512, 4
HALF = TOKENS // 2
PLACES = WIN * WIN
WIDE = 4 * PLACES


def nn(a, b):
    return lax.dot_general(a, b, (((1,), (0,)), ((), ())), preferred_element_type=F32)


def nt(a, b):
    return lax.dot_general(a, b, (((1,), (1,)), ((), ())), preferred_element_type=F32)


def tn(a, b):
    return lax.dot_general(a, b, (((0,), (0,)), ((), ())), preferred_element_type=F32)


def split2(t):
    high = t.astype(BF16)
    return high, (t - high.astype(F32)).astype(BF16)


def split3(t):
    high = t.astype(BF16)
    rest = t - high.astype(F32)
    middle = rest.astype(BF16)
    return high, middle, (rest - middle.astype(F32)).astype(BF16)


def iota(shape, axis):
    return lax.broadcasted_iota(jnp.int32, shape, axis)


def constants():
    half, w, r, c = np.meshgrid(*[np.arange(n) for n in (2, 4, 4, 8)], indexing="ij")
    natural = (half * 4 + r) * 32 + (w * 8 + c + SHIFT) % 32
    strip = np.eye(TOKENS, dtype=np.float32)[natural.reshape(-1)]
    k, rp, b = np.meshgrid(np.arange(4), np.arange(2), np.arange(16), indexing="ij")
    column = (2 * b + k // 2 - SHIFT) % 32
    place = (column // 8) * 32 + (2 * rp + k % 2) * 8 + column % 8
    quad = np.eye(HALF, dtype=np.float32)[place.reshape(-1)]
    ct, lane = np.meshgrid(np.arange(8), np.arange(128), indexing="ij")
    offset = np.where(lane < 120, (lane // 8) * 15 + lane % 8 - ct + 7, -1)
    onehot = (np.arange(256)[:, None] == offset.reshape(1, -1)).astype(np.float32)
    lanes = np.arange(256) % 128 // HEAD_DIM
    heads = (lanes[:, None] == lanes[None, :128]).astype(np.float32)
    return [jnp.asarray(t, BF16) for t in (strip, quad, onehot, heads)]


def head_sum(t, heads):
    return nn(jnp.concatenate(split2(t), axis=1), heads)


def stack_heads(t, lane_masks):
    return jnp.concatenate([t * mask for mask in lane_masks], axis=0)


def fold_heads(t, lane_masks):
    total = t[:PLACES] * lane_masks[0]
    for h in range(1, 4):
        total = total + t[h * PLACES : (h + 1) * PLACES] * lane_masks[h]
    return total


def norm_parts(t):
    centred = t - jnp.mean(t, -1, keepdims=True)
    scale = lax.rsqrt(jnp.mean(centred * centred, -1, keepdims=True) + 1e-05)
    return centred * scale, scale


def norm_back(grad, hat, scale):
    return scale * (
        grad - jnp.mean(grad, -1, keepdims=True) - hat * jnp.mean(grad * hat, -1, keepdims=True)
    )


def window_masks(place, region_ref, valid_ref, mask_ref):
    strip = place.y * NZ + place.z
    place_lane = iota((1, WIDE), 1) % PLACES
    row, col = place_lane // WIN, place_lane % WIN
    region = region_ref[...].astype(F32)
    valid = valid_ref[...].astype(F32)
    source_row = lax.rem(strip * WIN + SHIFT + row, 256)
    region_row = iota((64, WIDE), 0) == source_row // 4
    valid_row = iota((256, WIDE), 0) == source_row
    shifted_row = strip * WIN + row
    row_part = jnp.where(shifted_row < 256 - WIN, 0, jnp.where(shifted_row < 256 - SHIFT, 1, 2))
    diagonal = iota((PLACES, WIDE), 0) == place_lane
    pick = (iota((PLACES, WIDE), 0) == iota((PLACES, WIDE), 1)).astype(F32)
    for w in range(4):
        source_col = lax.rem(w * WIN + SHIFT + col, 32)
        shifted_col = w * WIN + col
        col_part = jnp.where(shifted_col < 32 - WIN, 0, jnp.where(shifted_col < 32 - SHIFT, 1, 2))
        region_pick = (iota((8, WIDE), 0) == source_col // 4).astype(F32)
        valid_pick = (iota((32, WIDE), 0) == source_col).astype(F32)
        swath = jnp.sum(jnp.where(region_row, nn(region, region_pick), 0.0), 0, keepdims=True)
        live = jnp.sum(jnp.where(valid_row, nn(valid, valid_pick), 0.0), 0, keepdims=True)
        label = swath * 9.0 + (row_part * 3 + col_part).astype(F32)
        label_key = jnp.sum(pick * label, 1, keepdims=True)
        live_key = jnp.sum(pick * live, 1, keepdims=True)
        same = (label_key == label).astype(F32)
        open_key = jnp.where(diagonal, 1.0, jnp.where(live_key == 1.0, 1.0, 0.0))
        mask_ref[w] = same * open_key


def spread_bias(table_ref, onehot_ref, padded_ref, grid_ref, bias_ref):
    padded_ref[...] = jnp.zeros_like(padded_ref)
    padded_ref[:, :OFFSETS] = table_ref[...]
    parts = nn(jnp.concatenate(split3(padded_ref[...]), axis=0), onehot_ref[...])
    spread = parts[:16] + parts[16:32] + parts[32:]
    for ct in range(8):
        grid_ref[pl.ds(ct, 16, stride=8), :] = spread[:, ct * 128 : (ct + 1) * 128]
    left = iota((8, 128), 1) < PLACES
    for pair in range(8):
        even = grid_ref[pair * 16 : pair * 16 + 8]
        odd = grid_ref[pair * 16 + 8 : pair * 16 + 16]
        lanes = pl.ds(pair % 2 * 128, 128)
        for rt in range(8):
            shift = (7 - rt) * 8
            bias_ref[pair // 2, rt * 8 : rt * 8 + 8, lanes] = jnp.where(
                left,
                pltpu.roll(even, (128 - shift) % 128, 1),
                pltpu.roll(odd, (128 + 64 - shift) % 128, 1),
            )


def gather_bias(acc_ref, onehot_ref, grid_ref):
    left = iota((8, 128), 1) < PLACES
    for pair in range(8):
        lanes = pl.ds(pair % 2 * 128, 128)
        even = jnp.zeros((8, 128), F32)
        odd = jnp.zeros((8, 128), F32)
        for rt in range(8):
            shift = (7 - rt) * 8
            piece = acc_ref[pair // 2, rt * 8 : rt * 8 + 8, lanes]
            even = even + pltpu.roll(jnp.where(left, piece, 0.0), shift, 1)
            odd = odd + pltpu.roll(jnp.where(left, 0.0, piece), (64 + shift) % 128, 1)
        grid_ref[pair * 16 : pair * 16 + 8] = even
        grid_ref[pair * 16 + 8 : pair * 16 + 16] = odd
    grid = jnp.concatenate([grid_ref[pl.ds(ct, 16, stride=8), :] for ct in range(8)], axis=1)
    parts = nt(jnp.concatenate(split3(grid), axis=0), onehot_ref[...])
    return parts[:16] + parts[16:32] + parts[32:]


def window_rows(w):
    return (
        pl.ds(pl.multiple_of(w * 32, 32), 32),
        pl.ds(pl.multiple_of(HALF + w * 32, 32), 32),
    )


def take(ref, w, start):
    first, second = window_rows(w)
    lanes = slice(start, start + LANES)
    return jnp.concatenate([ref[first, lanes], ref[second, lanes]], axis=0)


def put(ref, w, start, value):
    first, second = window_rows(w)
    lanes = slice(start, start + LANES)
    ref[first, lanes] = value[:32]
    ref[second, lanes] = value[32:]


def block_kernel(
    tok_ref,
    region_ref,
    valid_ref,
    wq_ref,
    wp_ref,
    wm_hbm,
    scale_ref,
    table_ref,
    gain_attn_ref,
    gain_merge_ref,
    cot_ref,
    strip_ref,
    quad_ref,
    onehot_ref,
    heads_ref,
    merged_out,
    tokens_out,
    qkv_out,
    proj_out,
    merge_out,
    bias_out,
    wm_ref,
    tw_ref,
    x_ref,
    qkv_ref,
    inv_ref,
    qh_ref,
    ql_ref,
    kh_ref,
    kl_ref,
    mask_ref,
    padded_ref,
    grid_ref,
    bias_ref,
    probs_ref,
    mixed_ref,
    normed_ref,
    hat_ref,
    normed_in,
    quads_ref,
    gh_ref,
    gn_ref,
    go_ref,
    roll_ref,
    gm_ref,
    dn_ref,
    act_ref,
    gs_ref,
    gs_in,
    acc_ref,
    sum_a,
    sum_b,
    part_a,
    part_b,
    sum_c,
    sum_d,
    *scratch,
):
    many = len(stream_scratch(32))
    bufs = [scratch[i * many : (i + 1) * many] for i in range(4)]
    bias_bufs = scratch[4 * many : 4 * many + 4]
    send, recv, local = scratch[4 * many + 4 :]
    place = Place()
    sems = Sems(send, recv)
    load = pltpu.make_async_copy(wm_hbm, wm_ref, local)
    load.start()

    strip = place.y * NZ + place.z
    image = place.x * CORES + place.c
    after = (lax.rem(strip + 1, NY * NZ), image)
    before = (lax.rem(strip + NY * NZ - 1, NY * NZ), image)
    own, far = slice(0, HALF), slice(HALF, TOKENS)

    tw_ref[...] = nn(strip_ref[...], tok_ref[...]).astype(BF16)
    enter(place.partners() + [after, before])
    halo_tokens = sems.copy(tw_ref.at[own], x_ref.at[far], before)
    x_ref[own] = tw_ref[far]

    lane = iota((1, LANES), 1)
    masks = [(lane // HEAD_DIM == h).astype(F32) for h in range(4)]
    masks16 = [mask.astype(BF16) for mask in masks]
    scales = []
    for g in range(GROUPS):
        row = jnp.zeros((1, LANES), F32)
        for h in range(4):
            row = row + masks[h] * scale_ref[g * 4 + h]
        scales.append(row)
    heads = heads_ref[...]

    qkv_ref[own] = nn(x_ref[own], wq_ref[...]).astype(BF16)
    window_masks(place, region_ref, valid_ref, mask_ref)
    spread_bias(table_ref, onehot_ref, padded_ref, grid_ref, bias_ref)
    halo_tokens.wait_recv()
    qkv_ref[far] = nn(x_ref[far], wq_ref[...]).astype(BF16)

    for g in range(GROUPS):
        cols = slice(g * LANES, (g + 1) * LANES)
        for part, high, low in ((0, qh_ref, ql_ref), (D, kh_ref, kl_ref)):
            raw = qkv_ref[:, part + g * LANES : part + (g + 1) * LANES].astype(F32)
            inverse = lax.rsqrt(head_sum(raw * raw, heads) + 1e-06)
            inv_ref[:, part + g * LANES : part + (g + 1) * LANES] = inverse
            unit = raw * inverse
            if part == 0:
                unit = unit * scales[g]
            a, b = split2(unit)
            high[:, cols] = a
            low[:, cols] = b

    def forward(w, carry):
        allowed = mask_ref[w] > 0.5
        for g in range(GROUPS):
            start = g * LANES
            kh, kl = take(kh_ref, w, start), take(kl_ref, w, start)
            qh = stack_heads(take(qh_ref, w, start), masks16)
            ql = stack_heads(take(ql_ref, w, start), masks16)
            score = nt(
                jnp.concatenate([kh, kl, kh], axis=1), jnp.concatenate([qh, qh, ql], axis=1)
            )
            score = jnp.where(allowed, score + bias_ref[g], -1000000000.0)
            expo = jnp.exp(score - jnp.max(score, 0, keepdims=True))
            probs = expo * (1.0 / jnp.sum(expo, 0, keepdims=True))
            probs_ref[w, g] = probs
            out = tn(probs.astype(BF16), take(qkv_ref, w, 2 * D + start))
            put(mixed_ref, w, start, fold_heads(out, masks).astype(BF16))
        return carry

    lax.fori_loop(0, 4, forward, 0)

    gain_attn = gain_attn_ref[...]

    def project(rows):
        hat, scale = norm_parts(nn(mixed_ref[rows], wp_ref[...]))
        hat_ref[rows] = hat
        normed_ref[rows] = (hat * gain_attn).astype(BF16)
        return scale

    scale_far = project(far)
    halo_normed = sems.copy(normed_ref.at[far], normed_in, after)
    scale_own = project(own)

    def make_quads(which, added):
        rows = slice(which * HALF, (which + 1) * HALF)
        hidden = (tw_ref[rows].astype(F32) + added.astype(F32)).astype(BF16)
        sorted_rows = nn(quad_ref[...], hidden).astype(BF16)
        for k in range(4):
            quads_ref[which * 32 : which * 32 + 32, k * D : (k + 1) * D] = sorted_rows[
                k * 32 : (k + 1) * 32
            ]

    make_quads(1, normed_ref[own])
    load.wait()
    halo_normed.wait_recv()
    make_quads(0, normed_in[...])

    gain_merge = gain_merge_ref[...]
    hat, scale = norm_parts(nn(quads_ref[...], wm_ref[...]))
    merged_out[...] = (hat * gain_merge).astype(BF16)
    grad_pre = norm_back(cot_ref[...].astype(F32) * gain_merge, hat, scale).astype(BF16)
    grad_quads = nt(grad_pre, wm_ref[...]).astype(BF16)
    for which in range(2):
        stacked = jnp.concatenate(
            [grad_quads[which * 32 : which * 32 + 32, k * D : (k + 1) * D] for k in range(4)],
            axis=0,
        )
        gh_ref[which * HALF : (which + 1) * HALF] = tn(quad_ref[...], stacked).astype(BF16)
        if which == 0:
            halo_hidden = sems.copy(gh_ref.at[own], gn_ref.at[far], before)
    gn_ref[own] = gh_ref[far]

    for x in range(NX):
        for y in range(NY):
            block = tn(
                quads_ref[:, y * D : (y + 1) * D], grad_pre[:, x * 256 : (x + 1) * 256]
            ).reshape(NZ, 2, 32, 256)
            for c in range(CORES):
                lanes = slice(c * LANES, (c + 1) * LANES)
                sum_a[c, x, y] = block[:, 0, :, lanes].reshape(NZ * 32, LANES).astype(BF16)
                sum_b[c, y, x] = block[:, 1, :, lanes].reshape(NZ * 32, LANES).astype(BF16)

    tasks = [
        stream(place, sems, "x", "y", 32, sum_a, merge_out.at[0:32], bufs[0]),
        stream(place, sems, "y", "x", 32, sum_b, merge_out.at[32:64], bufs[1]),
    ]

    def pump():
        for task in list(tasks):
            try:
                next(task)
            except StopIteration:
                tasks.remove(task)

    pump()

    def back_norm(rows, scale):
        grad = gn_ref[rows].astype(F32) * gain_attn
        out = norm_back(grad, hat_ref[rows], scale)
        go_ref[rows] = out.astype(BF16)
        for x in range(NX):
            lanes = slice(x * LANES, (x + 1) * LANES)
            roll_ref[rows, lanes] = pltpu.roll(out[:, lanes], 64, 1).astype(BF16)
        gm_ref[rows] = nt(go_ref[rows], wp_ref[...]).astype(BF16)

    back_norm(own, scale_own)
    halo_hidden.wait_recv()
    back_norm(far, scale_far)
    pump()

    acc_ref[...] = jnp.zeros_like(acc_ref)

    def backward(w, carry):
        for g in range(GROUPS):
            start = g * LANES
            grad = stack_heads(take(gm_ref, w, start), masks16)
            probs = probs_ref[w, g]
            grad_probs = nt(take(qkv_ref, w, 2 * D + start), grad)
            put(act_ref, w, 2 * D + start, nn(probs.astype(BF16), grad).astype(BF16))
            weighted = probs * grad_probs
            grad_score = weighted - probs * jnp.sum(weighted, 0, keepdims=True)
            acc_ref[g] += grad_score
            grad_score = grad_score.astype(BF16)
            query = stack_heads(take(qh_ref, w, start), masks16)
            put(dn_ref, w, D + start, nn(grad_score, query))
            put(dn_ref, w, start, fold_heads(tn(grad_score, take(kh_ref, w, start)), masks))
        return carry

    lax.fori_loop(0, 2, backward, 0)
    pump()
    lax.fori_loop(2, 4, backward, 0)
    pump()

    for g in range(GROUPS):
        for part in (0, D):
            cols = slice(part + g * LANES, part + (g + 1) * LANES)
            grad = dn_ref[:, cols]
            if part == 0:
                grad = grad * scales[g]
            inverse = inv_ref[:, cols]
            unit = qkv_ref[:, cols].astype(F32) * inverse
            act_ref[:, cols] = (inverse * (grad - unit * head_sum(unit * grad, heads))).astype(BF16)

    gs_ref[far] = nt(act_ref[far], wq_ref[...]).astype(BF16)
    halo_shifted = sems.copy(gs_ref.at[far], gs_in, after)
    pump()

    bias_part = gather_bias(acc_ref, onehot_ref, grid_ref)
    left = iota((1, LANES), 1) < 64
    for x in range(NX):
        block = tn(x_ref[...], act_ref[:, x * 384 : (x + 1) * 384])
        rolled = tn(mixed_ref[...], roll_ref[:, x * LANES : (x + 1) * LANES])
        middle = block[:, 128:256]
        firsts = (block[:, :128], block[:, 256:])
        seconds = (jnp.where(left, middle, rolled), jnp.where(left, rolled, middle))
        for c in range(CORES):
            one, two = firsts[c].astype(BF16), seconds[c].astype(BF16)
            for y in range(NY):
                rows = slice(y * 128, (y + 1) * 128)
                sum_c[c, x, y] = one[rows]
                sum_d[c, y, x] = two[rows]
    tasks += [
        stream(place, sems, "x", "y", 16, sum_c, part_a, bufs[2]),
        stream(place, sems, "y", "x", 16, sum_d, part_b, bufs[3]),
        bias_sum(place, sems, bias_part, padded_ref, bias_bufs),
    ]
    pump()

    gs_ref[own] = nt(act_ref[own], wq_ref[...]).astype(BF16)
    gs_ref[own] = (gh_ref[far].astype(F32) + gs_ref[own].astype(F32)).astype(BF16)
    halo_shifted.wait_recv()
    gn_own = (gh_ref[own].astype(F32) + gs_in[...].astype(F32)).astype(BF16)
    tokens_out[...] = tn(strip_ref[...], jnp.concatenate([gn_own, gs_ref[own]], axis=0)).astype(
        BF16
    )
    run_all(tasks)
    for copy in (halo_tokens, halo_normed, halo_hidden, halo_shifted):
        copy.wait_send()

    bias_out[...] = padded_ref[:, :OFFSETS]
    one, two = part_a[...], part_b[...]
    one_rolled, two_rolled = pltpu.roll(one, 64, 1), pltpu.roll(two, 64, 1)
    first_core = place.c == 0
    qkv_out[:, :128] = jnp.where(first_core, one, jnp.where(left, two_rolled, one_rolled))
    qkv_out[:, 128:] = jnp.where(first_core, two, one_rolled)[:, :64]
    proj_out[...] = jnp.where(first_core, two_rolled, two)[:, :64]


def block(tokens, region, valid, wq, wp, wm, scale, table, gain_attn, gain_merge, cot):
    vmem = pl.BlockSpec(memory_space=pltpu.VMEM)
    smem = pl.BlockSpec(memory_space=pltpu.SMEM)
    total = 4 + 4 * STREAM_COPIES + BIAS_COPIES

    def buf(*shape):
        return pltpu.VMEM(shape, BF16)

    def wide(*shape):
        return pltpu.VMEM(shape, F32)

    return pl.pallas_call(
        block_kernel,
        out_shape=[
            jax.ShapeDtypeStruct((64, 1024), BF16),
            jax.ShapeDtypeStruct((TOKENS, D), BF16),
            jax.ShapeDtypeStruct((16, 192), F32),
            jax.ShapeDtypeStruct((16, 64), F32),
            jax.ShapeDtypeStruct((64, 128), F32),
            jax.ShapeDtypeStruct((16, OFFSETS), F32),
        ],
        in_specs=[vmem] * 5 + [pl.BlockSpec(memory_space=pl.ANY), smem] + [vmem] * 8,
        out_specs=[vmem] * 6,
        scratch_shapes=[
            buf(2048, 1024),
            buf(TOKENS, D),
            buf(TOKENS, D),
            buf(TOKENS, 3 * D),
            wide(TOKENS, 2 * D),
            buf(TOKENS, D),
            buf(TOKENS, D),
            buf(TOKENS, D),
            buf(TOKENS, D),
            wide(4, PLACES, WIDE),
            wide(BIAS_ROWS, BIAS_LANES),
            wide(128, 128),
            wide(GROUPS, PLACES, WIDE),
            wide(4, GROUPS, PLACES, WIDE),
            buf(TOKENS, D),
            buf(TOKENS, D),
            wide(TOKENS, D),
            buf(HALF, D),
            buf(64, 2048),
            buf(TOKENS, D),
            buf(TOKENS, D),
            buf(TOKENS, D),
            buf(TOKENS, D),
            buf(TOKENS, D),
            wide(TOKENS, 2 * D),
            buf(TOKENS, 3 * D),
            buf(TOKENS, D),
            buf(HALF, D),
            wide(GROUPS, PLACES, WIDE),
            buf(CORES, NX, NY, NZ * 32, LANES),
            buf(CORES, NY, NX, NZ * 32, LANES),
            wide(16, LANES),
            wide(16, LANES),
            buf(CORES, NX, NY, NZ * 16, LANES),
            buf(CORES, NY, NX, NZ * 16, LANES),
        ]
        + stream_scratch(32)
        + stream_scratch(32)
        + stream_scratch(16)
        + stream_scratch(16)
        + bias_scratch()
        + [
            pltpu.SemaphoreType.DMA((total,)),
            pltpu.SemaphoreType.DMA((total,)),
            pltpu.SemaphoreType.DMA,
        ],
        compiler_params=pltpu.CompilerParams(
            collective_id=0, has_side_effects=True, vmem_limit_bytes=56 * 1024 * 1024
        ),
        name="block",
    )(tokens, region, valid, wq, wp, wm, scale, table, gain_attn, gain_merge, cot, *constants())


def shards(
    tokens,
    region,
    valid,
    qkv_weight,
    proj_weight,
    merge_weight,
    logit_scale,
    bias_table,
    gain_attn,
    gain_merge,
    cotangent,
):
    merged, grad_tokens, grad_qkv, grad_proj, grad_merge, grad_bias = block(
        tokens.reshape(TOKENS, D),
        region[0],
        valid[0],
        qkv_weight,
        proj_weight,
        merge_weight,
        logit_scale,
        bias_table,
        gain_attn[None],
        gain_merge[None],
        cotangent.reshape(64, 1024),
    )
    return (
        merged.reshape(cotangent.shape),
        grad_tokens.reshape(tokens.shape),
        grad_qkv,
        grad_proj,
        grad_merge,
        grad_bias,
    )


def solution(mesh):
    return jax.shard_map(
        shards,
        mesh=mesh,
        in_specs=(
            P("dp", "space", None, None),
            P("dp", None, None),
            P("dp", None, None),
            P(),
            P(),
            P(),
            P(),
            P(),
            P(),
            P(),
            P("dp", "space", None, None),
        ),
        out_specs=(
            P("dp", "space", None, None),
            P("dp", "space", None, None),
            P("space", "dp"),
            P("space", "dp"),
            P("space", "dp"),
            P(),
        ),
        check_vma=False,
    )
```

```python
import functools

import jax
import jax.numpy as jnp
from jax import lax
from jax.experimental import pallas as pl
from jax.experimental.pallas import tpu as pltpu
from jax.sharding import PartitionSpec as P

WIN = 8
HEAD_DIM = 32
SHIFT = 4
OFFSETS = 225
NX, NY, NZ, CORES = 4, 4, 8, 2
LANES = 128
MESH = pl.DeviceIdType.MESH


class Place:
    def __init__(self):
        strip, image = lax.axis_index("space"), lax.axis_index("dp")
        self.y, self.z = strip // NZ, lax.rem(strip, NZ)
        self.x, self.c = image // CORES, lax.rem(image, CORES)

    def at(self, x=None, y=None, z=None, c=None):
        x = self.x if x is None else x
        y = self.y if y is None else y
        z = self.z if z is None else z
        c = self.c if c is None else c
        return (y * NZ + z, x * CORES + c)

    def along(self, axis, step):
        count = {"x": NX, "y": NY, "z": NZ, "c": CORES}[axis]
        return self.at(**{axis: lax.rem(getattr(self, axis) + step, count)})

    def partners(self):
        return (
            [self.along("c", 1)]
            + [self.along("x", step) for step in range(1, NX)]
            + [self.along("y", step) for step in range(1, NY)]
            + [self.along("z", step) for step in range(1, NZ)]
        )


class Sems:
    def __init__(self, send, recv):
        self.send, self.recv, self.used = send, recv, 0

    def copy(self, source, target, device):
        index = self.used
        self.used += 1
        made = pltpu.make_async_remote_copy(
            src_ref=source,
            dst_ref=target,
            send_sem=self.send.at[index],
            recv_sem=self.recv.at[index],
            device_id=device,
            device_id_type=MESH,
        )
        made.start()
        return made


def add_blocks(count, put, parts):
    def body(index, carry):
        total = parts[0](index).astype(jnp.float32)
        for part in parts[1:]:
            total = total + part(index).astype(jnp.float32)
        put(index, total.astype(jnp.bfloat16))
        return carry

    if count == 1:
        body(0, 0)
    else:
        lax.fori_loop(0, count, body, 0)


def ring_sum(place, sems, axis, held, blocks, far_lo, far_hi, from_dn, from_up, put_out):
    me = getattr(place, axis)
    up, dn, far = lax.rem(me + 1, 4), lax.rem(me + 3, 4), lax.rem(me + 2, 4)
    to_up, to_dn = place.along(axis, 1), place.along(axis, 3)
    half = blocks // 2
    lo, hi = pl.ds(0, half), pl.ds(half, half)
    one = sems.copy(held.at[far, lo], far_lo, to_up)
    two = sems.copy(held.at[far, hi], far_hi, to_dn)
    three = sems.copy(held.at[up, hi], from_dn.at[hi], to_up)
    four = sems.copy(held.at[dn, lo], from_up.at[lo], to_dn)
    yield

    def put_up(i, v):
        held[up, i] = v

    def put_dn(i, v):
        held[dn, half + i] = v

    one.wait_recv()
    add_blocks(half, put_up, [lambda i: held[up, i], lambda i: far_lo[i]])
    five = sems.copy(held.at[up, lo], from_dn.at[lo], to_up)
    yield
    two.wait_recv()
    add_blocks(half, put_dn, [lambda i: held[dn, half + i], lambda i: far_hi[i]])
    six = sems.copy(held.at[dn, hi], from_up.at[hi], to_dn)
    yield
    three.wait_recv()
    four.wait_recv()
    five.wait_recv()
    six.wait_recv()
    add_blocks(
        blocks, put_out, [lambda i: held[me, i], lambda i: from_dn[i], lambda i: from_up[i]]
    )
    for copy in (one, two, three, four, five, six):
        copy.wait_send()


def shot_sum(place, sems, axis, count, held, parts, blocks, arrived, out):
    me = getattr(place, axis)
    sent = []
    for step in range(1, count):
        target = lax.rem(me + step, count)
        sent.append(
            sems.copy(held.at[target], arrived.at[step - 1], place.along(axis, step))
        )
    yield
    for copy in sent:
        copy.wait_recv()
    add_blocks(
        blocks,
        out,
        [lambda i: parts(held, me, i)]
        + [functools.partial(parts, arrived, step) for step in range(count - 1)],
    )
    for copy in sent:
        copy.wait_send()


def stream_scratch(rows, ring):
    full = NZ * rows
    shapes = [
        (4, 4, full, LANES),
        (4, 4, full, LANES),
        (4, NZ, rows, LANES),
        (3, NZ, rows, LANES),
        (NZ, rows, LANES),
        (NZ - 1, rows, LANES),
    ]
    if ring:
        shapes += [(2, full, LANES), (2, full, LANES), (4, full, LANES), (4, full, LANES)]
    else:
        shapes += [(3, 4, full, LANES)]
    return [pltpu.VMEM(shape, jnp.bfloat16) for shape in shapes]


def stream_copies(ring):
    return 1 + (6 if ring else 3) + 3 + (NZ - 1)


def stream(place, sems, first, second, rows, ring, source, out, bufs):
    other, core, one, late, two, last = bufs[:6]
    mine = place.c
    cross = sems.copy(source.at[1 - mine], other, place.along("c", 1))
    yield
    cross.wait_recv()

    def put_core(i, v):
        core[i // 4, lax.rem(i, 4)] = v

    def put_one(i, v):
        one[i] = v.reshape(NZ, rows, LANES)

    def put_two(i, v):
        two[...] = v

    add_blocks(
        16,
        put_core,
        [
            lambda i: source[mine, i // 4, lax.rem(i, 4)],
            lambda i: other[i // 4, lax.rem(i, 4)],
        ],
    )
    if ring:
        yield from ring_sum(place, sems, first, core, 4, *bufs[6:], put_one)
    else:
        yield from shot_sum(
            place, sems, first, 4, core, lambda ref, k, i: ref[k, i], 4, bufs[6], put_one
        )
    yield from shot_sum(
        place, sems, second, 4, one, lambda ref, k, i: ref[k], 1, late, put_two
    )
    sent = []
    for step in range(1, NZ):
        target = lax.rem(place.z + step, NZ)
        sent.append(sems.copy(two.at[target], last.at[step - 1], place.along("z", step)))
    yield
    total = two[place.z].astype(jnp.float32)
    for step in range(1, NZ):
        sent[step - 1].wait_recv()
        total = total + last[step - 1].astype(jnp.float32)
    out[...] = total
    for copy in sent:
        copy.wait_send()
    cross.wait_send()


BIAS_ROWS, BIAS_LANES = 16, 256
BIAS_COPIES = 1 + (NX - 1) + (NY - 1) + (NZ - 1)


def bias_scratch():
    return [
        pltpu.VMEM((count, BIAS_ROWS, BIAS_LANES), jnp.float32)
        for count in (CORES, NX, NY, NZ)
    ]


def bias_sum(place, sems, value, out, bufs):
    copies = []
    for axis, count, buf in zip("cxyz", (CORES, NX, NY, NZ), bufs):
        me = getattr(place, axis)
        buf[me] = value
        sent = [
            sems.copy(buf.at[me], buf.at[me], place.along(axis, step)) for step in range(1, count)
        ]
        yield
        for copy in sent:
            copy.wait_recv()
        value = buf[0]
        for index in range(1, count):
            value = value + buf[index]
        copies += sent
    out[...] = value
    for copy in copies:
        copy.wait_send()


def run_all(tasks):
    tasks = list(tasks)
    while tasks:
        for task in list(tasks):
            try:
                next(task)
            except StopIteration:
                tasks.remove(task)


def greet(partners):
    barrier = pltpu.get_barrier_semaphore()
    for device in partners:
        pl.semaphore_signal(barrier, inc=1, device_id=device, device_id_type=MESH)


def enter(partners):
    pl.semaphore_wait(pltpu.get_barrier_semaphore(), len(partners))


F32, BF16 = jnp.float32, jnp.bfloat16
TOKENS, D, GROUPS = 256, 512, 4
HALF = TOKENS // 2
PLACES = WIN * WIN
WIDE = 4 * PLACES


def nn(a, b):
    return lax.dot_general(a, b, (((1,), (0,)), ((), ())), preferred_element_type=F32)


def nt(a, b):
    return lax.dot_general(a, b, (((1,), (1,)), ((), ())), preferred_element_type=F32)


def tn(a, b):
    return lax.dot_general(a, b, (((0,), (0,)), ((), ())), preferred_element_type=F32)


def split2(t):
    high = t.astype(BF16)
    return high, (t - high.astype(F32)).astype(BF16)


def split3(t):
    high = t.astype(BF16)
    rest = t - high.astype(F32)
    middle = rest.astype(BF16)
    return high, middle, (rest - middle.astype(F32)).astype(BF16)


def iota(shape, axis):
    return lax.broadcasted_iota(jnp.int32, shape, axis)


def bits(t, low, count):
    return lax.bitwise_and(lax.shift_right_logical(t, low), (1 << count) - 1)


def one_hot(match):
    return jnp.where(match, 1.0, 0.0).astype(BF16)


def strip_order():
    i = iota((TOKENS, 1), 0)
    column = lax.bitwise_and(bits(i, 5, 2) * 8 + bits(i, 0, 3) + SHIFT, 31)
    natural = (bits(i, 7, 1) * 4 + bits(i, 3, 2)) * 32 + column
    return one_hot(iota((TOKENS, TOKENS), 1) == natural)


def quad_order():
    i = iota((HALF, 1), 0)
    column = lax.bitwise_and(2 * bits(i, 0, 4) + bits(i, 6, 1) + 32 - SHIFT, 31)
    row = 2 * bits(i, 4, 1) + bits(i, 5, 1)
    place = bits(column, 3, 2) * 32 + row * 8 + bits(column, 0, 3)
    return one_hot(iota((HALF, HALF), 1) == place)


def offset_order():
    j = iota((1, 1024), 1)
    offset = bits(j, 3, 4) * 15 + bits(j, 0, 3) - bits(j, 7, 3) + 7
    offset = jnp.where(bits(j, 3, 4) < 15, offset, -1)
    return one_hot(iota((256, 1024), 0) == offset)


def head_order():
    return one_hot(bits(iota((256, 128), 0), 5, 2) == bits(iota((256, 128), 1), 5, 2))


def head_sum(t, heads):
    return nn(jnp.concatenate(split2(t), axis=1), heads)


def stack_heads(t, lane_masks):
    return jnp.concatenate([t * mask for mask in lane_masks], axis=0)


def fold_heads(t, lane_masks):
    total = t[:PLACES] * lane_masks[0]
    for h in range(1, 4):
        total = total + t[h * PLACES : (h + 1) * PLACES] * lane_masks[h]
    return total


def norm_parts(t):
    centred = t - jnp.mean(t, -1, keepdims=True)
    scale = lax.rsqrt(jnp.mean(centred * centred, -1, keepdims=True) + 1e-05)
    return centred * scale, scale


def norm_back(grad, hat, scale):
    return scale * (
        grad - jnp.mean(grad, -1, keepdims=True) - hat * jnp.mean(grad * hat, -1, keepdims=True)
    )


def window_masks(place, region_ref, valid_ref, mask_ref):
    strip = place.y * NZ + place.z
    place_lane = iota((1, WIDE), 1) % PLACES
    row, col = place_lane // WIN, place_lane % WIN
    region = region_ref[...].astype(F32)
    valid = valid_ref[...].astype(F32)
    source_row = lax.rem(strip * WIN + SHIFT + row, 256)
    region_row = iota((64, WIDE), 0) == source_row // 4
    valid_row = iota((256, WIDE), 0) == source_row
    shifted_row = strip * WIN + row
    row_part = jnp.where(shifted_row < 256 - WIN, 0, jnp.where(shifted_row < 256 - SHIFT, 1, 2))
    diagonal = iota((PLACES, WIDE), 0) == place_lane
    pick = (iota((PLACES, WIDE), 0) == iota((PLACES, WIDE), 1)).astype(F32)
    for w in range(4):
        source_col = lax.rem(w * WIN + SHIFT + col, 32)
        shifted_col = w * WIN + col
        col_part = jnp.where(shifted_col < 32 - WIN, 0, jnp.where(shifted_col < 32 - SHIFT, 1, 2))
        region_pick = (iota((8, WIDE), 0) == source_col // 4).astype(F32)
        valid_pick = (iota((32, WIDE), 0) == source_col).astype(F32)
        swath = jnp.sum(jnp.where(region_row, tn(region, region_pick), 0.0), 0, keepdims=True)
        live = jnp.sum(jnp.where(valid_row, tn(valid, valid_pick), 0.0), 0, keepdims=True)
        label = swath * 9.0 + (row_part * 3 + col_part).astype(F32)
        label_key = jnp.sum(pick * label, 1, keepdims=True)
        live_key = jnp.sum(pick * live, 1, keepdims=True)
        same = (label_key == label).astype(F32)
        open_key = jnp.where(diagonal, 1.0, jnp.where(live_key == 1.0, 1.0, 0.0))
        mask_ref[w] = same * open_key


def spread_bias(table_ref, onehot_ref, padded_ref, grid_ref, bias_ref):
    padded_ref[...] = jnp.zeros_like(padded_ref)
    padded_ref[:, :OFFSETS] = table_ref[...]
    parts = nn(jnp.concatenate(split3(padded_ref[...]), axis=0), onehot_ref[...])
    spread = parts[:16] + parts[16:32] + parts[32:]
    for ct in range(8):
        grid_ref[pl.ds(ct, 16, stride=8), :] = spread[:, ct * 128 : (ct + 1) * 128]
    left = iota((8, 128), 1) < PLACES
    for pair in range(8):
        even = grid_ref[pair * 16 : pair * 16 + 8]
        odd = grid_ref[pair * 16 + 8 : pair * 16 + 16]
        lanes = pl.ds(pair % 2 * 128, 128)
        for rt in range(8):
            shift = (7 - rt) * 8
            bias_ref[pair // 2, rt * 8 : rt * 8 + 8, lanes] = jnp.where(
                left,
                pltpu.roll(even, (128 - shift) % 128, 1),
                pltpu.roll(odd, (128 + 64 - shift) % 128, 1),
            )


def gather_bias(acc_ref, onehot_ref, grid_ref):
    left = iota((8, 128), 1) < PLACES
    for pair in range(8):
        lanes = pl.ds(pair % 2 * 128, 128)
        even = jnp.zeros((8, 128), F32)
        odd = jnp.zeros((8, 128), F32)
        for rt in range(8):
            shift = (7 - rt) * 8
            piece = acc_ref[pair // 2, rt * 8 : rt * 8 + 8, lanes]
            even = even + pltpu.roll(jnp.where(left, piece, 0.0), shift, 1)
            odd = odd + pltpu.roll(jnp.where(left, 0.0, piece), (64 + shift) % 128, 1)
        grid_ref[pair * 16 : pair * 16 + 8] = even
        grid_ref[pair * 16 + 8 : pair * 16 + 16] = odd
    grid = jnp.concatenate([grid_ref[pl.ds(ct, 16, stride=8), :] for ct in range(8)], axis=1)
    parts = nt(jnp.concatenate(split3(grid), axis=0), onehot_ref[...])
    return parts[:16] + parts[16:32] + parts[32:]


def window_rows(w):
    return (
        pl.ds(pl.multiple_of(w * 32, 32), 32),
        pl.ds(pl.multiple_of(HALF + w * 32, 32), 32),
    )


def take(ref, w, start):
    first, second = window_rows(w)
    lanes = slice(start, start + LANES)
    return jnp.concatenate([ref[first, lanes], ref[second, lanes]], axis=0)


def put(ref, w, start, value):
    first, second = window_rows(w)
    lanes = slice(start, start + LANES)
    ref[first, lanes] = value[:32]
    ref[second, lanes] = value[32:]


STREAMS = ((32, True), (32, True), (16, False), (16, False))


def block_kernel(
    scale_ref,
    tok_hbm,
    wq_hbm,
    region_hbm,
    valid_hbm,
    table_hbm,
    wp_hbm,
    gain_attn_hbm,
    wm_hbm,
    gain_merge_hbm,
    cot_hbm,
    merged_out,
    tokens_out,
    qkv_out,
    proj_out,
    merge_out,
    bias_out,
    tok_ref,
    wq_ref,
    region_ref,
    valid_ref,
    table_ref,
    wp_ref,
    gain_attn_ref,
    wm_ref,
    gain_merge_ref,
    cot_ref,
    strip_ref,
    quad_ref,
    onehot_ref,
    tw_ref,
    x_ref,
    qkv_ref,
    inv_ref,
    qh_ref,
    ql_ref,
    kh_ref,
    kl_ref,
    mask_ref,
    padded_ref,
    grid_ref,
    bias_ref,
    probs_ref,
    mixed_ref,
    normed_ref,
    hat_ref,
    normed_in,
    quads_ref,
    gh_ref,
    gn_ref,
    go_ref,
    roll_ref,
    gm_ref,
    dn_ref,
    act_ref,
    gs_ref,
    gs_in,
    acc_ref,
    sum_a,
    sum_b,
    part_a,
    part_b,
    sum_c,
    sum_d,
    *scratch,
):
    bufs, at = [], 0
    for rows, ring in STREAMS:
        many = len(stream_scratch(rows, ring))
        bufs.append(scratch[at : at + many])
        at += many
    bias_bufs = scratch[at : at + 4]
    send, recv, local = scratch[at + 4 :]
    place = Place()
    sems = Sems(send, recv)
    strip = place.y * NZ + place.z
    image = place.x * CORES + place.c
    after = (lax.rem(strip + 1, NY * NZ), image)
    before = (lax.rem(strip + NY * NZ - 1, NY * NZ), image)
    own, far = slice(0, HALF), slice(HALF, TOKENS)

    partners = place.partners() + [after, before]
    greet(partners)
    loads = {}
    for index, (source, target) in enumerate(
        (
            (tok_hbm, tok_ref),
            (wq_hbm, wq_ref),
            (region_hbm, region_ref),
            (valid_hbm, valid_ref),
            (table_hbm, table_ref),
            (wp_hbm, wp_ref),
            (gain_attn_hbm, gain_attn_ref),
            (wm_hbm, wm_ref),
            (gain_merge_hbm, gain_merge_ref),
            (cot_hbm, cot_ref),
        )
    ):
        loads[id(target)] = pltpu.make_async_copy(source, target, local.at[index])
        loads[id(target)].start()

    def ready(*refs):
        for ref in refs:
            loads.pop(id(ref)).wait()

    strip_ref[...] = strip_order()
    ready(tok_ref)
    tw_ref[...] = nn(strip_ref[...], tok_ref[...]).astype(BF16)
    enter(partners)
    halo_tokens = sems.copy(tw_ref.at[own], x_ref.at[far], before)
    x_ref[own] = tw_ref[far]

    lane = iota((1, LANES), 1)
    masks = [(lane // HEAD_DIM == h).astype(F32) for h in range(4)]
    masks16 = [mask.astype(BF16) for mask in masks]
    scales = []
    for g in range(GROUPS):
        row = jnp.zeros((1, LANES), F32)
        for h in range(4):
            row = row + masks[h] * scale_ref[g * 4 + h]
        scales.append(row)
    ready(wq_ref)
    qkv_ref[own] = nn(x_ref[own], wq_ref[...]).astype(BF16)
    ready(region_ref, valid_ref)
    window_masks(place, region_ref, valid_ref, mask_ref)
    quad_ref[...] = quad_order()
    onehot_ref[...] = offset_order()
    ready(table_ref)
    spread_bias(table_ref, onehot_ref, padded_ref, grid_ref, bias_ref)
    halo_tokens.wait_recv()
    qkv_ref[far] = nn(x_ref[far], wq_ref[...]).astype(BF16)

    heads = head_order()
    for g in range(GROUPS):
        cols = slice(g * LANES, (g + 1) * LANES)
        for part, high, low in ((0, qh_ref, ql_ref), (D, kh_ref, kl_ref)):
            raw = qkv_ref[:, part + g * LANES : part + (g + 1) * LANES].astype(F32)
            inverse = lax.rsqrt(head_sum(raw * raw, heads) + 1e-06)
            inv_ref[:, part + g * LANES : part + (g + 1) * LANES] = inverse
            unit = raw * inverse
            if part == 0:
                unit = unit * scales[g]
            a, b = split2(unit)
            high[:, cols] = a
            low[:, cols] = b

    def forward(w, carry):
        allowed = mask_ref[w] > 0.5
        for g in range(GROUPS):
            start = g * LANES
            kh, kl = take(kh_ref, w, start), take(kl_ref, w, start)
            qh = stack_heads(take(qh_ref, w, start), masks16)
            ql = stack_heads(take(ql_ref, w, start), masks16)
            score = nt(
                jnp.concatenate([kh, kl, kh], axis=1), jnp.concatenate([qh, qh, ql], axis=1)
            )
            score = jnp.where(allowed, score + bias_ref[g], -1000000000.0)
            expo = jnp.exp(score - jnp.max(score, 0, keepdims=True))
            probs = expo * (1.0 / jnp.sum(expo, 0, keepdims=True))
            probs_ref[w, g] = probs
            out = tn(probs.astype(BF16), take(qkv_ref, w, 2 * D + start))
            put(mixed_ref, w, start, fold_heads(out, masks).astype(BF16))
        return carry

    lax.fori_loop(0, 4, forward, 0)

    ready(wp_ref, gain_attn_ref)
    gain_attn = gain_attn_ref[...]

    def project(rows):
        hat, scale = norm_parts(nn(mixed_ref[rows], wp_ref[...]))
        hat_ref[rows] = hat
        normed_ref[rows] = (hat * gain_attn).astype(BF16)
        return scale

    scale_far = project(far)
    halo_normed = sems.copy(normed_ref.at[far], normed_in, after)
    scale_own = project(own)

    def make_quads(which, added):
        rows = slice(which * HALF, (which + 1) * HALF)
        hidden = (tw_ref[rows].astype(F32) + added.astype(F32)).astype(BF16)
        sorted_rows = nn(quad_ref[...], hidden).astype(BF16)
        for k in range(4):
            quads_ref[which * 32 : which * 32 + 32, k * D : (k + 1) * D] = sorted_rows[
                k * 32 : (k + 1) * 32
            ]

    make_quads(1, normed_ref[own])
    ready(wm_ref, gain_merge_ref, cot_ref)
    halo_normed.wait_recv()
    make_quads(0, normed_in[...])

    gain_merge = gain_merge_ref[...]
    hat, scale = norm_parts(nn(quads_ref[...], wm_ref[...]))
    merged_out[...] = (hat * gain_merge).astype(BF16)
    grad_pre = norm_back(cot_ref[...].astype(F32) * gain_merge, hat, scale).astype(BF16)
    grad_quads = nt(grad_pre, wm_ref[...]).astype(BF16)
    for which in range(2):
        stacked = jnp.concatenate(
            [grad_quads[which * 32 : which * 32 + 32, k * D : (k + 1) * D] for k in range(4)],
            axis=0,
        )
        gh_ref[which * HALF : (which + 1) * HALF] = tn(quad_ref[...], stacked).astype(BF16)
        if which == 0:
            halo_hidden = sems.copy(gh_ref.at[own], gn_ref.at[far], before)
    gn_ref[own] = gh_ref[far]

    for x in range(NX):
        for y in range(NY):
            block = tn(
                quads_ref[:, y * D : (y + 1) * D], grad_pre[:, x * 256 : (x + 1) * 256]
            ).reshape(NZ, 2, 32, 256)
            for c in range(CORES):
                lanes = slice(c * LANES, (c + 1) * LANES)
                sum_a[c, x, y] = block[:, 0, :, lanes].reshape(NZ * 32, LANES).astype(BF16)
                sum_b[c, y, x] = block[:, 1, :, lanes].reshape(NZ * 32, LANES).astype(BF16)

    tasks = [
        stream(place, sems, "x", "y", 32, True, sum_a, merge_out.at[0:32], bufs[0]),
        stream(place, sems, "y", "x", 32, True, sum_b, merge_out.at[32:64], bufs[1]),
    ]

    def pump():
        for task in list(tasks):
            try:
                next(task)
            except StopIteration:
                tasks.remove(task)

    pump()

    def back_norm(rows, scale):
        grad = gn_ref[rows].astype(F32) * gain_attn
        out = norm_back(grad, hat_ref[rows], scale)
        go_ref[rows] = out.astype(BF16)
        for x in range(NX):
            lanes = slice(x * LANES, (x + 1) * LANES)
            roll_ref[rows, lanes] = pltpu.roll(out[:, lanes], 64, 1).astype(BF16)
        gm_ref[rows] = nt(go_ref[rows], wp_ref[...]).astype(BF16)

    back_norm(own, scale_own)
    pump()
    halo_hidden.wait_recv()
    back_norm(far, scale_far)

    acc_ref[...] = jnp.zeros_like(acc_ref)

    def backward(w, carry):
        for g in range(GROUPS):
            start = g * LANES
            grad = stack_heads(take(gm_ref, w, start), masks16)
            probs = probs_ref[w, g]
            grad_probs = nt(take(qkv_ref, w, 2 * D + start), grad)
            put(act_ref, w, 2 * D + start, nn(probs.astype(BF16), grad).astype(BF16))
            weighted = probs * grad_probs
            grad_score = weighted - probs * jnp.sum(weighted, 0, keepdims=True)
            acc_ref[g] += grad_score
            grad_score = grad_score.astype(BF16)
            query = stack_heads(take(qh_ref, w, start), masks16)
            put(dn_ref, w, D + start, nn(grad_score, query))
            put(dn_ref, w, start, fold_heads(tn(grad_score, take(kh_ref, w, start)), masks))
        return carry

    lax.fori_loop(0, 4, backward, 0)
    pump()
    for g in range(GROUPS):
        for part in (0, D):
            cols = slice(part + g * LANES, part + (g + 1) * LANES)
            grad = dn_ref[:, cols]
            if part == 0:
                grad = grad * scales[g]
            inverse = inv_ref[:, cols]
            unit = qkv_ref[:, cols].astype(F32) * inverse
            act_ref[:, cols] = (inverse * (grad - unit * head_sum(unit * grad, heads))).astype(BF16)

    gs_ref[far] = nt(act_ref[far], wq_ref[...]).astype(BF16)
    halo_shifted = sems.copy(gs_ref.at[far], gs_in, after)
    pump()

    bias_part = gather_bias(acc_ref, onehot_ref, grid_ref)
    left = iota((1, LANES), 1) < 64
    for x in range(NX):
        block = tn(x_ref[...], act_ref[:, x * 384 : (x + 1) * 384])
        rolled = tn(mixed_ref[...], roll_ref[:, x * LANES : (x + 1) * LANES])
        middle = block[:, 128:256]
        firsts = (block[:, :128], block[:, 256:])
        seconds = (jnp.where(left, middle, rolled), jnp.where(left, rolled, middle))
        for c in range(CORES):
            one, two = firsts[c].astype(BF16), seconds[c].astype(BF16)
            for y in range(NY):
                rows = slice(y * 128, (y + 1) * 128)
                sum_c[c, x, y] = one[rows]
                sum_d[c, y, x] = two[rows]
    tasks += [
        stream(place, sems, "x", "y", 16, False, sum_c, part_a, bufs[2]),
        stream(place, sems, "y", "x", 16, False, sum_d, part_b, bufs[3]),
        bias_sum(place, sems, bias_part, padded_ref, bias_bufs),
    ]
    pump()

    gs_ref[own] = nt(act_ref[own], wq_ref[...]).astype(BF16)
    gs_ref[own] = (gh_ref[far].astype(F32) + gs_ref[own].astype(F32)).astype(BF16)
    halo_shifted.wait_recv()
    gn_own = (gh_ref[own].astype(F32) + gs_in[...].astype(F32)).astype(BF16)
    tokens_out[...] = tn(strip_ref[...], jnp.concatenate([gn_own, gs_ref[own]], axis=0)).astype(
        BF16
    )
    run_all(tasks)
    for copy in (halo_tokens, halo_normed, halo_hidden, halo_shifted):
        copy.wait_send()

    bias_out[...] = padded_ref[:, :OFFSETS]
    one, two = part_a[...], part_b[...]
    one_rolled, two_rolled = pltpu.roll(one, 64, 1), pltpu.roll(two, 64, 1)
    first_core = place.c == 0
    qkv_out[:, :128] = jnp.where(first_core, one, jnp.where(left, two_rolled, one_rolled))
    qkv_out[:, 128:] = jnp.where(first_core, two, one_rolled)[:, :64]
    proj_out[...] = jnp.where(first_core, two_rolled, two)[:, :64]


def block(tokens, region, valid, wq, wp, wm, scale, table, gain_attn, gain_merge, cot):
    vmem = pl.BlockSpec(memory_space=pltpu.VMEM)
    smem = pl.BlockSpec(memory_space=pltpu.SMEM)
    far = pl.BlockSpec(memory_space=pl.ANY)
    total = 4 + sum(stream_copies(ring) for _, ring in STREAMS) + BIAS_COPIES
    inputs = [tokens, wq, region, valid, table, wp, gain_attn, wm, gain_merge, cot]

    def buf(*shape):
        return pltpu.VMEM(shape, BF16)

    def wide(*shape):
        return pltpu.VMEM(shape, F32)

    return pl.pallas_call(
        block_kernel,
        out_shape=[
            jax.ShapeDtypeStruct((64, 1024), BF16),
            jax.ShapeDtypeStruct((TOKENS, D), BF16),
            jax.ShapeDtypeStruct((16, 192), F32),
            jax.ShapeDtypeStruct((16, 64), F32),
            jax.ShapeDtypeStruct((64, 128), F32),
            jax.ShapeDtypeStruct((16, OFFSETS), F32),
        ],
        in_specs=[smem] + [far] * len(inputs),
        out_specs=[vmem] * 6,
        scratch_shapes=[pltpu.VMEM(value.shape, value.dtype) for value in inputs]
        + [
            buf(TOKENS, TOKENS),
            buf(HALF, HALF),
            buf(256, 1024),
            buf(TOKENS, D),
            buf(TOKENS, D),
            buf(TOKENS, 3 * D),
            wide(TOKENS, 2 * D),
            buf(TOKENS, D),
            buf(TOKENS, D),
            buf(TOKENS, D),
            buf(TOKENS, D),
            wide(4, PLACES, WIDE),
            wide(BIAS_ROWS, BIAS_LANES),
            wide(128, 128),
            wide(GROUPS, PLACES, WIDE),
            wide(4, GROUPS, PLACES, WIDE),
            buf(TOKENS, D),
            buf(TOKENS, D),
            wide(TOKENS, D),
            buf(HALF, D),
            buf(64, 2048),
            buf(TOKENS, D),
            buf(TOKENS, D),
            buf(TOKENS, D),
            buf(TOKENS, D),
            buf(TOKENS, D),
            wide(TOKENS, 2 * D),
            buf(TOKENS, 3 * D),
            buf(TOKENS, D),
            buf(HALF, D),
            wide(GROUPS, PLACES, WIDE),
            buf(CORES, NX, NY, NZ * 32, LANES),
            buf(CORES, NY, NX, NZ * 32, LANES),
            wide(16, LANES),
            wide(16, LANES),
            buf(CORES, NX, NY, NZ * 16, LANES),
            buf(CORES, NY, NX, NZ * 16, LANES),
        ]
        + sum([stream_scratch(*kind) for kind in STREAMS], [])
        + bias_scratch()
        + [
            pltpu.SemaphoreType.DMA((total,)),
            pltpu.SemaphoreType.DMA((total,)),
            pltpu.SemaphoreType.DMA((len(inputs),)),
        ],
        compiler_params=pltpu.CompilerParams(
            collective_id=0, has_side_effects=True, vmem_limit_bytes=56 * 1024 * 1024
        ),
        name="block",
    )(scale, *inputs)


def hand_out_kernel(*refs):
    count = len(refs) // 2
    copies = [
        pltpu.make_async_copy(refs[i], refs[count + i], refs[-1].at[i]) for i in range(count)
    ]
    for copy in copies:
        copy.start()
    for copy in copies:
        copy.wait()


def hand_out(values):
    near, far = pl.BlockSpec(memory_space=pltpu.VMEM), pl.BlockSpec(memory_space=pl.ANY)
    return pl.pallas_call(
        hand_out_kernel,
        out_shape=[jax.ShapeDtypeStruct(value.shape, value.dtype) for value in values],
        in_specs=[near] * len(values),
        out_specs=[far] * len(values),
        scratch_shapes=[pltpu.SemaphoreType.DMA((len(values),))],
        name="hand_out",
    )(*values)


def shards(
    tokens,
    region,
    valid,
    qkv_weight,
    proj_weight,
    merge_weight,
    logit_scale,
    bias_table,
    gain_attn,
    gain_merge,
    cotangent,
):
    merged, grad_tokens, grad_qkv, grad_proj, grad_merge, grad_bias = hand_out(
        block(
        tokens.reshape(TOKENS, D),
        region[0].T,
        valid[0].T,
        qkv_weight,
        proj_weight,
        merge_weight,
        logit_scale,
        bias_table,
        gain_attn[None],
        gain_merge[None],
        cotangent.reshape(64, 1024),
    ))
    return (
        merged.reshape(cotangent.shape),
        grad_tokens.reshape(tokens.shape),
        grad_qkv,
        grad_proj,
        grad_merge,
        grad_bias,
    )


def solution(mesh):
    return jax.shard_map(
        shards,
        mesh=mesh,
        in_specs=(
            P("dp", "space", None, None),
            P("dp", None, None),
            P("dp", None, None),
            P(),
            P(),
            P(),
            P(),
            P(),
            P(),
            P(),
            P("dp", "space", None, None),
        ),
        out_specs=(
            P("dp", "space", None, None),
            P("dp", "space", None, None),
            P("space", "dp"),
            P("space", "dp"),
            P("space", "dp"),
            P(),
        ),
        check_vma=False,
    )
```

```python
import functools

import jax
import jax.numpy as jnp
from jax import lax
from jax.experimental import pallas as pl
from jax.experimental.pallas import tpu as pltpu
from jax.sharding import PartitionSpec as P

WIN = 8
HEAD_DIM = 32
SHIFT = 4
OFFSETS = 225
NX, NY, NZ, CORES = 4, 4, 8, 2
LANES = 128
MESH = pl.DeviceIdType.MESH


class Place:
    def __init__(self):
        strip, image = lax.axis_index("space"), lax.axis_index("dp")
        self.y, self.z = strip // NZ, lax.rem(strip, NZ)
        self.x, self.c = image // CORES, lax.rem(image, CORES)

    def at(self, x=None, y=None, z=None, c=None):
        x = self.x if x is None else x
        y = self.y if y is None else y
        z = self.z if z is None else z
        c = self.c if c is None else c
        return (y * NZ + z, x * CORES + c)

    def along(self, axis, step):
        count = {"x": NX, "y": NY, "z": NZ, "c": CORES}[axis]
        return self.at(**{axis: lax.rem(getattr(self, axis) + step, count)})

    def partners(self):
        return (
            [self.along("c", 1)]
            + [self.along("x", step) for step in range(1, NX)]
            + [self.along("y", step) for step in range(1, NY)]
            + [self.along("z", step) for step in range(1, NZ)]
        )


class Sems:
    def __init__(self, send, recv):
        self.send, self.recv, self.used = send, recv, 0

    def copy(self, source, target, device):
        index = self.used
        self.used += 1
        made = pltpu.make_async_remote_copy(
            src_ref=source,
            dst_ref=target,
            send_sem=self.send.at[index],
            recv_sem=self.recv.at[index],
            device_id=device,
            device_id_type=MESH,
        )
        made.start()
        return made


def add_blocks(count, put, parts):
    def body(index, carry):
        total = parts[0](index).astype(jnp.float32)
        for part in parts[1:]:
            total = total + part(index).astype(jnp.float32)
        put(index, total.astype(jnp.bfloat16))
        return carry

    if count == 1:
        body(0, 0)
    else:
        lax.fori_loop(0, count, body, 0)


def ring_sum(place, sems, axis, held, prepare, blocks, far_lo, far_hi, from_dn, from_up, put_out):
    me = getattr(place, axis)
    up, dn, far = lax.rem(me + 1, 4), lax.rem(me + 3, 4), lax.rem(me + 2, 4)
    to_up, to_dn = place.along(axis, 1), place.along(axis, 3)
    half = blocks // 2
    lo, hi = pl.ds(0, half), pl.ds(half, half)
    prepare(far)
    one = sems.copy(held.at[far, lo], far_lo, to_up)
    two = sems.copy(held.at[far, hi], far_hi, to_dn)
    prepare(up)
    three = sems.copy(held.at[up, hi], from_dn.at[hi], to_up)
    prepare(dn)
    four = sems.copy(held.at[dn, lo], from_up.at[lo], to_dn)
    prepare(me)
    yield

    def put_up(i, v):
        held[up, i] = v

    def put_dn(i, v):
        held[dn, half + i] = v

    one.wait_recv()
    add_blocks(half, put_up, [lambda i: held[up, i], lambda i: far_lo[i]])
    five = sems.copy(held.at[up, lo], from_dn.at[lo], to_up)
    two.wait_recv()
    add_blocks(half, put_dn, [lambda i: held[dn, half + i], lambda i: far_hi[i]])
    six = sems.copy(held.at[dn, hi], from_up.at[hi], to_dn)
    yield
    three.wait_recv()
    four.wait_recv()
    five.wait_recv()
    six.wait_recv()
    add_blocks(
        blocks, put_out, [lambda i: held[me, i], lambda i: from_dn[i], lambda i: from_up[i]]
    )
    for copy in (one, two, three, four, five, six):
        copy.wait_send()


def shot_sum(place, sems, axis, count, held, prepare, parts, blocks, arrived, out):
    me = getattr(place, axis)
    sent = []
    for step in range(1, count):
        target = lax.rem(me + step, count)
        prepare(target)
        sent.append(
            sems.copy(held.at[target], arrived.at[step - 1], place.along(axis, step))
        )
    prepare(me)
    yield
    for copy in sent:
        copy.wait_recv()
    add_blocks(
        blocks,
        out,
        [lambda i: parts(held, me, i)]
        + [functools.partial(parts, arrived, step) for step in range(count - 1)],
    )
    for copy in sent:
        copy.wait_send()


def stream_scratch(rows, ring):
    full = NZ * rows
    shapes = [
        (4, 4, full, LANES),
        (4, 4, full, LANES),
        (4, NZ, rows, LANES),
        (3, NZ, rows, LANES),
        (NZ, rows, LANES),
        (NZ - 1, rows, LANES),
    ]
    if ring:
        shapes += [(2, full, LANES), (2, full, LANES), (4, full, LANES), (4, full, LANES)]
    else:
        shapes += [(3, 4, full, LANES)]
    return [pltpu.VMEM(shape, jnp.bfloat16) for shape in shapes]


def stream_copies(ring):
    return NX + (6 if ring else 3) + 3 + (NZ - 1)


class CorePart:
    def __init__(self, place, sems, x_first, source, other):
        self.place, self.sems, self.x_first = place, sems, x_first
        self.source, self.other, self.sent = source, other, []

    def send(self, x):
        across, theirs = self.place.along("c", 1), 1 - self.place.c
        if self.x_first:
            pair = self.source.at[theirs, x], self.other.at[x]
        else:
            pair = self.source.at[theirs, :, x], self.other.at[:, x]
        self.sent.append(self.sems.copy(*pair, across))


def stream(place, sems, first, second, rows, ring, cores, out, bufs):
    core, one, late, two, last = bufs[1:6]
    source, other, mine = cores.source, cores.other, place.c
    for copy in cores.sent:
        copy.wait_recv()

    def add_core(k):
        def put_core(i, v):
            core[k, i] = v

        add_blocks(4, put_core, [lambda i: source[mine, k, i], lambda i: other[k, i]])

    def put_one(i, v):
        one[i] = v.reshape(NZ, rows, LANES)

    def put_two(i, v):
        two[...] = v

    def nothing(k):
        pass

    if ring:
        yield from ring_sum(place, sems, first, core, add_core, 4, *bufs[6:], put_one)
    else:
        yield from shot_sum(
            place, sems, first, 4, core, add_core, lambda ref, k, i: ref[k, i], 4, bufs[6], put_one
        )
    yield from shot_sum(
        place, sems, second, 4, one, nothing, lambda ref, k, i: ref[k], 1, late, put_two
    )
    sent = []
    for step in range(1, NZ):
        target = lax.rem(place.z + step, NZ)
        sent.append(sems.copy(two.at[target], last.at[step - 1], place.along("z", step)))
    yield
    total = two[place.z].astype(jnp.float32)
    for step in range(1, NZ):
        sent[step - 1].wait_recv()
        total = total + last[step - 1].astype(jnp.float32)
    out[...] = total
    for copy in sent + cores.sent:
        copy.wait_send()


BIAS_ROWS, BIAS_LANES = 16, 256
BIAS_COPIES = 1 + (NX - 1) + (NY - 1) + (NZ - 1)


def bias_scratch():
    return [
        pltpu.VMEM((count, BIAS_ROWS, BIAS_LANES), jnp.float32)
        for count in (CORES, NX, NY, NZ)
    ]


def bias_sum(place, sems, value, out, bufs):
    copies = []
    for axis, count, buf in zip("cxyz", (CORES, NX, NY, NZ), bufs):
        me = getattr(place, axis)
        buf[me] = value
        sent = [
            sems.copy(buf.at[me], buf.at[me], place.along(axis, step)) for step in range(1, count)
        ]
        yield
        for copy in sent:
            copy.wait_recv()
        value = buf[0]
        for index in range(1, count):
            value = value + buf[index]
        copies += sent
    out[...] = value
    for copy in copies:
        copy.wait_send()


def advance(tasks):
    for task in list(tasks):
        try:
            next(task)
        except StopIteration:
            tasks.remove(task)


def greet(partners):
    barrier = pltpu.get_barrier_semaphore()
    for device in partners:
        pl.semaphore_signal(barrier, inc=1, device_id=device, device_id_type=MESH)


def enter(partners):
    pl.semaphore_wait(pltpu.get_barrier_semaphore(), len(partners))


F32, BF16 = jnp.float32, jnp.bfloat16
TOKENS, D, GROUPS = 256, 512, 4
HALF = TOKENS // 2
PLACES = WIN * WIN
WIDE = 4 * PLACES


def nn(a, b):
    return lax.dot_general(a, b, (((1,), (0,)), ((), ())), preferred_element_type=F32)


def nt(a, b):
    return lax.dot_general(a, b, (((1,), (1,)), ((), ())), preferred_element_type=F32)


def tn(a, b):
    return lax.dot_general(a, b, (((0,), (0,)), ((), ())), preferred_element_type=F32)


def split2(t):
    high = t.astype(BF16)
    return high, (t - high.astype(F32)).astype(BF16)


def split3(t):
    high = t.astype(BF16)
    rest = t - high.astype(F32)
    middle = rest.astype(BF16)
    return high, middle, (rest - middle.astype(F32)).astype(BF16)


def iota(shape, axis):
    return lax.broadcasted_iota(jnp.int32, shape, axis)


def bits(t, low, count):
    return lax.bitwise_and(lax.shift_right_logical(t, low), (1 << count) - 1)


def one_hot(match):
    return jnp.where(match, 1.0, 0.0).astype(BF16)


def strip_order():
    i = iota((TOKENS, 1), 0)
    column = lax.bitwise_and(bits(i, 5, 2) * 8 + bits(i, 0, 3) + SHIFT, 31)
    natural = (bits(i, 7, 1) * 4 + bits(i, 3, 2)) * 32 + column
    return one_hot(iota((TOKENS, TOKENS), 1) == natural)


def quad_order():
    i = iota((HALF, 1), 0)
    column = lax.bitwise_and(2 * bits(i, 0, 4) + bits(i, 6, 1) + 32 - SHIFT, 31)
    row = 2 * bits(i, 4, 1) + bits(i, 5, 1)
    place = bits(column, 3, 2) * 32 + row * 8 + bits(column, 0, 3)
    return one_hot(iota((HALF, HALF), 1) == place)


def offset_order():
    j = iota((1, 1024), 1)
    offset = bits(j, 3, 4) * 15 + bits(j, 0, 3) - bits(j, 7, 3) + 7
    offset = jnp.where(bits(j, 3, 4) < 15, offset, -1)
    return one_hot(iota((256, 1024), 0) == offset)


def head_order():
    return one_hot(bits(iota((256, 128), 0), 5, 2) == bits(iota((256, 128), 1), 5, 2))


def head_sum(t, heads):
    return nn(jnp.concatenate(split2(t), axis=1), heads)


def stack_heads(t, lane_masks):
    return jnp.concatenate([t * mask for mask in lane_masks], axis=0)


def fold_heads(t, lane_masks):
    total = t[:PLACES] * lane_masks[0]
    for h in range(1, 4):
        total = total + t[h * PLACES : (h + 1) * PLACES] * lane_masks[h]
    return total


def norm_parts(t):
    centred = t - jnp.mean(t, -1, keepdims=True)
    scale = lax.rsqrt(jnp.mean(centred * centred, -1, keepdims=True) + 1e-05)
    return centred * scale, scale


def norm_back(grad, hat, scale):
    return scale * (
        grad - jnp.mean(grad, -1, keepdims=True) - hat * jnp.mean(grad * hat, -1, keepdims=True)
    )


def window_masks(place, region_ref, valid_ref, mask_ref):
    strip = place.y * NZ + place.z
    place_lane = iota((1, WIDE), 1) % PLACES
    row, col = place_lane // WIN, place_lane % WIN
    region = region_ref[...].astype(F32)
    valid = valid_ref[...].astype(F32)
    source_row = lax.rem(strip * WIN + SHIFT + row, 256)
    region_row = iota((64, WIDE), 0) == source_row // 4
    valid_row = iota((256, WIDE), 0) == source_row
    shifted_row = strip * WIN + row
    row_part = jnp.where(shifted_row < 256 - WIN, 0, jnp.where(shifted_row < 256 - SHIFT, 1, 2))
    diagonal = iota((PLACES, WIDE), 0) == place_lane
    pick = (iota((PLACES, WIDE), 0) == iota((PLACES, WIDE), 1)).astype(F32)
    for w in range(4):
        source_col = lax.rem(w * WIN + SHIFT + col, 32)
        shifted_col = w * WIN + col
        col_part = jnp.where(shifted_col < 32 - WIN, 0, jnp.where(shifted_col < 32 - SHIFT, 1, 2))
        region_pick = (iota((8, WIDE), 0) == source_col // 4).astype(F32)
        valid_pick = (iota((32, WIDE), 0) == source_col).astype(F32)
        swath = jnp.sum(jnp.where(region_row, tn(region, region_pick), 0.0), 0, keepdims=True)
        live = jnp.sum(jnp.where(valid_row, tn(valid, valid_pick), 0.0), 0, keepdims=True)
        label = swath * 9.0 + (row_part * 3 + col_part).astype(F32)
        label_key = jnp.sum(pick * label, 1, keepdims=True)
        live_key = jnp.sum(pick * live, 1, keepdims=True)
        same = (label_key == label).astype(F32)
        open_key = jnp.where(diagonal, 1.0, jnp.where(live_key == 1.0, 1.0, 0.0))
        mask_ref[w] = same * open_key


def spread_bias(table_ref, onehot_ref, padded_ref, grid_ref, bias_ref):
    padded_ref[...] = jnp.zeros_like(padded_ref)
    padded_ref[:, :OFFSETS] = table_ref[...]
    parts = nn(jnp.concatenate(split3(padded_ref[...]), axis=0), onehot_ref[...])
    spread = parts[:16] + parts[16:32] + parts[32:]
    for ct in range(8):
        grid_ref[pl.ds(ct, 16, stride=8), :] = spread[:, ct * 128 : (ct + 1) * 128]
    left = iota((8, 128), 1) < PLACES
    for pair in range(8):
        even = grid_ref[pair * 16 : pair * 16 + 8]
        odd = grid_ref[pair * 16 + 8 : pair * 16 + 16]
        lanes = pl.ds(pair % 2 * 128, 128)
        for rt in range(8):
            shift = (7 - rt) * 8
            bias_ref[pair // 2, rt * 8 : rt * 8 + 8, lanes] = jnp.where(
                left,
                pltpu.roll(even, (128 - shift) % 128, 1),
                pltpu.roll(odd, (128 + 64 - shift) % 128, 1),
            )


def gather_bias(acc_ref, onehot_ref, grid_ref):
    left = iota((8, 128), 1) < PLACES
    for pair in range(8):
        lanes = pl.ds(pair % 2 * 128, 128)
        even = jnp.zeros((8, 128), F32)
        odd = jnp.zeros((8, 128), F32)
        for rt in range(8):
            shift = (7 - rt) * 8
            piece = acc_ref[pair // 2, rt * 8 : rt * 8 + 8, lanes]
            even = even + pltpu.roll(jnp.where(left, piece, 0.0), shift, 1)
            odd = odd + pltpu.roll(jnp.where(left, 0.0, piece), (64 + shift) % 128, 1)
        grid_ref[pair * 16 : pair * 16 + 8] = even
        grid_ref[pair * 16 + 8 : pair * 16 + 16] = odd
    grid = jnp.concatenate([grid_ref[pl.ds(ct, 16, stride=8), :] for ct in range(8)], axis=1)
    parts = nt(jnp.concatenate(split3(grid), axis=0), onehot_ref[...])
    return parts[:16] + parts[16:32] + parts[32:]


def window_rows(w):
    return (
        pl.ds(pl.multiple_of(w * 32, 32), 32),
        pl.ds(pl.multiple_of(HALF + w * 32, 32), 32),
    )


def take(ref, w, start):
    first, second = window_rows(w)
    lanes = slice(start, start + LANES)
    return jnp.concatenate([ref[first, lanes], ref[second, lanes]], axis=0)


def put(ref, w, start, value):
    first, second = window_rows(w)
    lanes = slice(start, start + LANES)
    ref[first, lanes] = value[:32]
    ref[second, lanes] = value[32:]


STREAMS = ((32, True), (32, True), (16, False), (16, False))


def block_kernel(
    scale_ref,
    tok_hbm,
    wq_hbm,
    region_hbm,
    valid_hbm,
    table_hbm,
    wp_hbm,
    gain_attn_hbm,
    wm_hbm,
    gain_merge_hbm,
    cot_hbm,
    merged_out,
    tokens_out,
    qkv_out,
    proj_out,
    merge_out,
    bias_out,
    tok_ref,
    wq_ref,
    region_ref,
    valid_ref,
    table_ref,
    wp_ref,
    gain_attn_ref,
    wm_ref,
    gain_merge_ref,
    cot_ref,
    strip_ref,
    quad_ref,
    onehot_ref,
    tw_ref,
    x_ref,
    qkv_ref,
    inv_ref,
    qh_ref,
    ql_ref,
    kh_ref,
    kl_ref,
    mask_ref,
    padded_ref,
    grid_ref,
    bias_ref,
    probs_ref,
    mixed_ref,
    normed_ref,
    hat_ref,
    normed_in,
    quads_ref,
    xt_ref,
    mixedt_ref,
    quadst_ref,
    gh_ref,
    gn_ref,
    go_ref,
    roll_ref,
    gm_ref,
    dn_ref,
    act_ref,
    gs_ref,
    gs_in,
    acc_ref,
    sum_a,
    sum_b,
    part_a,
    part_b,
    sum_c,
    sum_d,
    *scratch,
):
    bufs, at = [], 0
    for rows, ring in STREAMS:
        many = len(stream_scratch(rows, ring))
        bufs.append(scratch[at : at + many])
        at += many
    bias_bufs = scratch[at : at + 4]
    send, recv, local = scratch[at + 4 :]
    place = Place()
    sems = Sems(send, recv)
    strip = place.y * NZ + place.z
    image = place.x * CORES + place.c
    after = (lax.rem(strip + 1, NY * NZ), image)
    before = (lax.rem(strip + NY * NZ - 1, NY * NZ), image)
    own, far = slice(0, HALF), slice(HALF, TOKENS)

    partners = place.partners() + [after, before]
    greet(partners)
    loads = {}
    for index, (source, target) in enumerate(
        (
            (tok_hbm, tok_ref),
            (wq_hbm, wq_ref),
            (region_hbm, region_ref),
            (valid_hbm, valid_ref),
            (table_hbm, table_ref),
            (wp_hbm, wp_ref),
            (gain_attn_hbm, gain_attn_ref),
            (wm_hbm, wm_ref),
            (gain_merge_hbm, gain_merge_ref),
            (cot_hbm, cot_ref),
        )
    ):
        loads[id(target)] = pltpu.make_async_copy(source, target, local.at[index])
        loads[id(target)].start()

    def ready(*refs):
        for ref in refs:
            loads.pop(id(ref)).wait()

    strip_ref[...] = strip_order()
    ready(tok_ref)
    tw_ref[...] = nn(strip_ref[...], tok_ref[...]).astype(BF16)
    enter(partners)
    halo_tokens = sems.copy(tw_ref.at[own], x_ref.at[far], before)
    x_ref[own] = tw_ref[far]

    lane = iota((1, LANES), 1)
    masks = [(lane // HEAD_DIM == h).astype(F32) for h in range(4)]
    masks16 = [mask.astype(BF16) for mask in masks]
    scales = []
    for g in range(GROUPS):
        row = jnp.zeros((1, LANES), F32)
        for h in range(4):
            row = row + masks[h] * scale_ref[g * 4 + h]
        scales.append(row)
    ready(wq_ref)
    qkv_ref[own] = nn(x_ref[own], wq_ref[...]).astype(BF16)
    ready(region_ref, valid_ref)
    window_masks(place, region_ref, valid_ref, mask_ref)
    quad_ref[...] = quad_order()
    onehot_ref[...] = offset_order()
    ready(table_ref)
    spread_bias(table_ref, onehot_ref, padded_ref, grid_ref, bias_ref)
    halo_tokens.wait_recv()
    qkv_ref[far] = nn(x_ref[far], wq_ref[...]).astype(BF16)

    heads = head_order()
    for g in range(GROUPS):
        cols = slice(g * LANES, (g + 1) * LANES)
        for part, high, low in ((0, qh_ref, ql_ref), (D, kh_ref, kl_ref)):
            raw = qkv_ref[:, part + g * LANES : part + (g + 1) * LANES].astype(F32)
            inverse = lax.rsqrt(head_sum(raw * raw, heads) + 1e-06)
            inv_ref[:, part + g * LANES : part + (g + 1) * LANES] = inverse
            unit = raw * inverse
            if part == 0:
                unit = unit * scales[g]
            a, b = split2(unit)
            high[:, cols] = a
            low[:, cols] = b

    def forward(w, carry):
        allowed = mask_ref[w] > 0.5
        scores = []
        for g in range(GROUPS):
            start = g * LANES
            kh, kl = take(kh_ref, w, start), take(kl_ref, w, start)
            qh = stack_heads(take(qh_ref, w, start), masks16)
            ql = stack_heads(take(ql_ref, w, start), masks16)
            scores.append(
                nt(jnp.concatenate([kh, kl, kh], axis=1), jnp.concatenate([qh, qh, ql], axis=1))
            )
        rounded = []
        for g in range(GROUPS):
            score = jnp.where(allowed, scores[g] + bias_ref[g], -1000000000.0)
            expo = jnp.exp(score - jnp.max(score, 0, keepdims=True))
            probs = expo * (1.0 / jnp.sum(expo, 0, keepdims=True))
            probs_ref[w, g] = probs
            rounded.append(probs.astype(BF16))
        outs = [tn(rounded[g], take(qkv_ref, w, 2 * D + g * LANES)) for g in range(GROUPS)]
        for g in range(GROUPS):
            put(mixed_ref, w, g * LANES, fold_heads(outs[g], masks).astype(BF16))
        return carry

    lax.fori_loop(0, 4, forward, 0, unroll=2)

    ready(wp_ref, gain_attn_ref)
    gain_attn = gain_attn_ref[...]

    def project(rows):
        hat, scale = norm_parts(nn(mixed_ref[rows], wp_ref[...]))
        hat_ref[rows] = hat
        normed_ref[rows] = (hat * gain_attn).astype(BF16)
        return scale

    scale_far = project(far)
    halo_normed = sems.copy(normed_ref.at[far], normed_in, after)
    scale_own = project(own)

    def make_quads(which, added):
        rows = slice(which * HALF, (which + 1) * HALF)
        hidden = (tw_ref[rows].astype(F32) + added.astype(F32)).astype(BF16)
        sorted_rows = nn(quad_ref[...], hidden).astype(BF16)
        for k in range(4):
            quads_ref[which * 32 : which * 32 + 32, k * D : (k + 1) * D] = sorted_rows[
                k * 32 : (k + 1) * 32
            ]

    make_quads(1, normed_ref[own])
    xt_ref[...] = x_ref[...].T
    mixedt_ref[...] = mixed_ref[...].T
    ready(wm_ref, gain_merge_ref, cot_ref)
    halo_normed.wait_recv()
    make_quads(0, normed_in[...])
    quadst_ref[...] = quads_ref[...].T

    gain_merge = gain_merge_ref[...]
    hat, scale = norm_parts(nn(quads_ref[...], wm_ref[...]))
    merged_out[...] = (hat * gain_merge).astype(BF16)
    grad_pre = norm_back(cot_ref[...].astype(F32) * gain_merge, hat, scale).astype(BF16)
    parts_a = CorePart(place, sems, True, sum_a, bufs[0][0])
    parts_b = CorePart(place, sems, False, sum_b, bufs[1][0])
    parts_c = CorePart(place, sems, True, sum_c, bufs[2][0])
    parts_d = CorePart(place, sems, False, sum_d, bufs[3][0])
    for x in range(NX):
        for y in range(NY):
            block = nn(
                quadst_ref[y * D : (y + 1) * D], grad_pre[:, x * 256 : (x + 1) * 256]
            ).reshape(NZ, 2, 32, 256)
            for c in range(CORES):
                lanes = slice(c * LANES, (c + 1) * LANES)
                sum_a[c, x, y] = block[:, 0, :, lanes].reshape(NZ * 32, LANES).astype(BF16)
                sum_b[c, y, x] = block[:, 1, :, lanes].reshape(NZ * 32, LANES).astype(BF16)
        parts_a.send(x)
        parts_b.send(x)

    grad_quads = nt(grad_pre, wm_ref[...]).astype(BF16)
    for which in range(2):
        stacked = jnp.concatenate(
            [grad_quads[which * 32 : which * 32 + 32, k * D : (k + 1) * D] for k in range(4)],
            axis=0,
        )
        gh_ref[which * HALF : (which + 1) * HALF] = tn(quad_ref[...], stacked).astype(BF16)
        if which == 0:
            halo_hidden = sems.copy(gh_ref.at[own], gn_ref.at[far], before)
    gn_ref[own] = gh_ref[far]

    merging = [
        stream(place, sems, "x", "y", 32, True, parts_a, merge_out.at[0:32], bufs[0]),
        stream(place, sems, "y", "x", 32, True, parts_b, merge_out.at[32:64], bufs[1]),
    ]
    attending = [
        stream(place, sems, "x", "y", 16, False, parts_c, part_a, bufs[2]),
        stream(place, sems, "y", "x", 16, False, parts_d, part_b, bufs[3]),
    ]

    def back_norm(rows, scale):
        grad = gn_ref[rows].astype(F32) * gain_attn
        out = norm_back(grad, hat_ref[rows], scale)
        go_ref[rows] = out.astype(BF16)
        for x in range(NX):
            lanes = slice(x * LANES, (x + 1) * LANES)
            roll_ref[rows, lanes] = pltpu.roll(out[:, lanes], 64, 1).astype(BF16)
        gm_ref[rows] = nt(go_ref[rows], wp_ref[...]).astype(BF16)

    back_norm(own, scale_own)
    advance(merging)
    halo_hidden.wait_recv()
    back_norm(far, scale_far)

    acc_ref[...] = jnp.zeros_like(acc_ref)

    def backward(w, carry):
        starts = [g * LANES for g in range(GROUPS)]
        grads = [stack_heads(take(gm_ref, w, start), masks16) for start in starts]
        grad_probs = [
            nt(take(qkv_ref, w, 2 * D + start), grad) for start, grad in zip(starts, grads)
        ]
        for g, start in enumerate(starts):
            value = nn(probs_ref[w, g].astype(BF16), grads[g])
            put(act_ref, w, 2 * D + start, value.astype(BF16))
        grad_scores = []
        for g in range(GROUPS):
            probs = probs_ref[w, g]
            weighted = probs * grad_probs[g]
            grad_score = weighted - probs * jnp.sum(weighted, 0, keepdims=True)
            acc_ref[g] += grad_score
            grad_scores.append(grad_score.astype(BF16))
        for g, start in enumerate(starts):
            query = stack_heads(take(qh_ref, w, start), masks16)
            put(dn_ref, w, D + start, nn(grad_scores[g], query))
        outs = [tn(grad_scores[g], take(kh_ref, w, starts[g])) for g in range(GROUPS)]
        for g, start in enumerate(starts):
            put(dn_ref, w, start, fold_heads(outs[g], masks))
        return carry

    lax.fori_loop(0, 4, backward, 0, unroll=2)
    for g in range(GROUPS):
        for part in (0, D):
            cols = slice(part + g * LANES, part + (g + 1) * LANES)
            grad = dn_ref[:, cols]
            if part == 0:
                grad = grad * scales[g]
            inverse = inv_ref[:, cols]
            unit = qkv_ref[:, cols].astype(F32) * inverse
            act_ref[:, cols] = (inverse * (grad - unit * head_sum(unit * grad, heads))).astype(BF16)

    advance(merging)

    left = iota((1, LANES), 1) < 64
    for x in range(NX):
        block = nn(xt_ref[...], act_ref[:, x * 384 : (x + 1) * 384])
        rolled = nn(mixedt_ref[...], roll_ref[:, x * LANES : (x + 1) * LANES])
        middle = block[:, 128:256]
        firsts = (block[:, :128], block[:, 256:])
        seconds = (jnp.where(left, middle, rolled), jnp.where(left, rolled, middle))
        for c in range(CORES):
            one, two = firsts[c].astype(BF16), seconds[c].astype(BF16)
            for y in range(NY):
                rows = slice(y * 128, (y + 1) * 128)
                sum_c[c, x, y] = one[rows]
                sum_d[c, y, x] = two[rows]
        parts_c.send(x)
        parts_d.send(x)

    gs_ref[far] = nt(act_ref[far], wq_ref[...]).astype(BF16)
    halo_shifted = sems.copy(gs_ref.at[far], gs_in, after)
    advance(attending)

    bias_part = gather_bias(acc_ref, onehot_ref, grid_ref)
    biasing = [bias_sum(place, sems, bias_part, padded_ref, bias_bufs)]
    advance(biasing)
    gs_ref[own] = nt(act_ref[own], wq_ref[...]).astype(BF16)
    gs_ref[own] = (gh_ref[far].astype(F32) + gs_ref[own].astype(F32)).astype(BF16)
    advance(biasing)
    halo_shifted.wait_recv()
    gn_own = (gh_ref[own].astype(F32) + gs_in[...].astype(F32)).astype(BF16)
    tokens_out[...] = tn(strip_ref[...], jnp.concatenate([gn_own, gs_ref[own]], axis=0)).astype(
        BF16
    )
    while merging or attending or biasing:
        advance(attending)
        advance(merging)
        advance(biasing)
    for copy in (halo_tokens, halo_normed, halo_hidden, halo_shifted):
        copy.wait_send()

    bias_out[...] = padded_ref[:, :OFFSETS]
    one, two = part_a[...], part_b[...]
    one_rolled, two_rolled = pltpu.roll(one, 64, 1), pltpu.roll(two, 64, 1)
    first_core = place.c == 0
    qkv_out[:, :128] = jnp.where(first_core, one, jnp.where(left, two_rolled, one_rolled))
    qkv_out[:, 128:] = jnp.where(first_core, two, one_rolled)[:, :64]
    proj_out[...] = jnp.where(first_core, two_rolled, two)[:, :64]


def block(tokens, region, valid, wq, wp, wm, scale, table, gain_attn, gain_merge, cot):
    vmem = pl.BlockSpec(memory_space=pltpu.VMEM)
    smem = pl.BlockSpec(memory_space=pltpu.SMEM)
    far = pl.BlockSpec(memory_space=pl.ANY)
    total = 4 + sum(stream_copies(ring) for _, ring in STREAMS) + BIAS_COPIES
    inputs = [tokens, wq, region, valid, table, wp, gain_attn, wm, gain_merge, cot]

    def buf(*shape):
        return pltpu.VMEM(shape, BF16)

    def wide(*shape):
        return pltpu.VMEM(shape, F32)

    return pl.pallas_call(
        block_kernel,
        out_shape=[
            jax.ShapeDtypeStruct((64, 1024), BF16),
            jax.ShapeDtypeStruct((TOKENS, D), BF16),
            jax.ShapeDtypeStruct((16, 192), F32),
            jax.ShapeDtypeStruct((16, 64), F32),
            jax.ShapeDtypeStruct((64, 128), F32),
            jax.ShapeDtypeStruct((16, OFFSETS), F32),
        ],
        in_specs=[smem] + [far] * len(inputs),
        out_specs=[vmem] * 6,
        scratch_shapes=[pltpu.VMEM(value.shape, value.dtype) for value in inputs]
        + [
            buf(TOKENS, TOKENS),
            buf(HALF, HALF),
            buf(256, 1024),
            buf(TOKENS, D),
            buf(TOKENS, D),
            buf(TOKENS, 3 * D),
            wide(TOKENS, 2 * D),
            buf(TOKENS, D),
            buf(TOKENS, D),
            buf(TOKENS, D),
            buf(TOKENS, D),
            wide(4, PLACES, WIDE),
            wide(BIAS_ROWS, BIAS_LANES),
            wide(128, 128),
            wide(GROUPS, PLACES, WIDE),
            wide(4, GROUPS, PLACES, WIDE),
            buf(TOKENS, D),
            buf(TOKENS, D),
            wide(TOKENS, D),
            buf(HALF, D),
            buf(64, 2048),
            buf(D, TOKENS),
            buf(D, TOKENS),
            buf(2048, 64),
            buf(TOKENS, D),
            buf(TOKENS, D),
            buf(TOKENS, D),
            buf(TOKENS, D),
            buf(TOKENS, D),
            wide(TOKENS, 2 * D),
            buf(TOKENS, 3 * D),
            buf(TOKENS, D),
            buf(HALF, D),
            wide(GROUPS, PLACES, WIDE),
            buf(CORES, NX, NY, NZ * 32, LANES),
            buf(CORES, NY, NX, NZ * 32, LANES),
            wide(16, LANES),
            wide(16, LANES),
            buf(CORES, NX, NY, NZ * 16, LANES),
            buf(CORES, NY, NX, NZ * 16, LANES),
        ]
        + sum([stream_scratch(*kind) for kind in STREAMS], [])
        + bias_scratch()
        + [
            pltpu.SemaphoreType.DMA((total,)),
            pltpu.SemaphoreType.DMA((total,)),
            pltpu.SemaphoreType.DMA((len(inputs),)),
        ],
        compiler_params=pltpu.CompilerParams(
            collective_id=0, has_side_effects=True, vmem_limit_bytes=56 * 1024 * 1024
        ),
        name="block",
    )(scale, *inputs)


def hand_out_kernel(*refs):
    count = len(refs) // 2
    copies = [
        pltpu.make_async_copy(refs[i], refs[count + i], refs[-1].at[i]) for i in range(count)
    ]
    for copy in copies:
        copy.start()
    for copy in copies:
        copy.wait()


def hand_out(values):
    near, far = pl.BlockSpec(memory_space=pltpu.VMEM), pl.BlockSpec(memory_space=pl.ANY)
    return pl.pallas_call(
        hand_out_kernel,
        out_shape=[jax.ShapeDtypeStruct(value.shape, value.dtype) for value in values],
        in_specs=[near] * len(values),
        out_specs=[far] * len(values),
        scratch_shapes=[pltpu.SemaphoreType.DMA((len(values),))],
        name="hand_out",
    )(*values)


def shards(
    tokens,
    region,
    valid,
    qkv_weight,
    proj_weight,
    merge_weight,
    logit_scale,
    bias_table,
    gain_attn,
    gain_merge,
    cotangent,
):
    merged, grad_tokens, grad_qkv, grad_proj, grad_merge, grad_bias = hand_out(
        block(
        tokens.reshape(TOKENS, D),
        region[0].T,
        valid[0].T,
        qkv_weight,
        proj_weight,
        merge_weight,
        logit_scale,
        bias_table,
        gain_attn[None],
        gain_merge[None],
        cotangent.reshape(64, 1024),
    ))
    return (
        merged.reshape(cotangent.shape),
        grad_tokens.reshape(tokens.shape),
        grad_qkv,
        grad_proj,
        grad_merge,
        grad_bias,
    )


def solution(mesh):
    return jax.shard_map(
        shards,
        mesh=mesh,
        in_specs=(
            P("dp", "space", None, None),
            P("dp", None, None),
            P("dp", None, None),
            P(),
            P(),
            P(),
            P(),
            P(),
            P(),
            P(),
            P("dp", "space", None, None),
        ),
        out_specs=(
            P("dp", "space", None, None),
            P("dp", "space", None, None),
            P("space", "dp"),
            P("space", "dp"),
            P("space", "dp"),
            P(),
        ),
        check_vma=False,
    )
```

```python
import functools

import jax
import jax.numpy as jnp
from jax import lax
from jax.experimental import pallas as pl
from jax.experimental.pallas import tpu as pltpu
from jax.sharding import PartitionSpec as P

WIN = 8
HEAD_DIM = 32
SHIFT = 4
OFFSETS = 225
NX, NY, NZ, CORES = 4, 4, 8, 2
LANES = 128
MESH = pl.DeviceIdType.MESH


class Place:
    def __init__(self):
        strip, image = lax.axis_index("space"), lax.axis_index("dp")
        self.y, self.z = strip // NZ, lax.rem(strip, NZ)
        self.x, self.c = image // CORES, lax.rem(image, CORES)

    def at(self, x=None, y=None, z=None, c=None):
        x = self.x if x is None else x
        y = self.y if y is None else y
        z = self.z if z is None else z
        c = self.c if c is None else c
        return (y * NZ + z, x * CORES + c)

    def along(self, axis, step):
        count = {"x": NX, "y": NY, "z": NZ, "c": CORES}[axis]
        return self.at(**{axis: lax.rem(getattr(self, axis) + step, count)})

    def partners(self):
        return (
            [self.along("c", 1)]
            + [self.along("x", step) for step in range(1, NX)]
            + [self.along("y", step) for step in range(1, NY)]
            + [self.along("z", step) for step in range(1, NZ)]
        )


class Sems:
    def __init__(self, send, recv):
        self.send, self.recv, self.used = send, recv, 0

    def copy(self, source, target, device):
        index = self.used
        self.used += 1
        made = pltpu.make_async_remote_copy(
            src_ref=source,
            dst_ref=target,
            send_sem=self.send.at[index],
            recv_sem=self.recv.at[index],
            device_id=device,
            device_id_type=MESH,
        )
        made.start()
        return made


def add_blocks(count, put, parts):
    def body(index, carry):
        total = parts[0](index).astype(jnp.float32)
        for part in parts[1:]:
            total = total + part(index).astype(jnp.float32)
        put(index, total.astype(jnp.bfloat16))
        return carry

    if count == 1:
        body(0, 0)
    else:
        lax.fori_loop(0, count, body, 0)


def ring_sum(place, sems, axis, held, prepare, blocks, far_lo, far_hi, from_dn, from_up, put_out):
    me = getattr(place, axis)
    up, dn, far = lax.rem(me + 1, 4), lax.rem(me + 3, 4), lax.rem(me + 2, 4)
    to_up, to_dn = place.along(axis, 1), place.along(axis, 3)
    half = blocks // 2
    lo, hi = pl.ds(0, half), pl.ds(half, half)
    prepare(far)
    one = sems.copy(held.at[far, lo], far_lo, to_up)
    two = sems.copy(held.at[far, hi], far_hi, to_dn)
    prepare(up)
    three = sems.copy(held.at[up, hi], from_dn.at[hi], to_up)
    prepare(dn)
    four = sems.copy(held.at[dn, lo], from_up.at[lo], to_dn)
    prepare(me)
    yield

    def put_up(i, v):
        held[up, i] = v

    def put_dn(i, v):
        held[dn, half + i] = v

    one.wait_recv()
    add_blocks(half, put_up, [lambda i: held[up, i], lambda i: far_lo[i]])
    five = sems.copy(held.at[up, lo], from_dn.at[lo], to_up)
    two.wait_recv()
    add_blocks(half, put_dn, [lambda i: held[dn, half + i], lambda i: far_hi[i]])
    six = sems.copy(held.at[dn, hi], from_up.at[hi], to_dn)
    yield
    three.wait_recv()
    four.wait_recv()
    five.wait_recv()
    six.wait_recv()
    add_blocks(
        blocks, put_out, [lambda i: held[me, i], lambda i: from_dn[i], lambda i: from_up[i]]
    )
    for copy in (one, two, three, four, five, six):
        copy.wait_send()


def shot_sum(place, sems, axis, count, held, prepare, parts, blocks, arrived, out):
    me = getattr(place, axis)
    sent = []
    for step in range(1, count):
        target = lax.rem(me + step, count)
        prepare(target)
        sent.append(
            sems.copy(held.at[target], arrived.at[step - 1], place.along(axis, step))
        )
    prepare(me)
    yield
    for copy in sent:
        copy.wait_recv()
    add_blocks(
        blocks,
        out,
        [lambda i: parts(held, me, i)]
        + [functools.partial(parts, arrived, step) for step in range(count - 1)],
    )
    for copy in sent:
        copy.wait_send()


def stream_scratch(rows, ring):
    full = NZ * rows
    shapes = [
        (4, 4, full, LANES),
        (4, 4, full, LANES),
        (4, NZ, rows, LANES),
        (3, NZ, rows, LANES),
        (NZ, rows, LANES),
        (NZ - 1, rows, LANES),
    ]
    if ring:
        shapes += [(2, full, LANES), (2, full, LANES), (4, full, LANES), (4, full, LANES)]
    else:
        shapes += [(3, 4, full, LANES)]
    return [pltpu.VMEM(shape, jnp.bfloat16) for shape in shapes]


def stream_copies(ring):
    return NX + (6 if ring else 3) + 3 + (NZ - 1)


class CorePart:
    def __init__(self, place, sems, x_first, source, other):
        self.place, self.sems, self.x_first = place, sems, x_first
        self.source, self.other, self.sent = source, other, []

    def send(self, x):
        across, theirs = self.place.along("c", 1), 1 - self.place.c
        if self.x_first:
            pair = self.source.at[theirs, x], self.other.at[x]
        else:
            pair = self.source.at[theirs, :, x], self.other.at[:, x]
        self.sent.append(self.sems.copy(*pair, across))


def stream(place, sems, first, second, rows, ring, cores, out, bufs):
    core, one, late, two, last = bufs[1:6]
    source, other, mine = cores.source, cores.other, place.c
    for copy in cores.sent:
        copy.wait_recv()

    def add_core(k):
        def put_core(i, v):
            core[k, i] = v

        add_blocks(4, put_core, [lambda i: source[mine, k, i], lambda i: other[k, i]])

    def put_one(i, v):
        one[i] = v.reshape(NZ, rows, LANES)

    def put_two(i, v):
        two[...] = v

    def nothing(k):
        pass

    if ring:
        yield from ring_sum(place, sems, first, core, add_core, 4, *bufs[6:], put_one)
    else:
        yield from shot_sum(
            place, sems, first, 4, core, add_core, lambda ref, k, i: ref[k, i], 4, bufs[6], put_one
        )
    yield from shot_sum(
        place, sems, second, 4, one, nothing, lambda ref, k, i: ref[k], 1, late, put_two
    )
    sent = []
    for step in range(1, NZ):
        target = lax.rem(place.z + step, NZ)
        sent.append(sems.copy(two.at[target], last.at[step - 1], place.along("z", step)))
    yield
    total = two[place.z].astype(jnp.float32)
    for step in range(1, NZ):
        sent[step - 1].wait_recv()
        total = total + last[step - 1].astype(jnp.float32)
    out[...] = total
    for copy in sent + cores.sent:
        copy.wait_send()


BIAS_ROWS, BIAS_LANES = 16, 256
BIAS_COPIES = 1 + (NX - 1) + (NY - 1) + (NZ - 1)


def bias_scratch():
    return [
        pltpu.VMEM((count, BIAS_ROWS, BIAS_LANES), jnp.float32)
        for count in (CORES, NX, NY, NZ)
    ]


def bias_sum(place, sems, value, out, bufs):
    copies = []
    for axis, count, buf in zip("cxyz", (CORES, NX, NY, NZ), bufs):
        me = getattr(place, axis)
        buf[me] = value
        sent = [
            sems.copy(buf.at[me], buf.at[me], place.along(axis, step)) for step in range(1, count)
        ]
        yield
        for copy in sent:
            copy.wait_recv()
        value = buf[0]
        for index in range(1, count):
            value = value + buf[index]
        copies += sent
    out[...] = value
    for copy in copies:
        copy.wait_send()


def advance(tasks):
    for task in list(tasks):
        try:
            next(task)
        except StopIteration:
            tasks.remove(task)


def greet(partners):
    barrier = pltpu.get_barrier_semaphore()
    for device in partners:
        pl.semaphore_signal(barrier, inc=1, device_id=device, device_id_type=MESH)


def enter(partners):
    pl.semaphore_wait(pltpu.get_barrier_semaphore(), len(partners))


F32, BF16 = jnp.float32, jnp.bfloat16
TOKENS, D, GROUPS = 256, 512, 4
HALF = TOKENS // 2
PLACES = WIN * WIN
WIDE = 4 * PLACES


def nn(a, b):
    return lax.dot_general(a, b, (((1,), (0,)), ((), ())), preferred_element_type=F32)


def nt(a, b):
    return lax.dot_general(a, b, (((1,), (1,)), ((), ())), preferred_element_type=F32)


def tn(a, b):
    return lax.dot_general(a, b, (((0,), (0,)), ((), ())), preferred_element_type=F32)


def split2(t):
    high = t.astype(BF16)
    return high, (t - high.astype(F32)).astype(BF16)


def split3(t):
    high = t.astype(BF16)
    rest = t - high.astype(F32)
    middle = rest.astype(BF16)
    return high, middle, (rest - middle.astype(F32)).astype(BF16)


def iota(shape, axis):
    return lax.broadcasted_iota(jnp.int32, shape, axis)


def bits(t, low, count):
    return lax.bitwise_and(lax.shift_right_logical(t, low), (1 << count) - 1)


def one_hot(match):
    return jnp.where(match, 1.0, 0.0).astype(BF16)


def strip_order():
    i = iota((TOKENS, 1), 0)
    column = lax.bitwise_and(bits(i, 5, 2) * 8 + bits(i, 0, 3) + SHIFT, 31)
    natural = (bits(i, 7, 1) * 4 + bits(i, 3, 2)) * 32 + column
    return one_hot(iota((TOKENS, TOKENS), 1) == natural)


def quad_order():
    i = iota((HALF, 1), 0)
    column = lax.bitwise_and(2 * bits(i, 0, 4) + bits(i, 6, 1) + 32 - SHIFT, 31)
    row = 2 * bits(i, 4, 1) + bits(i, 5, 1)
    place = bits(column, 3, 2) * 32 + row * 8 + bits(column, 0, 3)
    return one_hot(iota((HALF, HALF), 1) == place)


def offset_order():
    j = iota((1, 1024), 1)
    offset = bits(j, 3, 4) * 15 + bits(j, 0, 3) - bits(j, 7, 3) + 7
    offset = jnp.where(bits(j, 3, 4) < 15, offset, -1)
    return one_hot(iota((256, 1024), 0) == offset)


def head_order():
    return one_hot(bits(iota((256, 128), 0), 5, 2) == bits(iota((256, 128), 1), 5, 2))


def head_sum(t, heads):
    return nn(jnp.concatenate(split2(t), axis=1), heads)


def stack_heads(t, lane_masks):
    return jnp.concatenate([t * mask for mask in lane_masks], axis=0)


def fold_heads(t, lane_masks):
    total = t[:PLACES] * lane_masks[0]
    for h in range(1, 4):
        total = total + t[h * PLACES : (h + 1) * PLACES] * lane_masks[h]
    return total


def norm_parts(t):
    centred = t - jnp.mean(t, -1, keepdims=True)
    scale = lax.rsqrt(jnp.mean(centred * centred, -1, keepdims=True) + 1e-05)
    return centred * scale, scale


def norm_back(grad, hat, scale):
    return scale * (
        grad - jnp.mean(grad, -1, keepdims=True) - hat * jnp.mean(grad * hat, -1, keepdims=True)
    )


def window_masks(place, region_ref, valid_ref, mask_ref):
    strip = place.y * NZ + place.z
    place_lane = iota((1, WIDE), 1) % PLACES
    row, col = place_lane // WIN, place_lane % WIN
    region = region_ref[...].astype(F32)
    valid = valid_ref[...].astype(F32)
    source_row = lax.rem(strip * WIN + SHIFT + row, 256)
    region_row = iota((64, WIDE), 0) == source_row // 4
    valid_row = iota((256, WIDE), 0) == source_row
    shifted_row = strip * WIN + row
    row_part = jnp.where(shifted_row < 256 - WIN, 0, jnp.where(shifted_row < 256 - SHIFT, 1, 2))
    diagonal = iota((PLACES, WIDE), 0) == place_lane
    pick = (iota((PLACES, WIDE), 0) == iota((PLACES, WIDE), 1)).astype(F32)
    for w in range(4):
        source_col = lax.rem(w * WIN + SHIFT + col, 32)
        shifted_col = w * WIN + col
        col_part = jnp.where(shifted_col < 32 - WIN, 0, jnp.where(shifted_col < 32 - SHIFT, 1, 2))
        region_pick = (iota((8, WIDE), 0) == source_col // 4).astype(F32)
        valid_pick = (iota((32, WIDE), 0) == source_col).astype(F32)
        swath = jnp.sum(jnp.where(region_row, tn(region, region_pick), 0.0), 0, keepdims=True)
        live = jnp.sum(jnp.where(valid_row, tn(valid, valid_pick), 0.0), 0, keepdims=True)
        label = swath * 9.0 + (row_part * 3 + col_part).astype(F32)
        label_key = jnp.sum(pick * label, 1, keepdims=True)
        live_key = jnp.sum(pick * live, 1, keepdims=True)
        same = (label_key == label).astype(F32)
        open_key = jnp.where(diagonal, 1.0, jnp.where(live_key == 1.0, 1.0, 0.0))
        mask_ref[w] = same * open_key


def spread_bias(table_ref, onehot_ref, padded_ref, grid_ref, bias_ref):
    padded_ref[...] = jnp.zeros_like(padded_ref)
    padded_ref[:, :OFFSETS] = table_ref[...]
    parts = nn(jnp.concatenate(split3(padded_ref[...]), axis=0), onehot_ref[...])
    spread = parts[:16] + parts[16:32] + parts[32:]
    for ct in range(8):
        grid_ref[pl.ds(ct, 16, stride=8), :] = spread[:, ct * 128 : (ct + 1) * 128]
    left = iota((8, 128), 1) < PLACES
    for pair in range(8):
        even = grid_ref[pair * 16 : pair * 16 + 8]
        odd = grid_ref[pair * 16 + 8 : pair * 16 + 16]
        lanes = pl.ds(pair % 2 * 128, 128)
        for rt in range(8):
            shift = (7 - rt) * 8
            bias_ref[pair // 2, rt * 8 : rt * 8 + 8, lanes] = jnp.where(
                left,
                pltpu.roll(even, (128 - shift) % 128, 1),
                pltpu.roll(odd, (128 + 64 - shift) % 128, 1),
            )


def gather_bias(acc_ref, onehot_ref, grid_ref):
    left = iota((8, 128), 1) < PLACES
    for pair in range(8):
        lanes = pl.ds(pair % 2 * 128, 128)
        even = jnp.zeros((8, 128), F32)
        odd = jnp.zeros((8, 128), F32)
        for rt in range(8):
            shift = (7 - rt) * 8
            piece = acc_ref[pair // 2, rt * 8 : rt * 8 + 8, lanes]
            even = even + pltpu.roll(jnp.where(left, piece, 0.0), shift, 1)
            odd = odd + pltpu.roll(jnp.where(left, 0.0, piece), (64 + shift) % 128, 1)
        grid_ref[pair * 16 : pair * 16 + 8] = even
        grid_ref[pair * 16 + 8 : pair * 16 + 16] = odd
    grid = jnp.concatenate([grid_ref[pl.ds(ct, 16, stride=8), :] for ct in range(8)], axis=1)
    parts = nt(jnp.concatenate(split3(grid), axis=0), onehot_ref[...])
    return parts[:16] + parts[16:32] + parts[32:]


def window_rows(w):
    return (
        pl.ds(pl.multiple_of(w * 32, 32), 32),
        pl.ds(pl.multiple_of(HALF + w * 32, 32), 32),
    )


def take(ref, w, start):
    first, second = window_rows(w)
    lanes = slice(start, start + LANES)
    return jnp.concatenate([ref[first, lanes], ref[second, lanes]], axis=0)


def put(ref, w, start, value):
    first, second = window_rows(w)
    lanes = slice(start, start + LANES)
    ref[first, lanes] = value[:32]
    ref[second, lanes] = value[32:]


STREAMS = ((32, True), (32, True), (16, False), (16, False))


def block_kernel(
    scale_ref,
    tok_hbm,
    wq_hbm,
    region_hbm,
    valid_hbm,
    table_hbm,
    wp_hbm,
    gain_attn_hbm,
    wm_hbm,
    gain_merge_hbm,
    cot_hbm,
    merged_out,
    tokens_out,
    qkv_out,
    proj_out,
    merge_out,
    bias_out,
    tok_ref,
    wq_ref,
    region_ref,
    valid_ref,
    table_ref,
    wp_ref,
    gain_attn_ref,
    wm_ref,
    gain_merge_ref,
    cot_ref,
    strip_ref,
    quad_ref,
    onehot_ref,
    tw_ref,
    x_ref,
    qkv_ref,
    inv_ref,
    qh_ref,
    ql_ref,
    kh_ref,
    kl_ref,
    mask_ref,
    padded_ref,
    grid_ref,
    bias_ref,
    probs_ref,
    mixed_ref,
    normed_ref,
    hat_ref,
    normed_in,
    quads_ref,
    xt_ref,
    mixedt_ref,
    quadst_ref,
    gh_ref,
    gn_ref,
    go_ref,
    roll_ref,
    gm_ref,
    dn_ref,
    act_ref,
    gs_ref,
    gs_in,
    acc_ref,
    sum_a,
    sum_b,
    part_a,
    part_b,
    sum_c,
    sum_d,
    *scratch,
):
    bufs, at = [], 0
    for rows, ring in STREAMS:
        many = len(stream_scratch(rows, ring))
        bufs.append(scratch[at : at + many])
        at += many
    bias_bufs = scratch[at : at + 4]
    send, recv, local = scratch[at + 4 :]
    place = Place()
    sems = Sems(send, recv)
    strip = place.y * NZ + place.z
    image = place.x * CORES + place.c
    after = (lax.rem(strip + 1, NY * NZ), image)
    before = (lax.rem(strip + NY * NZ - 1, NY * NZ), image)
    own, far = slice(0, HALF), slice(HALF, TOKENS)

    partners = place.partners() + [after, before]
    greet(partners)
    loads = {}
    for index, (source, target) in enumerate(
        (
            (tok_hbm, tok_ref),
            (wq_hbm, wq_ref),
            (region_hbm, region_ref),
            (valid_hbm, valid_ref),
            (table_hbm, table_ref),
            (wp_hbm, wp_ref),
            (gain_attn_hbm, gain_attn_ref),
            (wm_hbm, wm_ref),
            (gain_merge_hbm, gain_merge_ref),
            (cot_hbm, cot_ref),
        )
    ):
        loads[id(target)] = pltpu.make_async_copy(source, target, local.at[index])
        loads[id(target)].start()

    def ready(*refs):
        for ref in refs:
            loads.pop(id(ref)).wait()

    strip_ref[...] = strip_order()
    ready(tok_ref)
    tw_ref[...] = nn(strip_ref[...], tok_ref[...]).astype(BF16)
    enter(partners)
    halo_tokens = [
        sems.copy(tw_ref.at[pl.ds(at, 64)], x_ref.at[pl.ds(HALF + at, 64)], before)
        for at in (0, 64)
    ]
    x_ref[own] = tw_ref[far]

    lane = iota((1, LANES), 1)
    masks = [(lane // HEAD_DIM == h).astype(F32) for h in range(4)]
    masks16 = [mask.astype(BF16) for mask in masks]
    scales = []
    for g in range(GROUPS):
        row = jnp.zeros((1, LANES), F32)
        for h in range(4):
            row = row + masks[h] * scale_ref[g * 4 + h]
        scales.append(row)
    ready(wq_ref)
    heads = head_order()

    def normalise(rows):
        for part, high, low in ((0, qh_ref, ql_ref), (D, kh_ref, kl_ref)):
            columns = [slice(part + g * LANES, part + (g + 1) * LANES) for g in range(GROUPS)]
            raws = [qkv_ref[rows, cols].astype(F32) for cols in columns]
            sums = [head_sum(raw * raw, heads) for raw in raws]
            for g, cols in enumerate(columns):
                inverse = lax.rsqrt(sums[g] + 1e-06)
                inv_ref[rows, cols] = inverse
                unit = raws[g] * inverse
                if part == 0:
                    unit = unit * scales[g]
                near = slice(g * LANES, (g + 1) * LANES)
                high[rows, near], low[rows, near] = split2(unit)

    qkv_ref[own] = nn(x_ref[own], wq_ref[...]).astype(BF16)
    normalise(own)
    ready(region_ref, valid_ref)
    window_masks(place, region_ref, valid_ref, mask_ref)
    quad_ref[...] = quad_order()
    onehot_ref[...] = offset_order()
    ready(table_ref)
    spread_bias(table_ref, onehot_ref, padded_ref, grid_ref, bias_ref)
    def forward(w, carry):
        allowed = mask_ref[w] > 0.5
        scores = []
        for g in range(GROUPS):
            start = g * LANES
            kh, kl = take(kh_ref, w, start), take(kl_ref, w, start)
            qh = stack_heads(take(qh_ref, w, start), masks16)
            ql = stack_heads(take(ql_ref, w, start), masks16)
            scores.append(
                nt(jnp.concatenate([kh, kl, kh], axis=1), jnp.concatenate([qh, qh, ql], axis=1))
            )
        rounded = []
        for g in range(GROUPS):
            score = jnp.where(allowed, scores[g] + bias_ref[g], -1000000000.0)
            expo = jnp.exp(score - jnp.max(score, 0, keepdims=True))
            probs = expo * (1.0 / jnp.sum(expo, 0, keepdims=True))
            probs_ref[w, g] = probs
            rounded.append(probs.astype(BF16))
        outs = [tn(rounded[g], take(qkv_ref, w, 2 * D + g * LANES)) for g in range(GROUPS)]
        for g in range(GROUPS):
            put(mixed_ref, w, g * LANES, fold_heads(outs[g], masks).astype(BF16))
        return carry

    ready(wp_ref, gain_attn_ref)
    gain_attn = gain_attn_ref[...]

    def project(rows):
        hat, scale = norm_parts(nn(mixed_ref[rows], wp_ref[...]))
        hat_ref[rows] = hat
        normed_ref[rows] = (hat * gain_attn).astype(BF16)
        return scale

    pieces = [(at, slice(HALF + at, HALF + at + 64)) for at in (0, 64)]
    halo_normed, scales_far = [], []
    for index, (at, rows) in enumerate(pieces):
        halo_tokens[index].wait_recv()
        qkv_ref[rows] = nn(x_ref[rows], wq_ref[...]).astype(BF16)
        normalise(rows)
        lax.fori_loop(2 * index, 2 * index + 2, forward, 0, unroll=2)
        scales_far.append(project(rows))
        halo_normed.append(
            sems.copy(
                normed_ref.at[pl.ds(HALF + at, 64)], normed_in.at[pl.ds(at, 64)], after
            )
        )
    scale_own = project(own)

    def make_quads(which, added):
        rows = slice(which * HALF, (which + 1) * HALF)
        hidden = (tw_ref[rows].astype(F32) + added.astype(F32)).astype(BF16)
        sorted_rows = nn(quad_ref[...], hidden).astype(BF16)
        for k in range(4):
            quads_ref[which * 32 : which * 32 + 32, k * D : (k + 1) * D] = sorted_rows[
                k * 32 : (k + 1) * 32
            ]

    make_quads(1, normed_ref[own])
    xt_ref[...] = x_ref[...].T
    mixedt_ref[...] = mixed_ref[...].T
    ready(wm_ref, gain_merge_ref, cot_ref)
    for copy in halo_normed:
        copy.wait_recv()
    make_quads(0, normed_in[...])
    quadst_ref[...] = quads_ref[...].T

    gain_merge = gain_merge_ref[...]
    hat, scale = norm_parts(nn(quads_ref[...], wm_ref[...]))
    merged_out[...] = (hat * gain_merge).astype(BF16)
    grad_pre = norm_back(cot_ref[...].astype(F32) * gain_merge, hat, scale).astype(BF16)
    parts_a = CorePart(place, sems, True, sum_a, bufs[0][0])
    parts_b = CorePart(place, sems, False, sum_b, bufs[1][0])
    parts_c = CorePart(place, sems, True, sum_c, bufs[2][0])
    parts_d = CorePart(place, sems, False, sum_d, bufs[3][0])
    for x in range(NX):
        for y in range(NY):
            block = nn(
                quadst_ref[y * D : (y + 1) * D], grad_pre[:, x * 256 : (x + 1) * 256]
            ).reshape(NZ, 2, 32, 256)
            for c in range(CORES):
                lanes = slice(c * LANES, (c + 1) * LANES)
                sum_a[c, x, y] = block[:, 0, :, lanes].reshape(NZ * 32, LANES).astype(BF16)
                sum_b[c, y, x] = block[:, 1, :, lanes].reshape(NZ * 32, LANES).astype(BF16)
        parts_a.send(x)
        parts_b.send(x)

    grad_quads = nt(grad_pre, wm_ref[...]).astype(BF16)
    for which in range(2):
        stacked = jnp.concatenate(
            [grad_quads[which * 32 : which * 32 + 32, k * D : (k + 1) * D] for k in range(4)],
            axis=0,
        )
        gh_ref[which * HALF : (which + 1) * HALF] = tn(quad_ref[...], stacked).astype(BF16)
        if which == 0:
            halo_hidden = [
                sems.copy(gh_ref.at[pl.ds(at, 64)], gn_ref.at[pl.ds(HALF + at, 64)], before)
                for at in (0, 64)
            ]
    gn_ref[own] = gh_ref[far]

    merging = [
        stream(place, sems, "x", "y", 32, True, parts_a, merge_out.at[0:32], bufs[0]),
        stream(place, sems, "y", "x", 32, True, parts_b, merge_out.at[32:64], bufs[1]),
    ]
    attending = [
        stream(place, sems, "x", "y", 16, False, parts_c, part_a, bufs[2]),
        stream(place, sems, "y", "x", 16, False, parts_d, part_b, bufs[3]),
    ]

    def back_norm(rows, scale):
        grad = gn_ref[rows].astype(F32) * gain_attn
        out = norm_back(grad, hat_ref[rows], scale)
        go_ref[rows] = out.astype(BF16)
        for x in range(NX):
            lanes = slice(x * LANES, (x + 1) * LANES)
            roll_ref[rows, lanes] = pltpu.roll(out[:, lanes], 64, 1).astype(BF16)
        gm_ref[rows] = nt(go_ref[rows], wp_ref[...]).astype(BF16)

    back_norm(own, scale_own)
    advance(merging)
    acc_ref[...] = jnp.zeros_like(acc_ref)

    def backward(w, carry):
        starts = [g * LANES for g in range(GROUPS)]
        grads = [stack_heads(take(gm_ref, w, start), masks16) for start in starts]
        grad_probs = [
            nt(take(qkv_ref, w, 2 * D + start), grad) for start, grad in zip(starts, grads)
        ]
        for g, start in enumerate(starts):
            value = nn(probs_ref[w, g].astype(BF16), grads[g])
            put(act_ref, w, 2 * D + start, value.astype(BF16))
        grad_scores = []
        for g in range(GROUPS):
            probs = probs_ref[w, g]
            weighted = probs * grad_probs[g]
            grad_score = weighted - probs * jnp.sum(weighted, 0, keepdims=True)
            acc_ref[g] += grad_score
            grad_scores.append(grad_score.astype(BF16))
        for g, start in enumerate(starts):
            query = stack_heads(take(qh_ref, w, start), masks16)
            put(dn_ref, w, D + start, nn(grad_scores[g], query))
        outs = [tn(grad_scores[g], take(kh_ref, w, starts[g])) for g in range(GROUPS)]
        for g, start in enumerate(starts):
            put(dn_ref, w, start, fold_heads(outs[g], masks))
        return carry

    for index, (at, rows) in enumerate(pieces):
        halo_hidden[index].wait_recv()
        back_norm(rows, scales_far[index])
        lax.fori_loop(2 * index, 2 * index + 2, backward, 0, unroll=2)
    for part in (0, D):
        columns = [slice(part + g * LANES, part + (g + 1) * LANES) for g in range(GROUPS)]
        grads = [dn_ref[:, cols] for cols in columns]
        if part == 0:
            grads = [grad * scale for grad, scale in zip(grads, scales)]
        units = [qkv_ref[:, cols].astype(F32) * inv_ref[:, cols] for cols in columns]
        sums = [head_sum(unit * grad, heads) for unit, grad in zip(units, grads)]
        for g, cols in enumerate(columns):
            act_ref[:, cols] = (inv_ref[:, cols] * (grads[g] - units[g] * sums[g])).astype(BF16)

    left = iota((1, LANES), 1) < 64
    for x in range(NX):
        block = nn(xt_ref[...], act_ref[:, x * 384 : (x + 1) * 384])
        rolled = nn(mixedt_ref[...], roll_ref[:, x * LANES : (x + 1) * LANES])
        middle = block[:, 128:256]
        firsts = (block[:, :128], block[:, 256:])
        seconds = (jnp.where(left, middle, rolled), jnp.where(left, rolled, middle))
        for c in range(CORES):
            one, two = firsts[c].astype(BF16), seconds[c].astype(BF16)
            for y in range(NY):
                rows = slice(y * 128, (y + 1) * 128)
                sum_c[c, x, y] = one[rows]
                sum_d[c, y, x] = two[rows]
        parts_c.send(x)
        parts_d.send(x)

    advance(merging)
    gs_ref[far] = nt(act_ref[far], wq_ref[...]).astype(BF16)
    halo_shifted = sems.copy(gs_ref.at[far], gs_in, after)
    advance(attending)

    bias_part = gather_bias(acc_ref, onehot_ref, grid_ref)
    biasing = [bias_sum(place, sems, bias_part, padded_ref, bias_bufs)]
    advance(biasing)
    gs_ref[own] = nt(act_ref[own], wq_ref[...]).astype(BF16)
    gs_ref[own] = (gh_ref[far].astype(F32) + gs_ref[own].astype(F32)).astype(BF16)
    advance(biasing)
    halo_shifted.wait_recv()
    gn_own = (gh_ref[own].astype(F32) + gs_in[...].astype(F32)).astype(BF16)
    tokens_out[...] = tn(strip_ref[...], jnp.concatenate([gn_own, gs_ref[own]], axis=0)).astype(
        BF16
    )
    while merging or attending or biasing:
        advance(merging)
        advance(attending)
        advance(biasing)
    for copy in halo_tokens + halo_normed + halo_hidden + [halo_shifted]:
        copy.wait_send()

    bias_out[...] = padded_ref[:, :OFFSETS]
    one, two = part_a[...], part_b[...]
    one_rolled, two_rolled = pltpu.roll(one, 64, 1), pltpu.roll(two, 64, 1)
    first_core = place.c == 0
    qkv_out[:, :128] = jnp.where(first_core, one, jnp.where(left, two_rolled, one_rolled))
    qkv_out[:, 128:] = jnp.where(first_core, two, one_rolled)[:, :64]
    proj_out[...] = jnp.where(first_core, two_rolled, two)[:, :64]


def block(tokens, region, valid, wq, wp, wm, scale, table, gain_attn, gain_merge, cot):
    vmem = pl.BlockSpec(memory_space=pltpu.VMEM)
    smem = pl.BlockSpec(memory_space=pltpu.SMEM)
    far = pl.BlockSpec(memory_space=pl.ANY)
    total = 7 + sum(stream_copies(ring) for _, ring in STREAMS) + BIAS_COPIES
    inputs = [tokens, wq, region, valid, table, wp, gain_attn, wm, gain_merge, cot]

    def buf(*shape):
        return pltpu.VMEM(shape, BF16)

    def wide(*shape):
        return pltpu.VMEM(shape, F32)

    return pl.pallas_call(
        block_kernel,
        out_shape=[
            jax.ShapeDtypeStruct((64, 1024), BF16),
            jax.ShapeDtypeStruct((TOKENS, D), BF16),
            jax.ShapeDtypeStruct((16, 192), F32),
            jax.ShapeDtypeStruct((16, 64), F32),
            jax.ShapeDtypeStruct((64, 128), F32),
            jax.ShapeDtypeStruct((16, OFFSETS), F32),
        ],
        in_specs=[smem] + [far] * len(inputs),
        out_specs=[vmem] * 6,
        scratch_shapes=[pltpu.VMEM(value.shape, value.dtype) for value in inputs]
        + [
            buf(TOKENS, TOKENS),
            buf(HALF, HALF),
            buf(256, 1024),
            buf(TOKENS, D),
            buf(TOKENS, D),
            buf(TOKENS, 3 * D),
            wide(TOKENS, 2 * D),
            buf(TOKENS, D),
            buf(TOKENS, D),
            buf(TOKENS, D),
            buf(TOKENS, D),
            wide(4, PLACES, WIDE),
            wide(BIAS_ROWS, BIAS_LANES),
            wide(128, 128),
            wide(GROUPS, PLACES, WIDE),
            wide(4, GROUPS, PLACES, WIDE),
            buf(TOKENS, D),
            buf(TOKENS, D),
            wide(TOKENS, D),
            buf(HALF, D),
            buf(64, 2048),
            buf(D, TOKENS),
            buf(D, TOKENS),
            buf(2048, 64),
            buf(TOKENS, D),
            buf(TOKENS, D),
            buf(TOKENS, D),
            buf(TOKENS, D),
            buf(TOKENS, D),
            wide(TOKENS, 2 * D),
            buf(TOKENS, 3 * D),
            buf(TOKENS, D),
            buf(HALF, D),
            wide(GROUPS, PLACES, WIDE),
            buf(CORES, NX, NY, NZ * 32, LANES),
            buf(CORES, NY, NX, NZ * 32, LANES),
            wide(16, LANES),
            wide(16, LANES),
            buf(CORES, NX, NY, NZ * 16, LANES),
            buf(CORES, NY, NX, NZ * 16, LANES),
        ]
        + sum([stream_scratch(*kind) for kind in STREAMS], [])
        + bias_scratch()
        + [
            pltpu.SemaphoreType.DMA((total,)),
            pltpu.SemaphoreType.DMA((total,)),
            pltpu.SemaphoreType.DMA((len(inputs),)),
        ],
        compiler_params=pltpu.CompilerParams(
            collective_id=0, has_side_effects=True, vmem_limit_bytes=56 * 1024 * 1024
        ),
        name="block",
    )(scale, *inputs)


def hand_out_kernel(*refs):
    count = len(refs) // 2
    copies = [
        pltpu.make_async_copy(refs[i], refs[count + i], refs[-1].at[i]) for i in range(count)
    ]
    for copy in copies:
        copy.start()
    for copy in copies:
        copy.wait()


def hand_out(values):
    near, far = pl.BlockSpec(memory_space=pltpu.VMEM), pl.BlockSpec(memory_space=pl.ANY)
    return pl.pallas_call(
        hand_out_kernel,
        out_shape=[jax.ShapeDtypeStruct(value.shape, value.dtype) for value in values],
        in_specs=[near] * len(values),
        out_specs=[far] * len(values),
        scratch_shapes=[pltpu.SemaphoreType.DMA((len(values),))],
        name="hand_out",
    )(*values)


def shards(
    tokens,
    region,
    valid,
    qkv_weight,
    proj_weight,
    merge_weight,
    logit_scale,
    bias_table,
    gain_attn,
    gain_merge,
    cotangent,
):
    merged, grad_tokens, grad_qkv, grad_proj, grad_merge, grad_bias = hand_out(
        block(
        tokens.reshape(TOKENS, D),
        region[0].T,
        valid[0].T,
        qkv_weight,
        proj_weight,
        merge_weight,
        logit_scale,
        bias_table,
        gain_attn[None],
        gain_merge[None],
        cotangent.reshape(64, 1024),
    ))
    return (
        merged.reshape(cotangent.shape),
        grad_tokens.reshape(tokens.shape),
        grad_qkv,
        grad_proj,
        grad_merge,
        grad_bias,
    )


def solution(mesh):
    return jax.shard_map(
        shards,
        mesh=mesh,
        in_specs=(
            P("dp", "space", None, None),
            P("dp", None, None),
            P("dp", None, None),
            P(),
            P(),
            P(),
            P(),
            P(),
            P(),
            P(),
            P("dp", "space", None, None),
        ),
        out_specs=(
            P("dp", "space", None, None),
            P("dp", "space", None, None),
            P("space", "dp"),
            P("space", "dp"),
            P("space", "dp"),
            P(),
        ),
        check_vma=False,
    )
```

```python
import functools

import jax
import jax.numpy as jnp
from jax import lax
from jax.experimental import pallas as pl
from jax.experimental.pallas import tpu as pltpu
from jax.sharding import PartitionSpec as P

WIN = 8
HEAD_DIM = 32
SHIFT = 4
OFFSETS = 225
NX, NY, NZ, CORES = 4, 4, 8, 2
LANES = 128
MESH = pl.DeviceIdType.MESH


class Place:
    def __init__(self):
        strip, image = lax.axis_index("space"), lax.axis_index("dp")
        self.y, self.z = strip // NZ, lax.rem(strip, NZ)
        self.x, self.c = image // CORES, lax.rem(image, CORES)

    def at(self, x=None, y=None, z=None, c=None):
        x = self.x if x is None else x
        y = self.y if y is None else y
        z = self.z if z is None else z
        c = self.c if c is None else c
        return (y * NZ + z, x * CORES + c)

    def along(self, axis, step):
        count = {"x": NX, "y": NY, "z": NZ, "c": CORES}[axis]
        return self.at(**{axis: lax.rem(getattr(self, axis) + step, count)})

    def partners(self):
        return (
            [self.along("c", 1)]
            + [self.along("x", step) for step in range(1, NX)]
            + [self.along("y", step) for step in range(1, NY)]
            + [self.along("z", step) for step in range(1, NZ)]
        )


class Sems:
    def __init__(self, send, recv):
        self.send, self.recv, self.used = send, recv, 0

    def copy(self, source, target, device):
        index = self.used
        self.used += 1
        made = pltpu.make_async_remote_copy(
            src_ref=source,
            dst_ref=target,
            send_sem=self.send.at[index],
            recv_sem=self.recv.at[index],
            device_id=device,
            device_id_type=MESH,
        )
        made.start()
        return made


def add_blocks(count, put, parts):
    def body(index, carry):
        total = parts[0](index).astype(jnp.float32)
        for part in parts[1:]:
            total = total + part(index).astype(jnp.float32)
        put(index, total.astype(jnp.bfloat16))
        return carry

    if count == 1:
        body(0, 0)
    else:
        lax.fori_loop(0, count, body, 0)


def ring_sum(place, sems, axis, held, prepare, blocks, far_lo, far_hi, from_dn, from_up, put_out):
    me = getattr(place, axis)
    up, dn, far = lax.rem(me + 1, 4), lax.rem(me + 3, 4), lax.rem(me + 2, 4)
    to_up, to_dn = place.along(axis, 1), place.along(axis, 3)
    half = blocks // 2
    lo, hi = pl.ds(0, half), pl.ds(half, half)
    prepare(far)
    one = sems.copy(held.at[far, lo], far_lo, to_up)
    two = sems.copy(held.at[far, hi], far_hi, to_dn)
    prepare(up)
    three = sems.copy(held.at[up, hi], from_dn.at[hi], to_up)
    prepare(dn)
    four = sems.copy(held.at[dn, lo], from_up.at[lo], to_dn)
    prepare(me)
    yield

    def put_up(i, v):
        held[up, i] = v

    def put_dn(i, v):
        held[dn, half + i] = v

    one.wait_recv()
    add_blocks(half, put_up, [lambda i: held[up, i], lambda i: far_lo[i]])
    five = sems.copy(held.at[up, lo], from_dn.at[lo], to_up)
    two.wait_recv()
    add_blocks(half, put_dn, [lambda i: held[dn, half + i], lambda i: far_hi[i]])
    six = sems.copy(held.at[dn, hi], from_up.at[hi], to_dn)
    yield
    three.wait_recv()
    four.wait_recv()
    five.wait_recv()
    six.wait_recv()
    add_blocks(
        blocks, put_out, [lambda i: held[me, i], lambda i: from_dn[i], lambda i: from_up[i]]
    )
    for copy in (one, two, three, four, five, six):
        copy.wait_send()


def shot_sum(place, sems, axis, count, held, prepare, parts, blocks, arrived, out):
    me = getattr(place, axis)
    sent = []
    for step in range(1, count):
        target = lax.rem(me + step, count)
        prepare(target)
        sent.append(
            sems.copy(held.at[target], arrived.at[step - 1], place.along(axis, step))
        )
    prepare(me)
    yield
    for copy in sent:
        copy.wait_recv()
    add_blocks(
        blocks,
        out,
        [lambda i: parts(held, me, i)]
        + [functools.partial(parts, arrived, step) for step in range(count - 1)],
    )
    for copy in sent:
        copy.wait_send()


def stream_scratch(rows, ring):
    full = NZ * rows
    shapes = [
        (4, 4, full, LANES),
        (4, 4, full, LANES),
        (4, NZ, rows, LANES),
        (3, NZ, rows, LANES),
        (NZ, rows, LANES),
        (NZ - 1, rows, LANES),
    ]
    if ring:
        shapes += [(2, full, LANES), (2, full, LANES), (4, full, LANES), (4, full, LANES)]
    else:
        shapes += [(3, 4, full, LANES)]
    return [pltpu.VMEM(shape, jnp.bfloat16) for shape in shapes]


def stream_copies(ring):
    return NX + (6 if ring else 3) + 3 + (NZ - 1)


class CorePart:
    def __init__(self, place, sems, x_first, source, other):
        self.place, self.sems, self.x_first = place, sems, x_first
        self.source, self.other, self.sent = source, other, []

    def send(self, x):
        across, theirs = self.place.along("c", 1), 1 - self.place.c
        if self.x_first:
            pair = self.source.at[theirs, x], self.other.at[x]
        else:
            pair = self.source.at[theirs, :, x], self.other.at[:, x]
        self.sent.append(self.sems.copy(*pair, across))


def stream(place, sems, first, second, rows, ring, cores, out, bufs):
    core, one, late, two, last = bufs[1:6]
    source, other, mine = cores.source, cores.other, place.c
    for copy in cores.sent:
        copy.wait_recv()

    def add_core(k):
        def put_core(i, v):
            core[k, i] = v

        add_blocks(4, put_core, [lambda i: source[mine, k, i], lambda i: other[k, i]])

    def put_one(i, v):
        one[i] = v.reshape(NZ, rows, LANES)

    def put_two(i, v):
        two[...] = v

    def nothing(k):
        pass

    if ring:
        yield from ring_sum(place, sems, first, core, add_core, 4, *bufs[6:], put_one)
    else:
        yield from shot_sum(
            place, sems, first, 4, core, add_core, lambda ref, k, i: ref[k, i], 4, bufs[6], put_one
        )
    yield from shot_sum(
        place, sems, second, 4, one, nothing, lambda ref, k, i: ref[k], 1, late, put_two
    )
    sent = []
    for step in range(1, NZ):
        target = lax.rem(place.z + step, NZ)
        sent.append(sems.copy(two.at[target], last.at[step - 1], place.along("z", step)))
    yield
    total = two[place.z].astype(jnp.float32)
    for step in range(1, NZ):
        sent[step - 1].wait_recv()
        total = total + last[step - 1].astype(jnp.float32)
    out[...] = total
    for copy in sent + cores.sent:
        copy.wait_send()


BIAS_ROWS, BIAS_LANES = 16, 256
BIAS_COPIES = 1 + (NX - 1) + (NY - 1) + (NZ - 1)


def bias_scratch():
    return [
        pltpu.VMEM((count, BIAS_ROWS, BIAS_LANES), jnp.float32)
        for count in (CORES, NX, NY, NZ)
    ]


def bias_sum(place, sems, value, out, bufs):
    copies = []
    for axis, count, buf in zip("cxyz", (CORES, NX, NY, NZ), bufs):
        me = getattr(place, axis)
        buf[me] = value
        sent = [
            sems.copy(buf.at[me], buf.at[me], place.along(axis, step)) for step in range(1, count)
        ]
        yield
        for copy in sent:
            copy.wait_recv()
        value = buf[0]
        for index in range(1, count):
            value = value + buf[index]
        copies += sent
    out[...] = value
    for copy in copies:
        copy.wait_send()


def advance(tasks):
    for task in list(tasks):
        try:
            next(task)
        except StopIteration:
            tasks.remove(task)


def greet(partners):
    barrier = pltpu.get_barrier_semaphore()
    for device in partners:
        pl.semaphore_signal(barrier, inc=1, device_id=device, device_id_type=MESH)


def enter(partners):
    pl.semaphore_wait(pltpu.get_barrier_semaphore(), len(partners))


F32, BF16 = jnp.float32, jnp.bfloat16
TOKENS, D, GROUPS = 256, 512, 4
HALF = TOKENS // 2
PLACES = WIN * WIN
WIDE = 4 * PLACES


def nn(a, b):
    return lax.dot_general(a, b, (((1,), (0,)), ((), ())), preferred_element_type=F32)


def nt(a, b):
    return lax.dot_general(a, b, (((1,), (1,)), ((), ())), preferred_element_type=F32)


def tn(a, b):
    return lax.dot_general(a, b, (((0,), (0,)), ((), ())), preferred_element_type=F32)


def split2(t):
    high = t.astype(BF16)
    return high, (t - high.astype(F32)).astype(BF16)


def split3(t):
    high = t.astype(BF16)
    rest = t - high.astype(F32)
    middle = rest.astype(BF16)
    return high, middle, (rest - middle.astype(F32)).astype(BF16)


def iota(shape, axis):
    return lax.broadcasted_iota(jnp.int32, shape, axis)


def bits(t, low, count):
    return lax.bitwise_and(lax.shift_right_logical(t, low), (1 << count) - 1)


def one_hot(match):
    return jnp.where(match, 1.0, 0.0).astype(BF16)


def strip_order():
    i = iota((TOKENS, 1), 0)
    column = lax.bitwise_and(bits(i, 5, 2) * 8 + bits(i, 0, 3) + SHIFT, 31)
    natural = (bits(i, 7, 1) * 4 + bits(i, 3, 2)) * 32 + column
    return one_hot(iota((TOKENS, TOKENS), 1) == natural)


def quad_order():
    i = iota((HALF, 1), 0)
    column = lax.bitwise_and(2 * bits(i, 0, 4) + bits(i, 6, 1) + 32 - SHIFT, 31)
    row = 2 * bits(i, 4, 1) + bits(i, 5, 1)
    place = bits(column, 3, 2) * 32 + row * 8 + bits(column, 0, 3)
    return one_hot(iota((HALF, HALF), 1) == place)


def offset_order():
    j = iota((1, 1024), 1)
    offset = bits(j, 3, 4) * 15 + bits(j, 0, 3) - bits(j, 7, 3) + 7
    offset = jnp.where(bits(j, 3, 4) < 15, offset, -1)
    return one_hot(iota((256, 1024), 0) == offset)


def head_order():
    return one_hot(bits(iota((256, 128), 0), 5, 2) == bits(iota((256, 128), 1), 5, 2))


def head_sum(t, heads):
    return nn(jnp.concatenate(split2(t), axis=1), heads)


def stack_heads(t, lane_masks):
    return jnp.concatenate([t * mask for mask in lane_masks], axis=0)


def fold_heads(t, lane_masks):
    total = t[:PLACES] * lane_masks[0]
    for h in range(1, 4):
        total = total + t[h * PLACES : (h + 1) * PLACES] * lane_masks[h]
    return total


def norm_parts(t):
    centred = t - jnp.mean(t, -1, keepdims=True)
    scale = lax.rsqrt(jnp.mean(centred * centred, -1, keepdims=True) + 1e-05)
    return centred * scale, scale


def norm_back(grad, hat, scale):
    return scale * (
        grad - jnp.mean(grad, -1, keepdims=True) - hat * jnp.mean(grad * hat, -1, keepdims=True)
    )


def window_masks(place, region_ref, valid_ref, mask_ref):
    strip = place.y * NZ + place.z
    place_lane = iota((1, WIDE), 1) % PLACES
    row, col = place_lane // WIN, place_lane % WIN
    region = region_ref[...].astype(F32)
    valid = valid_ref[...].astype(F32)
    source_row = lax.rem(strip * WIN + SHIFT + row, 256)
    region_row = iota((64, WIDE), 0) == source_row // 4
    valid_row = iota((256, WIDE), 0) == source_row
    shifted_row = strip * WIN + row
    row_part = jnp.where(shifted_row < 256 - WIN, 0, jnp.where(shifted_row < 256 - SHIFT, 1, 2))
    diagonal = iota((PLACES, WIDE), 0) == place_lane
    pick = (iota((PLACES, WIDE), 0) == iota((PLACES, WIDE), 1)).astype(F32)
    for w in range(4):
        source_col = lax.rem(w * WIN + SHIFT + col, 32)
        shifted_col = w * WIN + col
        col_part = jnp.where(shifted_col < 32 - WIN, 0, jnp.where(shifted_col < 32 - SHIFT, 1, 2))
        region_pick = (iota((8, WIDE), 0) == source_col // 4).astype(F32)
        valid_pick = (iota((32, WIDE), 0) == source_col).astype(F32)
        swath = jnp.sum(jnp.where(region_row, tn(region, region_pick), 0.0), 0, keepdims=True)
        live = jnp.sum(jnp.where(valid_row, tn(valid, valid_pick), 0.0), 0, keepdims=True)
        label = swath * 9.0 + (row_part * 3 + col_part).astype(F32)
        label_key = jnp.sum(pick * label, 1, keepdims=True)
        live_key = jnp.sum(pick * live, 1, keepdims=True)
        same = (label_key == label).astype(F32)
        open_key = jnp.where(diagonal, 1.0, jnp.where(live_key == 1.0, 1.0, 0.0))
        mask_ref[w] = same * open_key


def spread_bias(table_ref, onehot_ref, padded_ref, grid_ref, bias_ref):
    padded_ref[...] = jnp.zeros_like(padded_ref)
    padded_ref[:, :OFFSETS] = table_ref[...]
    parts = nn(jnp.concatenate(split3(padded_ref[...]), axis=0), onehot_ref[...])
    spread = parts[:16] + parts[16:32] + parts[32:]
    for ct in range(8):
        grid_ref[pl.ds(ct, 16, stride=8), :] = spread[:, ct * 128 : (ct + 1) * 128]
    left = iota((8, 128), 1) < PLACES
    for pair in range(8):
        even = grid_ref[pair * 16 : pair * 16 + 8]
        odd = grid_ref[pair * 16 + 8 : pair * 16 + 16]
        lanes = pl.ds(pair % 2 * 128, 128)
        for rt in range(8):
            shift = (7 - rt) * 8
            bias_ref[pair // 2, rt * 8 : rt * 8 + 8, lanes] = jnp.where(
                left,
                pltpu.roll(even, (128 - shift) % 128, 1),
                pltpu.roll(odd, (128 + 64 - shift) % 128, 1),
            )


def gather_bias(acc_ref, onehot_ref, grid_ref):
    left = iota((8, 128), 1) < PLACES
    for pair in range(8):
        lanes = pl.ds(pair % 2 * 128, 128)
        even = jnp.zeros((8, 128), F32)
        odd = jnp.zeros((8, 128), F32)
        for rt in range(8):
            shift = (7 - rt) * 8
            piece = acc_ref[pair // 2, rt * 8 : rt * 8 + 8, lanes]
            even = even + pltpu.roll(jnp.where(left, piece, 0.0), shift, 1)
            odd = odd + pltpu.roll(jnp.where(left, 0.0, piece), (64 + shift) % 128, 1)
        grid_ref[pair * 16 : pair * 16 + 8] = even
        grid_ref[pair * 16 + 8 : pair * 16 + 16] = odd
    grid = jnp.concatenate([grid_ref[pl.ds(ct, 16, stride=8), :] for ct in range(8)], axis=1)
    parts = nt(jnp.concatenate(split3(grid), axis=0), onehot_ref[...])
    return parts[:16] + parts[16:32] + parts[32:]


def window_rows(w):
    return (
        pl.ds(pl.multiple_of(w * 32, 32), 32),
        pl.ds(pl.multiple_of(HALF + w * 32, 32), 32),
    )


def take(ref, w, start):
    first, second = window_rows(w)
    lanes = slice(start, start + LANES)
    return jnp.concatenate([ref[first, lanes], ref[second, lanes]], axis=0)


def put(ref, w, start, value):
    first, second = window_rows(w)
    lanes = slice(start, start + LANES)
    ref[first, lanes] = value[:32]
    ref[second, lanes] = value[32:]


STREAMS = ((32, True), (32, True), (16, False), (16, False))


def block_kernel(
    scale_ref,
    tok_hbm,
    wq_hbm,
    region_hbm,
    valid_hbm,
    table_hbm,
    wp_hbm,
    gain_attn_hbm,
    wm_hbm,
    gain_merge_hbm,
    cot_hbm,
    merged_hbm,
    tokens_hbm,
    qkv_out,
    proj_out,
    merge_out,
    bias_out,
    merged_out,
    tokens_out,
    tok_ref,
    wq_ref,
    region_ref,
    valid_ref,
    table_ref,
    wp_ref,
    gain_attn_ref,
    wm_ref,
    gain_merge_ref,
    cot_ref,
    strip_ref,
    quad_ref,
    onehot_ref,
    tw_ref,
    x_ref,
    qkv_ref,
    inv_ref,
    qh_ref,
    ql_ref,
    kh_ref,
    kl_ref,
    mask_ref,
    padded_ref,
    grid_ref,
    bias_ref,
    probs_ref,
    mixed_ref,
    normed_ref,
    hat_ref,
    normed_in,
    quads_ref,
    xt_ref,
    mixedt_ref,
    quadst_ref,
    gh_ref,
    gn_ref,
    go_ref,
    roll_ref,
    gm_ref,
    dn_ref,
    act_ref,
    gs_ref,
    gs_in,
    acc_ref,
    sum_a,
    sum_b,
    part_a,
    part_b,
    sum_c,
    sum_d,
    *scratch,
):
    bufs, at = [], 0
    for rows, ring in STREAMS:
        many = len(stream_scratch(rows, ring))
        bufs.append(scratch[at : at + many])
        at += many
    bias_bufs = scratch[at : at + 4]
    send, recv, local = scratch[at + 4 :]
    place = Place()
    sems = Sems(send, recv)
    strip = place.y * NZ + place.z
    image = place.x * CORES + place.c
    after = (lax.rem(strip + 1, NY * NZ), image)
    before = (lax.rem(strip + NY * NZ - 1, NY * NZ), image)
    own, far = slice(0, HALF), slice(HALF, TOKENS)

    partners = place.partners() + [after, before]
    greet(partners)
    loads = {}
    for index, (source, target) in enumerate(
        (
            (tok_hbm, tok_ref),
            (wq_hbm, wq_ref),
            (region_hbm, region_ref),
            (valid_hbm, valid_ref),
            (table_hbm, table_ref),
            (wp_hbm, wp_ref),
            (gain_attn_hbm, gain_attn_ref),
            (wm_hbm, wm_ref),
            (gain_merge_hbm, gain_merge_ref),
            (cot_hbm, cot_ref),
        )
    ):
        loads[id(target)] = pltpu.make_async_copy(source, target, local.at[index])
        loads[id(target)].start()

    def ready(*refs):
        for ref in refs:
            loads.pop(id(ref)).wait()

    strip_ref[...] = strip_order()
    ready(tok_ref)
    tw_ref[...] = nn(strip_ref[...], tok_ref[...]).astype(BF16)
    enter(partners)
    halo_tokens = [
        sems.copy(tw_ref.at[pl.ds(at, 64)], x_ref.at[pl.ds(HALF + at, 64)], before)
        for at in (0, 64)
    ]
    x_ref[own] = tw_ref[far]

    lane = iota((1, LANES), 1)
    masks = [(lane // HEAD_DIM == h).astype(F32) for h in range(4)]
    masks16 = [mask.astype(BF16) for mask in masks]
    scales = []
    for g in range(GROUPS):
        row = jnp.zeros((1, LANES), F32)
        for h in range(4):
            row = row + masks[h] * scale_ref[g * 4 + h]
        scales.append(row)
    ready(wq_ref)
    heads = head_order()

    def normalise(rows):
        for part, high, low in ((0, qh_ref, ql_ref), (D, kh_ref, kl_ref)):
            columns = [slice(part + g * LANES, part + (g + 1) * LANES) for g in range(GROUPS)]
            raws = [qkv_ref[rows, cols].astype(F32) for cols in columns]
            sums = [head_sum(raw * raw, heads) for raw in raws]
            for g, cols in enumerate(columns):
                inverse = lax.rsqrt(sums[g] + 1e-06)
                inv_ref[rows, cols] = inverse
                unit = raws[g] * inverse
                if part == 0:
                    unit = unit * scales[g]
                near = slice(g * LANES, (g + 1) * LANES)
                high[rows, near], low[rows, near] = split2(unit)

    qkv_ref[own] = nn(x_ref[own], wq_ref[...]).astype(BF16)
    normalise(own)
    ready(region_ref, valid_ref)
    window_masks(place, region_ref, valid_ref, mask_ref)
    quad_ref[...] = quad_order()
    onehot_ref[...] = offset_order()
    ready(table_ref)
    spread_bias(table_ref, onehot_ref, padded_ref, grid_ref, bias_ref)
    def forward(w, carry):
        allowed = mask_ref[w] > 0.5
        scores = []
        for g in range(GROUPS):
            start = g * LANES
            kh, kl = take(kh_ref, w, start), take(kl_ref, w, start)
            qh = stack_heads(take(qh_ref, w, start), masks16)
            ql = stack_heads(take(ql_ref, w, start), masks16)
            scores.append(
                nt(jnp.concatenate([kh, kl, kh], axis=1), jnp.concatenate([qh, qh, ql], axis=1))
            )
        rounded = []
        for g in range(GROUPS):
            score = jnp.where(allowed, scores[g] + bias_ref[g], -1000000000.0)
            expo = jnp.exp(score - jnp.max(score, 0, keepdims=True))
            probs = expo * (1.0 / jnp.sum(expo, 0, keepdims=True))
            probs_ref[w, g] = probs
            rounded.append(probs.astype(BF16))
        outs = [tn(rounded[g], take(qkv_ref, w, 2 * D + g * LANES)) for g in range(GROUPS)]
        for g in range(GROUPS):
            put(mixed_ref, w, g * LANES, fold_heads(outs[g], masks).astype(BF16))
        return carry

    ready(wp_ref, gain_attn_ref)
    gain_attn = gain_attn_ref[...]

    def project(rows):
        hat, scale = norm_parts(nn(mixed_ref[rows], wp_ref[...]))
        hat_ref[rows] = hat
        normed_ref[rows] = (hat * gain_attn).astype(BF16)
        return scale

    pieces = [(at, slice(HALF + at, HALF + at + 64)) for at in (0, 64)]
    halo_normed, scales_far = [], []
    for index, (at, rows) in enumerate(pieces):
        halo_tokens[index].wait_recv()
        qkv_ref[rows] = nn(x_ref[rows], wq_ref[...]).astype(BF16)
        normalise(rows)
        lax.fori_loop(2 * index, 2 * index + 2, forward, 0, unroll=2)
        scales_far.append(project(rows))
        halo_normed.append(
            sems.copy(
                normed_ref.at[pl.ds(HALF + at, 64)], normed_in.at[pl.ds(at, 64)], after
            )
        )
    scale_own = project(own)

    def make_quads(which, added):
        rows = slice(which * HALF, (which + 1) * HALF)
        hidden = (tw_ref[rows].astype(F32) + added.astype(F32)).astype(BF16)
        sorted_rows = nn(quad_ref[...], hidden).astype(BF16)
        for k in range(4):
            quads_ref[which * 32 : which * 32 + 32, k * D : (k + 1) * D] = sorted_rows[
                k * 32 : (k + 1) * 32
            ]

    make_quads(1, normed_ref[own])
    xt_ref[...] = x_ref[...].T
    mixedt_ref[...] = mixed_ref[...].T
    ready(wm_ref, gain_merge_ref, cot_ref)
    for copy in halo_normed:
        copy.wait_recv()
    make_quads(0, normed_in[...])
    quadst_ref[...] = quads_ref[...].T

    gain_merge = gain_merge_ref[...]
    hat, scale = norm_parts(nn(quads_ref[...], wm_ref[...]))
    merged_out[...] = (hat * gain_merge).astype(BF16)
    write_merged = pltpu.make_async_copy(merged_out, merged_hbm, local.at[10])
    write_merged.start()
    grad_pre = norm_back(cot_ref[...].astype(F32) * gain_merge, hat, scale).astype(BF16)
    parts_a = CorePart(place, sems, True, sum_a, bufs[0][0])
    parts_b = CorePart(place, sems, False, sum_b, bufs[1][0])
    parts_c = CorePart(place, sems, True, sum_c, bufs[2][0])
    parts_d = CorePart(place, sems, False, sum_d, bufs[3][0])
    for x in range(NX):
        for y in range(NY):
            block = nn(
                quadst_ref[y * D : (y + 1) * D], grad_pre[:, x * 256 : (x + 1) * 256]
            ).reshape(NZ, 2, 32, 256)
            for c in range(CORES):
                lanes = slice(c * LANES, (c + 1) * LANES)
                sum_a[c, x, y] = block[:, 0, :, lanes].reshape(NZ * 32, LANES).astype(BF16)
                sum_b[c, y, x] = block[:, 1, :, lanes].reshape(NZ * 32, LANES).astype(BF16)
        parts_a.send(x)
        parts_b.send(x)

    grad_quads = nt(grad_pre, wm_ref[...]).astype(BF16)
    for which in range(2):
        stacked = jnp.concatenate(
            [grad_quads[which * 32 : which * 32 + 32, k * D : (k + 1) * D] for k in range(4)],
            axis=0,
        )
        gh_ref[which * HALF : (which + 1) * HALF] = tn(quad_ref[...], stacked).astype(BF16)
        if which == 0:
            halo_hidden = [
                sems.copy(gh_ref.at[pl.ds(at, 64)], gn_ref.at[pl.ds(HALF + at, 64)], before)
                for at in (0, 64)
            ]
    gn_ref[own] = gh_ref[far]

    merging = [
        stream(place, sems, "x", "y", 32, True, parts_a, merge_out.at[0:32], bufs[0]),
        stream(place, sems, "y", "x", 32, True, parts_b, merge_out.at[32:64], bufs[1]),
    ]
    attending = [
        stream(place, sems, "x", "y", 16, False, parts_c, part_a, bufs[2]),
        stream(place, sems, "y", "x", 16, False, parts_d, part_b, bufs[3]),
    ]

    def back_norm(rows, scale):
        grad = gn_ref[rows].astype(F32) * gain_attn
        out = norm_back(grad, hat_ref[rows], scale)
        go_ref[rows] = out.astype(BF16)
        for x in range(NX):
            lanes = slice(x * LANES, (x + 1) * LANES)
            roll_ref[rows, lanes] = pltpu.roll(out[:, lanes], 64, 1).astype(BF16)
        gm_ref[rows] = nt(go_ref[rows], wp_ref[...]).astype(BF16)

    back_norm(own, scale_own)
    advance(merging)
    acc_ref[...] = jnp.zeros_like(acc_ref)

    def backward(w, carry):
        starts = [g * LANES for g in range(GROUPS)]
        grads = [stack_heads(take(gm_ref, w, start), masks16) for start in starts]
        grad_probs = [
            nt(take(qkv_ref, w, 2 * D + start), grad) for start, grad in zip(starts, grads)
        ]
        for g, start in enumerate(starts):
            value = nn(probs_ref[w, g].astype(BF16), grads[g])
            put(act_ref, w, 2 * D + start, value.astype(BF16))
        grad_scores = []
        for g in range(GROUPS):
            probs = probs_ref[w, g]
            weighted = probs * grad_probs[g]
            grad_score = weighted - probs * jnp.sum(weighted, 0, keepdims=True)
            acc_ref[g] += grad_score
            grad_scores.append(grad_score.astype(BF16))
        for g, start in enumerate(starts):
            query = stack_heads(take(qh_ref, w, start), masks16)
            put(dn_ref, w, D + start, nn(grad_scores[g], query))
        outs = [tn(grad_scores[g], take(kh_ref, w, starts[g])) for g in range(GROUPS)]
        for g, start in enumerate(starts):
            put(dn_ref, w, start, fold_heads(outs[g], masks))
        return carry

    for index, (at, rows) in enumerate(pieces):
        halo_hidden[index].wait_recv()
        back_norm(rows, scales_far[index])
        lax.fori_loop(2 * index, 2 * index + 2, backward, 0, unroll=2)
    for part in (0, D):
        columns = [slice(part + g * LANES, part + (g + 1) * LANES) for g in range(GROUPS)]
        grads = [dn_ref[:, cols] for cols in columns]
        if part == 0:
            grads = [grad * scale for grad, scale in zip(grads, scales)]
        units = [qkv_ref[:, cols].astype(F32) * inv_ref[:, cols] for cols in columns]
        sums = [head_sum(unit * grad, heads) for unit, grad in zip(units, grads)]
        for g, cols in enumerate(columns):
            act_ref[:, cols] = (inv_ref[:, cols] * (grads[g] - units[g] * sums[g])).astype(BF16)

    left = iota((1, LANES), 1) < 64
    for x in range(NX):
        block = nn(xt_ref[...], act_ref[:, x * 384 : (x + 1) * 384])
        rolled = nn(mixedt_ref[...], roll_ref[:, x * LANES : (x + 1) * LANES])
        middle = block[:, 128:256]
        firsts = (block[:, :128], block[:, 256:])
        seconds = (jnp.where(left, middle, rolled), jnp.where(left, rolled, middle))
        for c in range(CORES):
            one, two = firsts[c].astype(BF16), seconds[c].astype(BF16)
            for y in range(NY):
                rows = slice(y * 128, (y + 1) * 128)
                sum_c[c, x, y] = one[rows]
                sum_d[c, y, x] = two[rows]
        parts_c.send(x)
        parts_d.send(x)

    advance(merging)
    gs_ref[far] = nt(act_ref[far], wq_ref[...]).astype(BF16)
    halo_shifted = sems.copy(gs_ref.at[far], gs_in, after)
    advance(attending)

    bias_part = gather_bias(acc_ref, onehot_ref, grid_ref)
    biasing = [bias_sum(place, sems, bias_part, padded_ref, bias_bufs)]
    advance(biasing)
    gs_ref[own] = nt(act_ref[own], wq_ref[...]).astype(BF16)
    gs_ref[own] = (gh_ref[far].astype(F32) + gs_ref[own].astype(F32)).astype(BF16)
    advance(biasing)
    halo_shifted.wait_recv()
    gn_own = (gh_ref[own].astype(F32) + gs_in[...].astype(F32)).astype(BF16)
    tokens_out[...] = tn(strip_ref[...], jnp.concatenate([gn_own, gs_ref[own]], axis=0)).astype(
        BF16
    )
    write_tokens = pltpu.make_async_copy(tokens_out, tokens_hbm, local.at[11])
    write_tokens.start()
    while merging or attending or biasing:
        advance(merging)
        advance(attending)
        advance(biasing)
    for copy in halo_tokens + halo_normed + halo_hidden + [halo_shifted]:
        copy.wait_send()

    bias_out[...] = padded_ref[:, :OFFSETS]
    write_merged.wait()
    write_tokens.wait()
    one, two = part_a[...], part_b[...]
    one_rolled, two_rolled = pltpu.roll(one, 64, 1), pltpu.roll(two, 64, 1)
    first_core = place.c == 0
    qkv_out[:, :128] = jnp.where(first_core, one, jnp.where(left, two_rolled, one_rolled))
    qkv_out[:, 128:] = jnp.where(first_core, two, one_rolled)[:, :64]
    proj_out[...] = jnp.where(first_core, two_rolled, two)[:, :64]


def block(tokens, region, valid, wq, wp, wm, scale, table, gain_attn, gain_merge, cot):
    vmem = pl.BlockSpec(memory_space=pltpu.VMEM)
    smem = pl.BlockSpec(memory_space=pltpu.SMEM)
    far = pl.BlockSpec(memory_space=pl.ANY)
    total = 7 + sum(stream_copies(ring) for _, ring in STREAMS) + BIAS_COPIES
    inputs = [tokens, wq, region, valid, table, wp, gain_attn, wm, gain_merge, cot]

    def buf(*shape):
        return pltpu.VMEM(shape, BF16)

    def wide(*shape):
        return pltpu.VMEM(shape, F32)

    return pl.pallas_call(
        block_kernel,
        out_shape=[
            jax.ShapeDtypeStruct((64, 1024), BF16),
            jax.ShapeDtypeStruct((TOKENS, D), BF16),
            jax.ShapeDtypeStruct((16, 192), F32),
            jax.ShapeDtypeStruct((16, 64), F32),
            jax.ShapeDtypeStruct((64, 128), F32),
            jax.ShapeDtypeStruct((16, OFFSETS), F32),
        ],
        in_specs=[smem] + [far] * len(inputs),
        out_specs=[far] * 2 + [vmem] * 4,
        scratch_shapes=[buf(64, 1024), buf(TOKENS, D)]
        + [pltpu.VMEM(value.shape, value.dtype) for value in inputs]
        + [
            buf(TOKENS, TOKENS),
            buf(HALF, HALF),
            buf(256, 1024),
            buf(TOKENS, D),
            buf(TOKENS, D),
            buf(TOKENS, 3 * D),
            wide(TOKENS, 2 * D),
            buf(TOKENS, D),
            buf(TOKENS, D),
            buf(TOKENS, D),
            buf(TOKENS, D),
            wide(4, PLACES, WIDE),
            wide(BIAS_ROWS, BIAS_LANES),
            wide(128, 128),
            wide(GROUPS, PLACES, WIDE),
            wide(4, GROUPS, PLACES, WIDE),
            buf(TOKENS, D),
            buf(TOKENS, D),
            wide(TOKENS, D),
            buf(HALF, D),
            buf(64, 2048),
            buf(D, TOKENS),
            buf(D, TOKENS),
            buf(2048, 64),
            buf(TOKENS, D),
            buf(TOKENS, D),
            buf(TOKENS, D),
            buf(TOKENS, D),
            buf(TOKENS, D),
            wide(TOKENS, 2 * D),
            buf(TOKENS, 3 * D),
            buf(TOKENS, D),
            buf(HALF, D),
            wide(GROUPS, PLACES, WIDE),
            buf(CORES, NX, NY, NZ * 32, LANES),
            buf(CORES, NY, NX, NZ * 32, LANES),
            wide(16, LANES),
            wide(16, LANES),
            buf(CORES, NX, NY, NZ * 16, LANES),
            buf(CORES, NY, NX, NZ * 16, LANES),
        ]
        + sum([stream_scratch(*kind) for kind in STREAMS], [])
        + bias_scratch()
        + [
            pltpu.SemaphoreType.DMA((total,)),
            pltpu.SemaphoreType.DMA((total,)),
            pltpu.SemaphoreType.DMA((len(inputs) + 2,)),
        ],
        compiler_params=pltpu.CompilerParams(
            collective_id=0, has_side_effects=True, vmem_limit_bytes=56 * 1024 * 1024
        ),
        name="block",
    )(scale, *inputs)


def hand_out_kernel(*refs):
    count = len(refs) // 2
    copies = [
        pltpu.make_async_copy(refs[i], refs[count + i], refs[-1].at[i]) for i in range(count)
    ]
    for copy in copies:
        copy.start()
    for copy in copies:
        copy.wait()


def hand_out(values):
    near, far = pl.BlockSpec(memory_space=pltpu.VMEM), pl.BlockSpec(memory_space=pl.ANY)
    return pl.pallas_call(
        hand_out_kernel,
        out_shape=[jax.ShapeDtypeStruct(value.shape, value.dtype) for value in values],
        in_specs=[near] * len(values),
        out_specs=[far] * len(values),
        scratch_shapes=[pltpu.SemaphoreType.DMA((len(values),))],
        name="hand_out",
    )(*values)


def shards(
    tokens,
    region,
    valid,
    qkv_weight,
    proj_weight,
    merge_weight,
    logit_scale,
    bias_table,
    gain_attn,
    gain_merge,
    cotangent,
):
    merged, grad_tokens, grad_qkv, grad_proj, grad_merge, grad_bias = hand_out(
        block(
        tokens.reshape(TOKENS, D),
        region[0].T,
        valid[0].T,
        qkv_weight,
        proj_weight,
        merge_weight,
        logit_scale,
        bias_table,
        gain_attn[None],
        gain_merge[None],
        cotangent.reshape(64, 1024),
    ))
    return (
        merged.reshape(cotangent.shape),
        grad_tokens.reshape(tokens.shape),
        grad_qkv,
        grad_proj,
        grad_merge,
        grad_bias,
    )


def solution(mesh):
    return jax.shard_map(
        shards,
        mesh=mesh,
        in_specs=(
            P("dp", "space", None, None),
            P("dp", None, None),
            P("dp", None, None),
            P(),
            P(),
            P(),
            P(),
            P(),
            P(),
            P(),
            P("dp", "space", None, None),
        ),
        out_specs=(
            P("dp", "space", None, None),
            P("dp", "space", None, None),
            P("space", "dp"),
            P("space", "dp"),
            P("space", "dp"),
            P(),
        ),
        check_vma=False,
    )
```
